32 devices in a mesh: row: 4 (over z), col: 8 (over y, x, core).
Axes of the slice: x: 2, y: 2, z: 4, core: 2. Of those that a mesh axis runs over, the one named last changes fastest.
Arguments:
- density: float32 [8192, 8192], P('row', 'col'), may hold values from -0.01171875 to 0.01171875
- h_core: float32 [8192, 8192], P('row', 'col'), may hold values from -6 to 6
- phi: float32 [64, 1024, 512], P(('row', 'col')), may hold values from -6 to 6
- v_ext: float32 [64, 1024], P(('row', 'col')), may hold values from -6 to 6
- tile_blocks: int32 [64, 4], replicated, may hold values from 0 to 63, as said below
- tile_count: int32 [64], replicated, may hold values from 3 to 4
Outputs:
- hamiltonian: float32 [8192, 8192], P('row', 'col')
- dm_ham: float32 [8192, 8192], P('row', 'col')
The draws below stay inside these ranges and needn't reach their ends.
Inputs may be any that keep to these rules, and one draw needn't show every extreme that they name: Tile t belongs to device t // 2, devices counted as row index * col size + col index. Over all slots of one device's 2 tiles, the numbers tile_blocks // 8 are all different; within one tile the numbers tile_blocks // 16 are all different. So every device gets at most one live block pair of its tiles from any one device, and on some draws a device pair does exchange exactly one such pair.
All inputs are finite; a program needn't handle non-finite values.
Results may differ from the reference program's by a relative error of at most 0.004.
Values may be sent and summed in bfloat16 or wider, within the bound.
No kernel may reach another device: no remote copies, remote signals or barrier semaphores. Data moves between devices by JAX's collectives and lax.ppermute only.
A program may use at most 192 MiB of HBM per device.

```python
import jax
import jax.numpy as jnp
from jax import lax

NORB = 8192
BLK = 128
MAXB = 4
G = 1024
LOC = 512
NB = 64
ROWB = 16
COLB = 8
RATIO = 2
TILE_DEV = 2
NTILES = 64
DEVICES = 32


def draw_tile_blocks(key, part):
    devices_all = DEVICES
    row_shards = NB // ROWB
    keys = jax.random.split(key, 2)
    order_keys = jax.random.split(keys[0], devices_all)
    orders = jax.vmap(lambda sub: jax.random.permutation(sub, row_shards))(order_keys)
    tile_pos = jnp.arange(TILE_DEV, dtype=jnp.int32)
    slot_pos = jnp.arange(MAXB, dtype=jnp.int32)
    half = tile_pos % RATIO
    place = (tile_pos // RATIO)[:, None] * MAXB + slot_pos[None, :]
    row_dev = orders[:, place]
    group = RATIO * row_dev + half[None, :, None]
    offset = jax.random.randint(keys[1], (devices_all, TILE_DEV, MAXB), 0, COLB)
    return (group * COLB + offset).reshape(devices_all * TILE_DEV, MAXB).astype(jnp.int32)


def plant(result, stream_key, least, largest):
    index_at = [jax.random.randint(jax.random.fold_in(stream_key, axis), (), 0, length) for axis, length in enumerate(result.shape)]
    widest = result.shape.index(max(result.shape))
    next_to = index_at[:widest] + [(index_at[widest] + 1) % result.shape[widest]] + index_at[widest + 1:]
    return result.at[tuple(index_at)].set(least).at[tuple(next_to)].set(largest)


def level_of(rng, shape, cuts, least, top_value):
    def one(position, shards_of):
        steps = jax.random.uniform(jax.random.fold_in(jax.random.fold_in(rng, 6), position), (shards_of,), jnp.float32, least / len(cuts), top_value / len(cuts))
        return jnp.repeat(jnp.exp(steps), shape[position] // shards_of).reshape((-1,) + (1,) * (len(shape) - position - 1))

    level = one(*cuts[0])
    for cut in cuts[1:]:
        level = level * one(*cut)
    return level


def bell_draw(stream_key, extent, deviation, limit, cuts=(), held_as=jnp.bfloat16):
    drawn = deviation * jax.random.normal(stream_key, extent, jnp.float32)
    if cuts:
        drawn = drawn * level_of(stream_key, extent, cuts, -0.22, 0.18)
    return jnp.clip(drawn, -limit, limit).astype(held_as)


def setup_inputs(seed: int = 0) -> dict:
    splits = jax.random.split(jax.random.key(seed), 7)
    return {
        "density": bell_draw(splits[0], (NORB, NORB), (1.0 / LOC), 0.01171875, ((0, 4), (1, 8)), jnp.float32),
        "h_core": bell_draw(splits[1], (NORB, NORB), 1.0, 6.0, ((0, 4), (1, 8)), jnp.float32),
        "phi": bell_draw(splits[2], (NTILES, G, LOC), 1.0, 6.0, ((0, 32),), jnp.float32),
        "v_ext": bell_draw(splits[3], (NTILES, G), 1.0, 6.0, ((0, 32),), jnp.float32),
        "tile_blocks": draw_tile_blocks(jax.random.fold_in(splits[6], 71), 0),
        "tile_count": plant(jax.random.randint(splits[5], (NTILES,), 3, MAXB + 1), jax.random.fold_in(splits[5], 1), 3, MAXB).astype(jnp.int32),
    }


cube_coef = 0.5
cell_volume = 0.03125


def reference(density, h_core, phi, v_ext, tile_blocks, tile_count):
    nblocks = NORB // BLK
    dm_tiles = density.reshape(nblocks, BLK, nblocks, BLK)

    def tile_step(ham_tiles, item):
        basis, outer, blocks, count = item
        slot_live = jnp.arange(MAXB, dtype=jnp.int32) < count
        column_live = jnp.repeat(slot_live, BLK).astype(basis.dtype)
        masked = basis * column_live[None, :]
        local_dm = dm_tiles[blocks[:, None], :, blocks[None, :], :]
        local_dm = local_dm.transpose(0, 2, 1, 3).reshape(LOC, LOC)
        spread = jnp.dot(masked, local_dm, precision=lax.Precision.HIGHEST, preferred_element_type=jnp.float32)
        rho = jnp.sum(spread * masked, axis=1)
        potential = outer + rho + cube_coef * rho * rho * rho
        weighted = masked * potential[:, None]
        local_ham = cell_volume * jnp.dot(weighted.T, masked, precision=lax.Precision.HIGHEST, preferred_element_type=jnp.float32)
        pieces = local_ham.reshape(MAXB, BLK, MAXB, BLK).transpose(0, 2, 1, 3)
        ham_tiles = ham_tiles.at[blocks[:, None], :, blocks[None, :], :].add(pieces)
        return ham_tiles, None

    start = h_core.reshape(nblocks, BLK, nblocks, BLK)
    ham_tiles, _ = lax.scan(tile_step, start, (phi, v_ext, tile_blocks, tile_count))
    hamiltonian = ham_tiles.reshape(NORB, NORB)
    dm_low = density.astype(jnp.bfloat16).astype(jnp.float32)
    ham_low = hamiltonian.astype(jnp.bfloat16).astype(jnp.float32)
    dm_ham = jnp.dot(dm_low, ham_low, precision=lax.Precision.HIGHEST, preferred_element_type=jnp.float32)
    return hamiltonian, dm_ham
```

```python
import jax
import jax.numpy as jnp
from jax import lax
from jax.experimental import pallas as pl
from jax.experimental.pallas import tpu as pltpu
from jax.sharding import PartitionSpec as P

BLK = 128

cube_coef = 0.5
cell_volume = 0.03125
DM_SCALE = float(2**20)

F32 = jnp.float32
BF16 = jnp.bfloat16
MIB = 1 << 20


def gather_kernel(row_ref, col_ref, dens_ref, out_ref, sems):
    n = out_ref.shape[0]

    def copy(s):
        r = pl.multiple_of(row_ref[s] * BLK, BLK)
        c = pl.multiple_of(col_ref[s] * BLK, BLK)
        return pltpu.make_async_copy(
            dens_ref.at[pl.ds(r, BLK), pl.ds(c, BLK)], out_ref.at[s], sems.at[s]
        )

    def start(s, carry):
        copy(s).start()
        return carry

    def wait(s, carry):
        copy(s).wait()
        return carry

    lax.fori_loop(0, n, start, 0)
    lax.fori_loop(0, n, wait, 0)


def gather_blocks(density, row_pick, col_pick):
    n = row_pick.shape[0]
    return pl.pallas_call(
        gather_kernel,
        grid_spec=pltpu.PrefetchScalarGridSpec(
            num_scalar_prefetch=2,
            grid=(1,),
            in_specs=[pl.BlockSpec(memory_space=pl.ANY)],
            out_specs=pl.BlockSpec((n, BLK, BLK), lambda i, *_: (0, 0, 0)),
            scratch_shapes=[pltpu.SemaphoreType.DMA((n,))],
        ),
        out_shape=jax.ShapeDtypeStruct((n, BLK, BLK), F32),
        compiler_params=pltpu.CompilerParams(vmem_limit_bytes=24 * MIB),
        cost_estimate=pl.CostEstimate(
            flops=0, bytes_accessed=2 * n * BLK * BLK * 4, transcendentals=0
        ),
        name="gather_blocks",
    )(row_pick, col_pick, density)


def split(x):
    hi = x.astype(BF16)
    return hi, (x - hi.astype(F32)).astype(BF16)


def dot3(a, b, dims):
    (ah, al), (bh, bl) = a, b

    def one(x, y):
        return lax.dot_general(x, y, (dims, ((), ())), preferred_element_type=F32)

    return one(ah, bh) + (one(al, bh) + one(ah, bl))


def tile_kernel(hold_ref, count_ref, in_ref, phi_ref, v_ref, out_ref, dh_ref, dl_ref):
    t = pl.program_id(0)
    maxb = phi_ref.shape[2] // BLK
    for i in range(maxb):
        for j in range(maxb):
            blk = in_ref[hold_ref[t, i * maxb + j]] * (1.0 / DM_SCALE)
            hi, lo = split(blk)
            dh_ref[i * BLK : (i + 1) * BLK, j * BLK : (j + 1) * BLK] = hi
            dl_ref[i * BLK : (i + 1) * BLK, j * BLK : (j + 1) * BLK] = lo
    basis = phi_ref[0]
    column = lax.broadcasted_iota(jnp.int32, basis.shape, 1)
    count = count_ref[t]
    masked = jnp.where(column < count * BLK, basis, 0.0)
    ms = split(masked)
    spread = dot3(ms, (dh_ref[...], dl_ref[...]), ((1,), (0,)))
    rho = jnp.sum(spread * masked, axis=1, keepdims=True)
    potential = v_ref[0] + rho + cube_coef * rho * rho * rho
    ws = split(masked * (potential * cell_volume))
    ham = dot3(ws, ms, ((0,), (0,))).astype(BF16)
    for i in range(maxb):
        for j in range(maxb):

            @pl.when((i < count) & (j < count))
            def _():
                out_ref[hold_ref[t, i * maxb + j]] = ham[
                    i * BLK : (i + 1) * BLK, j * BLK : (j + 1) * BLK
                ]


def tile_ham(incoming, phi, v_ext, hold, counts):
    n = incoming.shape[0]
    tdev, npts, local = phi.shape
    flops = tdev * 3 * 2 * 2 * npts * local * local
    return pl.pallas_call(
        tile_kernel,
        grid_spec=pltpu.PrefetchScalarGridSpec(
            num_scalar_prefetch=2,
            grid=(tdev,),
            in_specs=[
                pl.BlockSpec((n, BLK, BLK), lambda t, *_: (0, 0, 0)),
                pl.BlockSpec((1, npts, local), lambda t, *_: (t, 0, 0)),
                pl.BlockSpec((1, npts, 1), lambda t, *_: (t, 0, 0)),
            ],
            out_specs=pl.BlockSpec((n, BLK, BLK), lambda t, *_: (0, 0, 0)),
            scratch_shapes=[
                pltpu.VMEM((local, local), BF16),
                pltpu.VMEM((local, local), BF16),
            ],
        ),
        out_shape=jax.ShapeDtypeStruct((n, BLK, BLK), BF16),
        compiler_params=pltpu.CompilerParams(vmem_limit_bytes=56 * MIB),
        cost_estimate=pl.CostEstimate(
            flops=flops, bytes_accessed=tdev * npts * local * 4, transcendentals=0
        ),
        name="tile_ham",
    )(hold, counts, incoming, phi, v_ext[:, :, None])


def assemble_kernel(row_ref, col_ref, present_ref, in_ref, h_ref, out_ref, low_ref):
    step = pl.program_id(0)
    n = in_ref.shape[0]
    per = h_ref.shape[0] // BLK
    out_ref[...] = h_ref[...]

    def add(s, carry):
        r = row_ref[s]

        @pl.when((present_ref[s] > 0) & (r // per == step))
        def _():
            rows = pl.ds(pl.multiple_of((r - step * per) * BLK, BLK), BLK)
            cols = pl.ds(pl.multiple_of(col_ref[s] * BLK, BLK), BLK)
            out_ref[rows, cols] = out_ref[rows, cols] + in_ref[s].astype(F32)

        return carry

    lax.fori_loop(0, n, add, 0)
    low_ref[...] = out_ref[...].astype(BF16)


def assemble(h_core, arriving, row_pick, col_pick, present):
    rows, cols = h_core.shape
    n = arriving.shape[0]
    bm = 2 * BLK
    return pl.pallas_call(
        assemble_kernel,
        grid_spec=pltpu.PrefetchScalarGridSpec(
            num_scalar_prefetch=3,
            grid=(rows // bm,),
            in_specs=[
                pl.BlockSpec((n, BLK, BLK), lambda i, *_: (0, 0, 0)),
                pl.BlockSpec((bm, cols), lambda i, *_: (i, 0)),
            ],
            out_specs=[
                pl.BlockSpec((bm, cols), lambda i, *_: (i, 0)),
                pl.BlockSpec((bm, cols), lambda i, *_: (i, 0)),
            ],
        ),
        out_shape=[
            jax.ShapeDtypeStruct((rows, cols), F32),
            jax.ShapeDtypeStruct((rows, cols), BF16),
        ],
        compiler_params=pltpu.CompilerParams(vmem_limit_bytes=32 * MIB),
        cost_estimate=pl.CostEstimate(
            flops=rows * cols, bytes_accessed=rows * cols * 10, transcendentals=0
        ),
        name="assemble",
    )(row_pick, col_pick, present, arriving, h_core)


def product(total, dm_panel, pieces):
    ncol, rows, width = dm_panel.shape
    depth, cols = pieces[0][0][0].shape
    per = depth // width
    bm = min(512, rows)
    counts = [len(c) for c, _, _ in pieces]
    npiece = len(pieces)
    nh = sum(counts)
    scalars = jnp.stack(
        [jnp.asarray(s, jnp.int32) for _, _, s in pieces]
        + [jnp.asarray(w, jnp.int32) for _, w, _ in pieces]
    )

    def kernel(sc_ref, *refs):
        h_refs = refs[:nh]
        d_refs = refs[nh : nh + npiece]
        rest = refs[nh + npiece :]
        if total is not None:
            c_ref, rest = rest[0], rest[1:]
        out_ref = rest[0]
        held = rest[1 : 1 + npiece]
        sems = rest[1 + npiece]

        @pl.when(pl.program_id(0) == 0)
        def _():
            at = 0
            for p in range(npiece):
                for q in range(counts[p]):

                    @pl.when(sc_ref[npiece + p] == q)
                    def _(p=p, at=at):
                        pltpu.make_async_copy(h_refs[at], held[p], sems.at[p]).start()

                    at += 1
            first = 0
            for p in range(npiece):
                pltpu.make_async_copy(h_refs[first], held[p], sems.at[p]).wait()
                first += counts[p]

        acc = None
        for p in range(npiece):
            for q in range(per):
                part = jnp.dot(
                    d_refs[p][q],
                    held[p][q * width : (q + 1) * width, :],
                    preferred_element_type=F32,
                )
                acc = part if acc is None else acc + part
        if total is not None:
            acc = acc + c_ref[...]
        out_ref[...] = acc

    def d_map(p):
        return lambda i, sc: (sc[p], i, 0)

    c_spec = pl.BlockSpec((bm, cols), lambda i, sc: (i, 0))
    args = [h for c, _, _ in pieces for h in c] + [dm_panel] * npiece
    in_specs = [pl.BlockSpec(memory_space=pl.ANY)] * nh + [
        pl.BlockSpec((per, bm, width), d_map(p)) for p in range(npiece)
    ]
    aliases = {}
    if total is not None:
        aliases = {1 + len(args): 0}
        args.append(total)
        in_specs.append(c_spec)
    return pl.pallas_call(
        kernel,
        grid_spec=pltpu.PrefetchScalarGridSpec(
            num_scalar_prefetch=1,
            grid=(rows // bm,),
            in_specs=in_specs,
            out_specs=c_spec,
            scratch_shapes=[pltpu.VMEM((depth, cols), BF16)] * npiece
            + [pltpu.SemaphoreType.DMA((npiece,))],
        ),
        out_shape=jax.ShapeDtypeStruct((rows, cols), F32),
        input_output_aliases=aliases,
        compiler_params=pltpu.CompilerParams(vmem_limit_bytes=56 * MIB),
        cost_estimate=pl.CostEstimate(
            flops=2 * npiece * rows * depth * cols,
            bytes_accessed=npiece * (rows + cols) * depth * 2 + rows * cols * 8,
            transcendentals=0,
        ),
        name="product",
    )(scalars, *args)


def body(density, h_core, phi, v_ext, tile_blocks, tile_count):
    nrow = lax.axis_size("row")
    ncol = lax.axis_size("col")
    ndev = nrow * ncol
    row_idx = lax.axis_index("row")
    col_idx = lax.axis_index("col")
    myself = row_idx * ncol + col_idx
    rows_loc, cols_loc = density.shape
    rowb = rows_loc // BLK
    colb = cols_loc // BLK
    tdev, npts, local = phi.shape
    maxb = tile_blocks.shape[1]

    dm_low = density.astype(BF16)
    dm_panel = lax.all_gather(dm_low, "col", axis=0, tiled=False)

    blocks = tile_blocks.reshape(ndev, tdev, maxb)
    counts = tile_count.reshape(ndev, tdev)
    live = jnp.arange(maxb, dtype=jnp.int32)[None, None, :] < counts[:, :, None]
    row_hit = live & (blocks // rowb == row_idx)
    col_hit = live & (blocks // colb == col_idx)
    both = jnp.any(row_hit, axis=2) & jnp.any(col_hit, axis=2)
    row_in = jnp.sum(jnp.where(row_hit, blocks - row_idx * rowb, 0), axis=2)
    col_in = jnp.sum(jnp.where(col_hit, blocks - col_idx * colb, 0), axis=2)
    row_pick = jnp.sum(jnp.where(both, row_in, 0), axis=1)
    col_pick = jnp.sum(jnp.where(both, col_in, 0), axis=1)
    present = jnp.any(both, axis=1).astype(jnp.int32)
    mine = lax.dynamic_index_in_dim(blocks, myself, 0, keepdims=False)
    my_counts = lax.dynamic_index_in_dim(counts, myself, 0, keepdims=False)
    hold = ((mine // rowb)[:, :, None] * ncol + (mine // colb)[:, None, :]).reshape(tdev, -1)

    outgoing = (gather_blocks(density, row_pick, col_pick) * DM_SCALE).astype(jnp.float16)
    incoming = lax.all_to_all(outgoing, ("row", "col"), split_axis=0, concat_axis=0, tiled=True)
    returning = tile_ham(incoming.astype(F32), phi, v_ext, hold, my_counts)
    arriving = lax.all_to_all(returning, ("row", "col"), split_axis=0, concat_axis=0, tiled=True)
    hamiltonian, ham_low = assemble(h_core, arriving, row_pick, col_pick, present)

    if nrow == 4:
        swap = [(0, 1), (1, 0), (2, 3), (3, 2)]
        cross = [(1, 2), (2, 1)]
        outward = [(1, 0), (2, 3)]
        partner = lax.ppermute(ham_low, "row", swap)
        near_mid = lax.ppermute(ham_low, "row", cross)
        far_mid = lax.ppermute(partner, "row", cross)
        near_end = lax.ppermute(near_mid, "row", outward)
        far_end = lax.ppermute(far_mid, "row", outward)
        low = row_idx < 2
        is_end = ((row_idx == 0) | (row_idx == 3)).astype(jnp.int32)
        pair_idx = row_idx + 1 - 2 * (row_idx % 2)
        near_idx = jnp.where(low, 2, 1)
        far_idx = jnp.where(low, 3, 0)
        total = product(None, dm_panel, [((ham_low,), 0, row_idx), ((partner,), 0, pair_idx)])
        total = product(total, dm_panel, [((near_mid, near_end), is_end, near_idx)])
        total = product(total, dm_panel, [((far_mid, far_end), is_end, far_idx)])
    else:
        ham_panel = lax.all_gather(ham_low, "row", axis=0, tiled=False)
        total = None
        for k in range(nrow):
            total = product(total, dm_panel, [((ham_panel[k],), 0, k)])
    return hamiltonian, total


def solution(mesh):
    placed = (
        P("row", "col"),
        P("row", "col"),
        P(("row", "col"), None, None),
        P(("row", "col"), None),
        P(),
        P(),
    )
    return jax.shard_map(
        body,
        mesh=mesh,
        in_specs=placed,
        out_specs=(P("row", "col"), P("row", "col")),
        check_vma=False,
    )
```

```python
import jax
import jax.numpy as jnp
from jax import lax
from jax.experimental import pallas as pl
from jax.experimental.pallas import tpu as pltpu
from jax.sharding import PartitionSpec as P

BLK = 128

cube_coef = 0.5
cell_volume = 0.03125
DM_SCALE = float(2**20)

F32 = jnp.float32
BF16 = jnp.bfloat16
MIB = 1 << 20


def gather_kernel(row_ref, col_ref, dens_ref, out_ref, sems):
    n = out_ref.shape[0]

    def copy(s):
        r = pl.multiple_of(row_ref[s] * BLK, BLK)
        c = pl.multiple_of(col_ref[s] * BLK, BLK)
        return pltpu.make_async_copy(
            dens_ref.at[pl.ds(r, BLK), pl.ds(c, BLK)], out_ref.at[s], sems.at[s]
        )

    def start(s, carry):
        copy(s).start()
        return carry

    def wait(s, carry):
        copy(s).wait()
        return carry

    lax.fori_loop(0, n, start, 0)
    lax.fori_loop(0, n, wait, 0)


def gather_blocks(density, row_pick, col_pick):
    n = row_pick.shape[0]
    return pl.pallas_call(
        gather_kernel,
        grid_spec=pltpu.PrefetchScalarGridSpec(
            num_scalar_prefetch=2,
            grid=(1,),
            in_specs=[pl.BlockSpec(memory_space=pl.ANY)],
            out_specs=pl.BlockSpec((n, BLK, BLK), lambda i, *_: (0, 0, 0)),
            scratch_shapes=[pltpu.SemaphoreType.DMA((n,))],
        ),
        out_shape=jax.ShapeDtypeStruct((n, BLK, BLK), F32),
        compiler_params=pltpu.CompilerParams(vmem_limit_bytes=56 * MIB),
        cost_estimate=pl.CostEstimate(
            flops=0, bytes_accessed=2 * n * BLK * BLK * 4, transcendentals=0
        ),
        name="gather_blocks",
    )(row_pick, col_pick, density)


def split(x):
    hi = x.astype(BF16)
    return hi, (x - hi.astype(F32)).astype(BF16)


def basis_kernel(count_ref, phi_ref, hi_ref, lo_ref, hit_ref, lot_ref):
    basis = phi_ref[0]
    column = lax.broadcasted_iota(jnp.int32, basis.shape, 1)
    masked = jnp.where(column < count_ref[pl.program_id(0)] * BLK, basis, 0.0)
    hi, lo = split(masked)
    hi_ref[0] = hi
    lo_ref[0] = lo
    hit_ref[0] = hi.T
    lot_ref[0] = lo.T


def split_basis(phi, counts):
    tdev, npts, local = phi.shape
    spec = pl.BlockSpec((1, npts, local), lambda t, *_: (t, 0, 0))
    spec_t = pl.BlockSpec((1, local, npts), lambda t, *_: (t, 0, 0))
    return pl.pallas_call(
        basis_kernel,
        grid_spec=pltpu.PrefetchScalarGridSpec(
            num_scalar_prefetch=1,
            grid=(tdev,),
            in_specs=[spec],
            out_specs=[spec, spec, spec_t, spec_t],
        ),
        out_shape=[jax.ShapeDtypeStruct((tdev, npts, local), BF16)] * 2
        + [jax.ShapeDtypeStruct((tdev, local, npts), BF16)] * 2,
        compiler_params=pltpu.CompilerParams(vmem_limit_bytes=40 * MIB),
        cost_estimate=pl.CostEstimate(
            flops=4 * phi.size, bytes_accessed=12 * phi.size, transcendentals=0
        ),
        name="split_basis",
    )(counts, phi)


def mm(x, y):
    return jnp.dot(x, y, preferred_element_type=F32)


def tile_kernel(
    hold_ref, count_ref, in_ref, hi_ref, lo_ref, hit_ref, lot_ref, v_ref, out_ref, dh_ref, dl_ref
):
    t = pl.program_id(0)
    maxb = hi_ref.shape[2] // BLK
    for i in range(maxb):
        for j in range(maxb):
            blk = in_ref[hold_ref[t, i * maxb + j]].astype(F32) * (1.0 / DM_SCALE)
            hi, lo = split(blk)
            dh_ref[i * BLK : (i + 1) * BLK, j * BLK : (j + 1) * BLK] = hi
            dl_ref[i * BLK : (i + 1) * BLK, j * BLK : (j + 1) * BLK] = lo
    count = count_ref[t]
    mh, ml = hi_ref[0], lo_ref[0]
    dh, dl = dh_ref[...], dl_ref[...]
    spread = mm(mh, dh) + (mm(ml, dh) + mm(mh, dl))
    masked = mh.astype(F32) + ml.astype(F32)
    rho = jnp.sum(spread * masked, axis=1, keepdims=True)
    potential = v_ref[0] + rho + cube_coef * rho * rho * rho
    wh, wl = split(masked * (potential * cell_volume))
    mht, mlt = hit_ref[0], lot_ref[0]
    ham = (mm(mht, wh) + (mm(mlt, wh) + mm(mht, wl))).astype(BF16)
    for i in range(maxb):
        for j in range(maxb):

            @pl.when((i < count) & (j < count))
            def _():
                out_ref[hold_ref[t, i * maxb + j]] = ham[
                    i * BLK : (i + 1) * BLK, j * BLK : (j + 1) * BLK
                ]


def tile_ham(incoming, basis, v_ext, hold, counts):
    n = incoming.shape[0]
    tdev, npts, local = basis[0].shape
    flops = tdev * 3 * 2 * 2 * npts * local * local
    spec = pl.BlockSpec((1, npts, local), lambda t, *_: (t, 0, 0))
    spec_t = pl.BlockSpec((1, local, npts), lambda t, *_: (t, 0, 0))
    return pl.pallas_call(
        tile_kernel,
        grid_spec=pltpu.PrefetchScalarGridSpec(
            num_scalar_prefetch=2,
            grid=(tdev,),
            in_specs=[
                pl.BlockSpec((n, BLK, BLK), lambda t, *_: (0, 0, 0)),
                spec,
                spec,
                spec_t,
                spec_t,
                pl.BlockSpec((1, npts, 1), lambda t, *_: (t, 0, 0)),
            ],
            out_specs=pl.BlockSpec((n, BLK, BLK), lambda t, *_: (0, 0, 0)),
            scratch_shapes=[
                pltpu.VMEM((local, local), BF16),
                pltpu.VMEM((local, local), BF16),
            ],
        ),
        out_shape=jax.ShapeDtypeStruct((n, BLK, BLK), BF16),
        compiler_params=pltpu.CompilerParams(vmem_limit_bytes=44 * MIB),
        cost_estimate=pl.CostEstimate(
            flops=flops, bytes_accessed=tdev * npts * local * 8, transcendentals=0
        ),
        name="tile_ham",
    )(hold, counts, incoming, *basis, v_ext[:, :, None])


def assemble(h_core, arriving, row_pick, col_pick, present, dtype, parts):
    rows, cols = h_core.shape
    n = arriving.shape[0]
    per = 2
    bm = per * BLK
    steps = rows // bm
    wide = cols // parts

    def kernel(row_ref, col_ref, present_ref, in_ref, h_ref, *rest):
        outs, (work_ref, num_ref, list_ref) = rest[:parts], rest[parts:]
        step = pl.program_id(0)

        @pl.when(step == 0)
        def _():
            def clear(g, carry):
                num_ref[g] = 0
                return carry

            def note(s, carry):
                @pl.when(present_ref[s] > 0)
                def _():
                    g = row_ref[s] // per
                    k = num_ref[g]
                    list_ref[g * n + k] = s
                    num_ref[g] = k + 1

                return carry

            lax.fori_loop(0, steps, clear, 0)
            lax.fori_loop(0, n, note, 0)

        work_ref[...] = h_ref[...]

        def add(k, carry):
            s = list_ref[step * n + k]
            top = pl.ds(pl.multiple_of((row_ref[s] - step * per) * BLK, BLK), BLK)
            left = pl.ds(pl.multiple_of(col_ref[s] * BLK, BLK), BLK)
            work_ref[top, left] = work_ref[top, left] + in_ref[s].astype(F32)
            return carry

        lax.fori_loop(0, num_ref[step], add, 0)
        for p in range(parts):
            outs[p][...] = work_ref[:, p * wide : (p + 1) * wide].astype(dtype)

    return pl.pallas_call(
        kernel,
        grid_spec=pltpu.PrefetchScalarGridSpec(
            num_scalar_prefetch=3,
            grid=(steps,),
            in_specs=[
                pl.BlockSpec((n, BLK, BLK), lambda i, *_: (0, 0, 0)),
                pl.BlockSpec((bm, cols), lambda i, *_: (i, 0)),
            ],
            out_specs=[pl.BlockSpec((bm, wide), lambda i, *_: (i, 0))] * parts,
            scratch_shapes=[
                pltpu.VMEM((bm, cols), F32),
                pltpu.SMEM((steps,), jnp.int32),
                pltpu.SMEM((steps * n,), jnp.int32),
            ],
        ),
        out_shape=[jax.ShapeDtypeStruct((rows, wide), dtype)] * parts,
        compiler_params=pltpu.CompilerParams(vmem_limit_bytes=56 * MIB),
        cost_estimate=pl.CostEstimate(
            flops=rows * cols, bytes_accessed=rows * cols * 6, transcendentals=0
        ),
        name="assemble",
    )(row_pick, col_pick, present, arriving, h_core)


def product(total, part, cols, dm_panel, pieces, fresh):
    ncol, rows, width = dm_panel.shape
    depth, wide = pieces[0][0][0].shape
    per = depth // width
    bm = min(512, rows)
    counts = [len(c) for c, _, _ in pieces]
    npiece = len(pieces)
    nh = sum(counts)
    scalars = jnp.stack(
        [jnp.asarray(s, jnp.int32) for _, _, s in pieces]
        + [jnp.asarray(w, jnp.int32) for _, w, _ in pieces]
    )

    def kernel(sc_ref, *refs):
        h_refs = refs[:nh]
        d_refs = refs[nh : nh + npiece]
        rest = refs[nh + npiece :]
        if total is not None:
            c_ref, rest = rest[0], rest[1:]
        out_ref = rest[0]
        held = rest[1 : 1 + npiece]
        sems = rest[1 + npiece]

        @pl.when(pl.program_id(0) == 0)
        def _():
            at = 0
            for p in range(npiece):
                for q in range(counts[p]):

                    @pl.when(sc_ref[npiece + p] == q)
                    def _(p=p, at=at):
                        pltpu.make_async_copy(h_refs[at], held[p], sems.at[p]).start()

                    at += 1
            first = 0
            for p in range(npiece):
                pltpu.make_async_copy(h_refs[first], held[p], sems.at[p]).wait()
                first += counts[p]

        acc = None
        for p in range(npiece):
            left = jnp.concatenate([d_refs[p][q] for q in range(per)], axis=1)
            term = mm(left, held[p][...])
            acc = term if acc is None else acc + term
        if not fresh:
            acc = acc + c_ref[...]
        out_ref[...] = acc

    def d_map(p):
        return lambda i, sc: (sc[p], i, 0)

    c_spec = pl.BlockSpec((bm, wide), lambda i, sc: (i, part))
    args = [h for c, _, _ in pieces for h in c] + [dm_panel] * npiece
    in_specs = [pl.BlockSpec(memory_space=pl.ANY)] * nh + [
        pl.BlockSpec((per, bm, width), d_map(p)) for p in range(npiece)
    ]
    aliases = {}
    if total is not None:
        aliases = {1 + len(args): 0}
        args.append(total)
        in_specs.append(pl.BlockSpec(memory_space=pl.ANY) if fresh else c_spec)
    return pl.pallas_call(
        kernel,
        grid_spec=pltpu.PrefetchScalarGridSpec(
            num_scalar_prefetch=1,
            grid=(rows // bm,),
            in_specs=in_specs,
            out_specs=c_spec,
            scratch_shapes=[pltpu.VMEM((depth, wide), BF16)] * npiece
            + [pltpu.SemaphoreType.DMA((npiece,))],
        ),
        out_shape=jax.ShapeDtypeStruct((rows, cols), F32),
        input_output_aliases=aliases,
        compiler_params=pltpu.CompilerParams(vmem_limit_bytes=56 * MIB),
        cost_estimate=pl.CostEstimate(
            flops=2 * npiece * rows * depth * wide,
            bytes_accessed=npiece * (rows + wide) * depth * 2 + rows * wide * 8,
            transcendentals=0,
        ),
        name="product",
    )(scalars, *args)


def body(density, h_core, phi, v_ext, tile_blocks, tile_count):
    nrow = lax.axis_size("row")
    ncol = lax.axis_size("col")
    ndev = nrow * ncol
    row_idx = lax.axis_index("row")
    col_idx = lax.axis_index("col")
    myself = row_idx * ncol + col_idx
    rows_loc, cols_loc = density.shape
    rowb = rows_loc // BLK
    colb = cols_loc // BLK
    tdev, npts, local = phi.shape
    maxb = tile_blocks.shape[1]

    blocks = tile_blocks.reshape(ndev, tdev, maxb)
    counts = tile_count.reshape(ndev, tdev)
    live = jnp.arange(maxb, dtype=jnp.int32)[None, None, :] < counts[:, :, None]
    row_hit = live & (blocks // rowb == row_idx)
    col_hit = live & (blocks // colb == col_idx)
    both = jnp.any(row_hit, axis=2) & jnp.any(col_hit, axis=2)
    row_in = jnp.sum(jnp.where(row_hit, blocks - row_idx * rowb, 0), axis=2)
    col_in = jnp.sum(jnp.where(col_hit, blocks - col_idx * colb, 0), axis=2)
    row_pick = jnp.sum(jnp.where(both, row_in, 0), axis=1)
    col_pick = jnp.sum(jnp.where(both, col_in, 0), axis=1)
    present = jnp.any(both, axis=1).astype(jnp.int32)
    mine = lax.dynamic_index_in_dim(blocks, myself, 0, keepdims=False)
    my_counts = lax.dynamic_index_in_dim(counts, myself, 0, keepdims=False)
    hold = ((mine // rowb)[:, :, None] * ncol + (mine // colb)[:, None, :]).reshape(tdev, -1)

    outgoing = (gather_blocks(density, row_pick, col_pick) * DM_SCALE).astype(jnp.float16)
    incoming = lax.all_to_all(outgoing, ("row", "col"), split_axis=0, concat_axis=0, tiled=True)

    later, _ = lax.optimization_barrier((density, outgoing))
    dm_panel = lax.all_gather(later.astype(BF16), "col", axis=0, tiled=False)

    basis = split_basis(phi, my_counts)
    returning = tile_ham(incoming.astype(F32), basis, v_ext, hold, my_counts)
    arriving = lax.all_to_all(returning, ("row", "col"), split_axis=0, concat_axis=0, tiled=True)
    where = (row_pick, col_pick, present)
    parts = 2 if nrow == 4 else 1
    low = assemble(h_core, arriving, *where, BF16, parts)
    (hamiltonian,) = assemble(h_core, arriving, *where, F32, 1)

    total = None
    if nrow == 4:
        swap = [(0, 1), (1, 0), (2, 3), (3, 2)]
        cross = [(1, 2), (2, 1)]
        outward = [(1, 0), (2, 3)]
        partner = [lax.ppermute(x, "row", swap) for x in low]
        near_mid = [lax.ppermute(x, "row", cross) for x in low]
        far_mid = [lax.ppermute(x, "row", cross) for x in partner]
        near_end = [lax.ppermute(x, "row", outward) for x in near_mid]
        far_end = [lax.ppermute(x, "row", outward) for x in far_mid]
        is_low = row_idx < 2
        is_end = ((row_idx == 0) | (row_idx == 3)).astype(jnp.int32)
        pair_idx = row_idx + 1 - 2 * (row_idx % 2)
        near_idx = jnp.where(is_low, 2, 1)
        far_idx = jnp.where(is_low, 3, 0)
        for p in range(parts):
            pieces = [((low[p],), 0, row_idx), ((partner[p],), 0, pair_idx)]
            total = product(total, p, cols_loc, dm_panel, pieces, True)
        for p in range(parts):
            pieces = [((near_mid[p], near_end[p]), is_end, near_idx)]
            total = product(total, p, cols_loc, dm_panel, pieces, False)
        for p in range(parts):
            pieces = [((far_mid[p], far_end[p]), is_end, far_idx)]
            total = product(total, p, cols_loc, dm_panel, pieces, False)
    else:
        ham_panel = lax.all_gather(low[0], "row", axis=0, tiled=False)
        for k in range(nrow):
            total = product(total, 0, cols_loc, dm_panel, [((ham_panel[k],), 0, k)], k == 0)
    return hamiltonian, total


def solution(mesh):
    placed = (
        P("row", "col"),
        P("row", "col"),
        P(("row", "col"), None, None),
        P(("row", "col"), None),
        P(),
        P(),
    )
    return jax.shard_map(
        body,
        mesh=mesh,
        in_specs=placed,
        out_specs=(P("row", "col"), P("row", "col")),
        check_vma=False,
    )
```

```python
import jax
import jax.numpy as jnp
from jax import lax
from jax.experimental import pallas as pl
from jax.experimental.pallas import tpu as pltpu
from jax.sharding import PartitionSpec as P

BLK = 128

cube_coef = 0.5
cell_volume = 0.03125
DM_SCALE = float(2**20)

F32 = jnp.float32
BF16 = jnp.bfloat16
MIB = 1 << 20


def gather_kernel(row_ref, col_ref, dens_ref, out_ref, sems):
    n = out_ref.shape[0]

    def copy(s):
        r = pl.multiple_of(row_ref[s] * BLK, BLK)
        c = pl.multiple_of(col_ref[s] * BLK, BLK)
        return pltpu.make_async_copy(
            dens_ref.at[pl.ds(r, BLK), pl.ds(c, BLK)], out_ref.at[s], sems.at[s]
        )

    def start(s, carry):
        copy(s).start()
        return carry

    def wait(s, carry):
        copy(s).wait()
        return carry

    lax.fori_loop(0, n, start, 0)
    lax.fori_loop(0, n, wait, 0)


def gather_blocks(density, row_pick, col_pick):
    n = row_pick.shape[0]
    return pl.pallas_call(
        gather_kernel,
        grid_spec=pltpu.PrefetchScalarGridSpec(
            num_scalar_prefetch=2,
            grid=(1,),
            in_specs=[pl.BlockSpec(memory_space=pl.ANY)],
            out_specs=pl.BlockSpec((n, BLK, BLK), lambda i, *_: (0, 0, 0)),
            scratch_shapes=[pltpu.SemaphoreType.DMA((n,))],
        ),
        out_shape=jax.ShapeDtypeStruct((n, BLK, BLK), F32),
        compiler_params=pltpu.CompilerParams(vmem_limit_bytes=56 * MIB),
        cost_estimate=pl.CostEstimate(
            flops=0, bytes_accessed=2 * n * BLK * BLK * 4, transcendentals=0
        ),
        name="gather_blocks",
    )(row_pick, col_pick, density)


def split(x):
    hi = x.astype(BF16)
    return hi, (x - hi.astype(F32)).astype(BF16)


def basis_kernel(count_ref, phi_ref, hi_ref, lo_ref, hit_ref, lot_ref):
    basis = phi_ref[0]
    column = lax.broadcasted_iota(jnp.int32, basis.shape, 1)
    masked = jnp.where(column < count_ref[pl.program_id(0)] * BLK, basis, 0.0)
    hi, lo = split(masked)
    hi_ref[0] = hi
    lo_ref[0] = lo
    hit_ref[0] = hi.T
    lot_ref[0] = lo.T


def split_basis(phi, counts):
    tdev, npts, local = phi.shape
    spec = pl.BlockSpec((1, npts, local), lambda t, *_: (t, 0, 0))
    spec_t = pl.BlockSpec((1, local, npts), lambda t, *_: (t, 0, 0))
    return pl.pallas_call(
        basis_kernel,
        grid_spec=pltpu.PrefetchScalarGridSpec(
            num_scalar_prefetch=1,
            grid=(tdev,),
            in_specs=[spec],
            out_specs=[spec, spec, spec_t, spec_t],
        ),
        out_shape=[jax.ShapeDtypeStruct((tdev, npts, local), BF16)] * 2
        + [jax.ShapeDtypeStruct((tdev, local, npts), BF16)] * 2,
        compiler_params=pltpu.CompilerParams(vmem_limit_bytes=40 * MIB),
        cost_estimate=pl.CostEstimate(
            flops=4 * phi.size, bytes_accessed=12 * phi.size, transcendentals=0
        ),
        name="split_basis",
    )(counts, phi)


def mm(x, y):
    return jnp.dot(x, y, preferred_element_type=F32)


def tile_kernel(
    hold_ref, count_ref, in_ref, hi_ref, lo_ref, hit_ref, lot_ref, v_ref, out_ref, dh_ref, dl_ref
):
    t = pl.program_id(0)
    maxb = hi_ref.shape[2] // BLK
    for i in range(maxb):
        for j in range(maxb):
            blk = in_ref[hold_ref[t, i * maxb + j]].astype(F32) * (1.0 / DM_SCALE)
            hi, lo = split(blk)
            dh_ref[i * BLK : (i + 1) * BLK, j * BLK : (j + 1) * BLK] = hi
            dl_ref[i * BLK : (i + 1) * BLK, j * BLK : (j + 1) * BLK] = lo
    count = count_ref[t]
    mh, ml = hi_ref[0], lo_ref[0]
    dh, dl = dh_ref[...], dl_ref[...]
    spread = mm(mh, dh) + (mm(ml, dh) + mm(mh, dl))
    masked = mh.astype(F32) + ml.astype(F32)
    rho = jnp.sum(spread * masked, axis=1, keepdims=True)
    potential = v_ref[0] + rho + cube_coef * rho * rho * rho
    wh, wl = split(masked * (potential * cell_volume))
    mht, mlt = hit_ref[0], lot_ref[0]
    ham = (mm(mht, wh) + (mm(mlt, wh) + mm(mht, wl))).astype(BF16)
    for i in range(maxb):
        for j in range(maxb):

            @pl.when((i < count) & (j < count))
            def _():
                out_ref[hold_ref[t, i * maxb + j]] = ham[
                    i * BLK : (i + 1) * BLK, j * BLK : (j + 1) * BLK
                ]


def tile_ham(incoming, basis, v_ext, hold, counts):
    n = incoming.shape[0]
    tdev, npts, local = basis[0].shape
    flops = tdev * 3 * 2 * 2 * npts * local * local
    spec = pl.BlockSpec((1, npts, local), lambda t, *_: (t, 0, 0))
    spec_t = pl.BlockSpec((1, local, npts), lambda t, *_: (t, 0, 0))
    return pl.pallas_call(
        tile_kernel,
        grid_spec=pltpu.PrefetchScalarGridSpec(
            num_scalar_prefetch=2,
            grid=(tdev,),
            in_specs=[
                pl.BlockSpec((n, BLK, BLK), lambda t, *_: (0, 0, 0)),
                spec,
                spec,
                spec_t,
                spec_t,
                pl.BlockSpec((1, npts, 1), lambda t, *_: (t, 0, 0)),
            ],
            out_specs=pl.BlockSpec((n, BLK, BLK), lambda t, *_: (0, 0, 0)),
            scratch_shapes=[
                pltpu.VMEM((local, local), BF16),
                pltpu.VMEM((local, local), BF16),
            ],
        ),
        out_shape=jax.ShapeDtypeStruct((n, BLK, BLK), BF16),
        compiler_params=pltpu.CompilerParams(vmem_limit_bytes=44 * MIB),
        cost_estimate=pl.CostEstimate(
            flops=flops, bytes_accessed=tdev * npts * local * 8, transcendentals=0
        ),
        name="tile_ham",
    )(hold, counts, incoming, *basis, v_ext[:, :, None])


def assemble(h_core, arriving, picks, dtype, parts):
    nband = len(h_core)
    rows, cols = sum(x.shape[0] for x in h_core), h_core[0].shape[1]
    n = arriving.shape[0]
    per = 2
    bm = per * BLK
    steps = rows // bm
    wide = cols // parts
    widen = h_core[0].dtype != F32
    narrow = dtype != F32
    source = [(k, g) for k, x in enumerate(h_core) for g in range(x.shape[0] // bm)]

    def kernel(row_ref, col_ref, present_ref, in_ref, *rest):
        h_refs, outs, rest = rest[:nband], rest[nband : nband + parts], rest[nband + parts :]
        work_ref, in_sems, out_sems, num_ref, list_ref = rest[:5]
        rest = rest[5:]
        raw_ref = work_ref
        if widen:
            raw_ref, rest = rest[0], rest[1:]
        low_refs = rest if narrow else (work_ref,)

        def band(g):
            return pl.ds(g * bm, bm)

        def read(g):
            k, at = source[g]
            return pltpu.make_async_copy(
                h_refs[k].at[band(at)], raw_ref.at[band(g)], in_sems.at[g]
            )

        def write(g, p):
            return pltpu.make_async_copy(
                low_refs[p].at[band(g)], outs[p].at[band(g)], out_sems.at[g, p]
            )

        for g in range(steps):
            read(g).start()
            num_ref[g] = 0

        def note(s, carry):
            @pl.when(present_ref[s] > 0)
            def _():
                g = row_ref[s] // per
                k = num_ref[g]
                list_ref[g * n + k] = s
                num_ref[g] = k + 1

            return carry

        lax.fori_loop(0, n, note, 0)

        for g in range(steps):
            read(g).wait()
            if widen:
                work_ref[band(g), :] = raw_ref[band(g), :].astype(F32)

            def add(k, carry, g=g):
                s = list_ref[g * n + k]
                top = pl.ds(pl.multiple_of(row_ref[s] * BLK, BLK), BLK)
                left = pl.ds(pl.multiple_of(col_ref[s] * BLK, BLK), BLK)
                work_ref[top, left] = work_ref[top, left] + in_ref[s].astype(F32)
                return carry

            lax.fori_loop(0, num_ref[g], add, 0)
            for p in range(parts):
                if narrow:
                    low_refs[p][band(g), :] = work_ref[band(g), p * wide : (p + 1) * wide].astype(
                        dtype
                    )
                write(g, p).start()
        for g in range(steps):
            for p in range(parts):
                write(g, p).wait()

    scratch = [
        pltpu.VMEM((rows, cols), F32),
        pltpu.SemaphoreType.DMA((steps,)),
        pltpu.SemaphoreType.DMA((steps, parts)),
        pltpu.SMEM((steps,), jnp.int32),
        pltpu.SMEM((steps * n,), jnp.int32),
    ]
    if widen:
        scratch.append(pltpu.VMEM((rows, cols), h_core[0].dtype))
    if narrow:
        scratch.extend([pltpu.VMEM((rows, wide), dtype)] * parts)
    return pl.pallas_call(
        kernel,
        grid_spec=pltpu.PrefetchScalarGridSpec(
            num_scalar_prefetch=3,
            grid=(1,),
            in_specs=[
                pl.BlockSpec((n, BLK, BLK), lambda i, *_: (0, 0, 0)),
            ]
            + [pl.BlockSpec(memory_space=pl.ANY)] * nband,
            out_specs=[pl.BlockSpec(memory_space=pl.ANY)] * parts,
            scratch_shapes=scratch,
        ),
        out_shape=[jax.ShapeDtypeStruct((rows, wide), dtype)] * parts,
        compiler_params=pltpu.CompilerParams(vmem_limit_bytes=56 * MIB),
        cost_estimate=pl.CostEstimate(
            flops=rows * cols, bytes_accessed=rows * cols * 6, transcendentals=0
        ),
        name="assemble",
    )(*picks, arriving, *h_core)


def product(cols, dm_panel, pieces):
    ncol, rows, width = dm_panel.shape
    depth = pieces[0][0][0][0].shape[0]
    per = depth // width
    bm = min(512, rows)
    npiece = len(pieces)
    nh = sum(len(arrays) for c, _, _ in pieces for arrays in c)
    scalars = jnp.stack(
        [jnp.asarray(s, jnp.int32) for _, _, s in pieces]
        + [jnp.asarray(w, jnp.int32) for _, w, _ in pieces]
    )

    def kernel(sc_ref, *refs):
        h_refs = refs[:nh]
        d_refs = refs[nh : nh + npiece]
        out_ref = refs[nh + npiece]
        held = refs[nh + npiece + 1 : -1]
        sems = refs[-1]

        @pl.when(pl.program_id(0) == 0)
        def _():
            at = 0
            for p, (candidates, _, _) in enumerate(pieces):
                for q, arrays in enumerate(candidates):
                    mine = h_refs[at : at + len(arrays)]
                    at += len(arrays)

                    @pl.when(sc_ref[npiece + p] == q)
                    def _(p=p, mine=mine):
                        left = 0
                        for ref in mine:
                            right = left + ref.shape[1]
                            pltpu.make_async_copy(
                                ref, held[p].at[:, left:right], sems.at[p]
                            ).start()
                            left = right

            for p in range(npiece):
                pltpu.make_async_copy(held[p], held[p], sems.at[p]).wait()

        acc = None
        for p in range(npiece):
            for q in range(per):
                term = mm(d_refs[p][q], held[p][q * width : (q + 1) * width, :])
                acc = term if acc is None else acc + term
        out_ref[...] = acc

    def d_map(p):
        return lambda i, sc: (sc[p], i, 0)

    return pl.pallas_call(
        kernel,
        grid_spec=pltpu.PrefetchScalarGridSpec(
            num_scalar_prefetch=1,
            grid=(rows // bm,),
            in_specs=[pl.BlockSpec(memory_space=pl.ANY)] * nh
            + [pl.BlockSpec((per, bm, width), d_map(p)) for p in range(npiece)],
            out_specs=pl.BlockSpec((bm, cols), lambda i, sc: (i, 0)),
            scratch_shapes=[pltpu.VMEM((depth, cols), BF16)] * npiece
            + [pltpu.SemaphoreType.DMA((npiece,))],
        ),
        out_shape=jax.ShapeDtypeStruct((rows, cols), F32),
        compiler_params=pltpu.CompilerParams(vmem_limit_bytes=56 * MIB),
        cost_estimate=pl.CostEstimate(
            flops=2 * npiece * rows * depth * cols,
            bytes_accessed=npiece * (rows + cols) * depth * 2 + rows * cols * 4,
            transcendentals=0,
        ),
        name="product",
    )(scalars, *[x for c, _, _ in pieces for arrays in c for x in arrays], *[dm_panel] * npiece)


def product_add(total, part, dm_panel, candidates, which, shard):
    ncol, rows, width = dm_panel.shape
    depth, wide = candidates[0].shape
    per = depth // width
    bm = min(512, rows)
    steps = rows // bm
    nh = len(candidates)
    scalars = jnp.stack([jnp.asarray(which, jnp.int32), jnp.asarray(shard, jnp.int32)])

    def kernel(sc_ref, *refs):
        h_refs = refs[:nh]
        dm_ref, total_ref, out_ref, held, d_ref, c_ref, h_sem, d_sems, c_sems, o_sems = refs[nh:]
        columns = pl.ds(part * wide, wide)

        def read_d(i, q):
            return pltpu.make_async_copy(
                dm_ref.at[sc_ref[1] * per + q, pl.ds(i * bm, bm)],
                d_ref.at[i, :, pl.ds(q * width, width)],
                d_sems.at[i, q],
            )

        def read_c(i):
            return pltpu.make_async_copy(
                total_ref.at[pl.ds(i * bm, bm), columns], c_ref.at[i], c_sems.at[i]
            )

        def write(i):
            return pltpu.make_async_copy(
                c_ref.at[i], out_ref.at[pl.ds(i * bm, bm), columns], o_sems.at[i]
            )

        for k in range(nh):

            @pl.when(sc_ref[0] == k)
            def _(k=k):
                pltpu.make_async_copy(h_refs[k], held, h_sem.at[0]).start()

        for i in range(steps):
            for q in range(per):
                read_d(i, q).start()
            read_c(i).start()
        pltpu.make_async_copy(h_refs[0], held, h_sem.at[0]).wait()
        for i in range(steps):
            for q in range(per):
                read_d(i, q).wait()
            read_c(i).wait()
            c_ref[i] = c_ref[i] + mm(d_ref[i], held[...])
            write(i).start()
        for i in range(steps):
            write(i).wait()

    return pl.pallas_call(
        kernel,
        grid_spec=pltpu.PrefetchScalarGridSpec(
            num_scalar_prefetch=1,
            grid=(1,),
            in_specs=[pl.BlockSpec(memory_space=pl.ANY)] * (nh + 2),
            out_specs=pl.BlockSpec(memory_space=pl.ANY),
            scratch_shapes=[
                pltpu.VMEM((depth, wide), BF16),
                pltpu.VMEM((steps, bm, depth), BF16),
                pltpu.VMEM((steps, bm, wide), F32),
                pltpu.SemaphoreType.DMA((1,)),
                pltpu.SemaphoreType.DMA((steps, per)),
                pltpu.SemaphoreType.DMA((steps,)),
                pltpu.SemaphoreType.DMA((steps,)),
            ],
        ),
        out_shape=jax.ShapeDtypeStruct(total.shape, F32),
        input_output_aliases={2 + nh: 0},
        compiler_params=pltpu.CompilerParams(vmem_limit_bytes=56 * MIB),
        cost_estimate=pl.CostEstimate(
            flops=2 * rows * depth * wide,
            bytes_accessed=(rows + wide) * depth * 2 + rows * wide * 8,
            transcendentals=0,
        ),
        name="product_add",
    )(scalars, *candidates, dm_panel, total)


PARTS = 2
EARLY = (2, 1, 1, 1, 3)


def tie(x, y):
    return lax.optimization_barrier((x, y))


def body(density, h_core, phi, v_ext, tile_blocks, tile_count):
    nrow = lax.axis_size("row")
    ncol = lax.axis_size("col")
    ndev = nrow * ncol
    row_idx = lax.axis_index("row")
    col_idx = lax.axis_index("col")
    myself = row_idx * ncol + col_idx
    rows_loc, cols_loc = density.shape
    rowb = rows_loc // BLK
    colb = cols_loc // BLK
    tdev, npts, local = phi.shape
    maxb = tile_blocks.shape[1]
    line = nrow == 4

    inward = [(0, 1), (3, 2)]
    cross = [(1, 2), (2, 1)]
    outward = [(1, 0), (2, 3)]

    blocks = tile_blocks.reshape(ndev, tdev, maxb)
    counts = tile_count.reshape(ndev, tdev)
    live = jnp.arange(maxb, dtype=jnp.int32)[None, None, :] < counts[:, :, None]
    col_hit = live & (blocks // colb == col_idx)
    col_in = jnp.sum(jnp.where(col_hit, blocks - col_idx * colb, 0), axis=2)

    def picks_of(row):
        row_hit = live & (blocks // rowb == row)
        both = jnp.any(row_hit, axis=2) & jnp.any(col_hit, axis=2)
        row_in = jnp.sum(jnp.where(row_hit, blocks - row * rowb, 0), axis=2)
        row_pick = jnp.sum(jnp.where(both, row_in, 0), axis=1)
        col_pick = jnp.sum(jnp.where(both, col_in, 0), axis=1)
        return row_pick, col_pick, jnp.any(both, axis=1).astype(jnp.int32)

    picks = picks_of(row_idx)
    mine = lax.dynamic_index_in_dim(blocks, myself, 0, keepdims=False)
    my_counts = lax.dynamic_index_in_dim(counts, myself, 0, keepdims=False)
    hold = ((mine // rowb)[:, :, None] * ncol + (mine // colb)[:, None, :]).reshape(tdev, -1)

    if line:
        unit = rows_loc // sum(EARLY)
        tops = [unit * sum(EARLY[:k]) for k in range(len(EARLY))]
        early = [
            lax.ppermute(h_core[t : t + unit * k].astype(BF16), "row", outward)
            for t, k in zip(tops, EARLY)
        ]
    outgoing = (gather_blocks(density, picks[0], picks[1]) * DM_SCALE).astype(jnp.float16)
    incoming = lax.all_to_all(outgoing, ("row", "col"), split_axis=0, concat_axis=0, tiled=True)

    later, _ = lax.optimization_barrier((density, outgoing))
    dm_panel = lax.all_gather(later.astype(BF16), "col", axis=0, tiled=False)

    basis = split_basis(phi, my_counts)
    if line:
        incoming, early[0] = tie(incoming, early[0])
    returning = tile_ham(incoming.astype(F32), basis, v_ext, hold, my_counts)
    if line:
        returning, early[1] = tie(returning, early[1])
    arriving = lax.all_to_all(returning, ("row", "col"), split_axis=0, concat_axis=0, tiled=True)
    if line:
        arriving, early[2] = tie(arriving, early[2])
    low = assemble([h_core], arriving, picks, BF16, PARTS if line else 1)
    (hamiltonian,) = assemble([h_core], arriving, picks, F32, 1)

    if line:
        pair_idx = row_idx + 1 - 2 * (row_idx % 2)
        is_low = row_idx < 2
        is_end = ((row_idx == 0) | (row_idx == 3)).astype(jnp.int32)
        near_idx = jnp.where(is_low, 2, 1)
        far_idx = jnp.where(is_low, 3, 0)
        pair_blocks = lax.ppermute(arriving, "row", outward)
        low, early[3] = tie(low, early[3])
        near_mid = [lax.ppermute(x, "row", cross) for x in low]
        pair_mid = []
        for p in range(PARTS):
            ready = low[p] if p == 0 else tie(low[p], near_mid[p - 1])[0]
            pair_mid.append(lax.ppermute(ready, "row", inward))
        ready, (pair_blocks, early[4]) = tie(near_mid[0], (pair_blocks, early[4]))
        near_end = [lax.ppermute(x, "row", outward) for x in [ready] + near_mid[1:]]
        far_mid = [lax.ppermute(pair_mid[0], "row", cross)]
        for p in range(1, PARTS):
            ready, near_end[p - 1] = tie(pair_mid[p], near_end[p - 1])
            far_mid.append(lax.ppermute(ready, "row", cross))
        ready, near_end[-1] = tie(far_mid[0], near_end[-1])
        far_end = [lax.ppermute(x, "row", outward) for x in [ready] + far_mid[1:]]
        pair_end = assemble(early, pair_blocks, picks_of(pair_idx), BF16, 1)
        total = product(
            cols_loc,
            dm_panel,
            [
                ((low,), 0, row_idx),
                ((pair_mid, pair_end), is_end, pair_idx),
                ((near_mid, near_end), is_end, near_idx),
            ],
        )
        for p in range(PARTS):
            total = product_add(
                total, p, dm_panel, (far_mid[p], far_end[p]), is_end, far_idx
            )
    else:
        ham_panel = lax.all_gather(low[0], "row", axis=0, tiled=False)
        total = product(cols_loc, dm_panel, [(((ham_panel[0],),), 0, 0)])
        for k in range(1, nrow):
            total = product_add(total, 0, dm_panel, (ham_panel[k],), 0, k)
    return hamiltonian, total


def solution(mesh):
    placed = (
        P("row", "col"),
        P("row", "col"),
        P(("row", "col"), None, None),
        P(("row", "col"), None),
        P(),
        P(),
    )
    return jax.shard_map(
        body,
        mesh=mesh,
        in_specs=placed,
        out_specs=(P("row", "col"), P("row", "col")),
        check_vma=False,
    )
```

```python
import jax
import jax.numpy as jnp
from jax import lax
from jax.experimental import pallas as pl
from jax.experimental.pallas import tpu as pltpu
from jax.sharding import PartitionSpec as P

BLK = 128

cube_coef = 0.5
cell_volume = 0.03125
DM_SCALE = float(2**20)

F32 = jnp.float32
BF16 = jnp.bfloat16
MIB = 1 << 20
AHEAD = 3


def gather_kernel(row_ref, col_ref, dens_ref, out_ref, sems):
    n = out_ref.shape[0]

    def copy(s):
        r = pl.multiple_of(row_ref[s] * BLK, BLK)
        c = pl.multiple_of(col_ref[s] * BLK, BLK)
        return pltpu.make_async_copy(
            dens_ref.at[pl.ds(r, BLK), pl.ds(c, BLK)], out_ref.at[s], sems.at[s]
        )

    def start(s, carry):
        copy(s).start()
        return carry

    def wait(s, carry):
        copy(s).wait()
        return carry

    lax.fori_loop(0, n, start, 0)
    lax.fori_loop(0, n, wait, 0)


def gather_blocks(density, row_pick, col_pick):
    n = row_pick.shape[0]
    return pl.pallas_call(
        gather_kernel,
        grid_spec=pltpu.PrefetchScalarGridSpec(
            num_scalar_prefetch=2,
            grid=(1,),
            in_specs=[pl.BlockSpec(memory_space=pl.ANY)],
            out_specs=pl.BlockSpec((n, BLK, BLK), lambda i, *_: (0, 0, 0)),
            scratch_shapes=[pltpu.SemaphoreType.DMA((n,))],
        ),
        out_shape=jax.ShapeDtypeStruct((n, BLK, BLK), F32),
        compiler_params=pltpu.CompilerParams(vmem_limit_bytes=56 * MIB),
        cost_estimate=pl.CostEstimate(
            flops=0, bytes_accessed=2 * n * BLK * BLK * 4, transcendentals=0
        ),
        name="gather_blocks",
    )(row_pick, col_pick, density)


def round_bands(x, top, sizes):
    cols = x.shape[1]
    bm = min(256, min(sizes))
    source = [(k, g) for k, size in enumerate(sizes) for g in range(size // bm)]
    steps = len(source)

    def kernel(x_ref, *rest):
        outs = rest[: len(sizes)]
        raw_ref, low_ref, in_sems, out_sems = rest[len(sizes) :]

        def read(g):
            return pltpu.make_async_copy(
                x_ref.at[pl.ds(top + g * bm, bm)], raw_ref.at[g], in_sems.at[g]
            )

        def write(g):
            k, at = source[g]
            return pltpu.make_async_copy(
                low_ref.at[g], outs[k].at[pl.ds(at * bm, bm)], out_sems.at[g]
            )

        for g in range(min(AHEAD, steps)):
            read(g).start()
        for g in range(steps):
            read(g).wait()
            if g + AHEAD < steps:
                read(g + AHEAD).start()
            low_ref[g] = raw_ref[g].astype(BF16)
            write(g).start()
        for g in range(steps):
            write(g).wait()

    return pl.pallas_call(
        kernel,
        grid=(1,),
        in_specs=[pl.BlockSpec(memory_space=pl.ANY)],
        out_specs=[pl.BlockSpec(memory_space=pl.ANY)] * len(sizes),
        scratch_shapes=[
            pltpu.VMEM((steps, bm, cols), F32),
            pltpu.VMEM((steps, bm, cols), BF16),
            pltpu.SemaphoreType.DMA((steps,)),
            pltpu.SemaphoreType.DMA((steps,)),
        ],
        out_shape=[jax.ShapeDtypeStruct((size, cols), BF16) for size in sizes],
        compiler_params=pltpu.CompilerParams(vmem_limit_bytes=56 * MIB),
        cost_estimate=pl.CostEstimate(
            flops=sum(sizes) * cols, bytes_accessed=sum(sizes) * cols * 6, transcendentals=0
        ),
        name="round_bands",
    )(x)


def split(x):
    hi = x.astype(BF16)
    return hi, (x - hi.astype(F32)).astype(BF16)


def basis_kernel(count_ref, phi_ref, hi_ref, lo_ref, hit_ref, lot_ref):
    basis = phi_ref[0]
    column = lax.broadcasted_iota(jnp.int32, basis.shape, 1)
    masked = jnp.where(column < count_ref[pl.program_id(0)] * BLK, basis, 0.0)
    hi, lo = split(masked)
    hi_ref[0] = hi
    lo_ref[0] = lo
    hit_ref[0] = hi.T
    lot_ref[0] = lo.T


def split_basis(phi, counts):
    tdev, npts, local = phi.shape
    spec = pl.BlockSpec((1, npts, local), lambda t, *_: (t, 0, 0))
    spec_t = pl.BlockSpec((1, local, npts), lambda t, *_: (t, 0, 0))
    return pl.pallas_call(
        basis_kernel,
        grid_spec=pltpu.PrefetchScalarGridSpec(
            num_scalar_prefetch=1,
            grid=(tdev,),
            in_specs=[spec],
            out_specs=[spec, spec, spec_t, spec_t],
        ),
        out_shape=[jax.ShapeDtypeStruct((tdev, npts, local), BF16)] * 2
        + [jax.ShapeDtypeStruct((tdev, local, npts), BF16)] * 2,
        compiler_params=pltpu.CompilerParams(vmem_limit_bytes=40 * MIB),
        cost_estimate=pl.CostEstimate(
            flops=4 * phi.size, bytes_accessed=12 * phi.size, transcendentals=0
        ),
        name="split_basis",
    )(counts, phi)


def mm(x, y):
    return jnp.dot(x, y, preferred_element_type=F32)


def tile_kernel(
    hold_ref,
    count_ref,
    in_ref,
    hi_ref,
    lo_ref,
    hit_ref,
    lot_ref,
    v_ref,
    dens_ref,
    out_ref,
    dens_low_ref,
    dh_ref,
    dl_ref,
):
    t = pl.program_id(0)
    dens_low_ref[...] = dens_ref[...].astype(BF16)
    maxb = hi_ref.shape[2] // BLK
    for i in range(maxb):
        for j in range(maxb):
            blk = in_ref[hold_ref[t, i * maxb + j]].astype(F32) * (1.0 / DM_SCALE)
            hi, lo = split(blk)
            dh_ref[i * BLK : (i + 1) * BLK, j * BLK : (j + 1) * BLK] = hi
            dl_ref[i * BLK : (i + 1) * BLK, j * BLK : (j + 1) * BLK] = lo
    count = count_ref[t]
    mh, ml = hi_ref[0], lo_ref[0]
    dh, dl = dh_ref[...], dl_ref[...]
    spread = mm(mh, dh) + (mm(ml, dh) + mm(mh, dl))
    masked = mh.astype(F32) + ml.astype(F32)
    rho = jnp.sum(spread * masked, axis=1, keepdims=True)
    potential = v_ref[0] + rho + cube_coef * rho * rho * rho
    wh, wl = split(masked * (potential * cell_volume))
    mht, mlt = hit_ref[0], lot_ref[0]
    ham = (mm(mht, wh) + (mm(mlt, wh) + mm(mht, wl))).astype(BF16)
    for i in range(maxb):
        for j in range(maxb):

            @pl.when((i < count) & (j < count))
            def _():
                out_ref[hold_ref[t, i * maxb + j]] = ham[
                    i * BLK : (i + 1) * BLK, j * BLK : (j + 1) * BLK
                ]


def tile_ham(incoming, basis, v_ext, hold, counts, density):
    n = incoming.shape[0]
    rows, cols = density.shape
    band = pl.BlockSpec((rows // basis[0].shape[0], cols), lambda t, *_: (t, 0))
    tdev, npts, local = basis[0].shape
    flops = tdev * 3 * 2 * 2 * npts * local * local
    spec = pl.BlockSpec((1, npts, local), lambda t, *_: (t, 0, 0))
    spec_t = pl.BlockSpec((1, local, npts), lambda t, *_: (t, 0, 0))
    return pl.pallas_call(
        tile_kernel,
        grid_spec=pltpu.PrefetchScalarGridSpec(
            num_scalar_prefetch=2,
            grid=(tdev,),
            in_specs=[
                pl.BlockSpec((n, BLK, BLK), lambda t, *_: (0, 0, 0)),
                spec,
                spec,
                spec_t,
                spec_t,
                pl.BlockSpec((1, npts, 1), lambda t, *_: (t, 0, 0)),
                band,
            ],
            out_specs=[pl.BlockSpec((n, BLK, BLK), lambda t, *_: (0, 0, 0)), band],
            scratch_shapes=[
                pltpu.VMEM((local, local), BF16),
                pltpu.VMEM((local, local), BF16),
            ],
        ),
        out_shape=[
            jax.ShapeDtypeStruct((n, BLK, BLK), BF16),
            jax.ShapeDtypeStruct((rows, cols), BF16),
        ],
        compiler_params=pltpu.CompilerParams(vmem_limit_bytes=52 * MIB),
        cost_estimate=pl.CostEstimate(
            flops=flops, bytes_accessed=tdev * npts * local * 8, transcendentals=0
        ),
        name="tile_ham",
    )(hold, counts, incoming, *basis, v_ext[:, :, None], density)


def assemble(h_core, arriving, picks, dtype, parts):
    nband = len(h_core)
    rows, cols = sum(x.shape[0] for x in h_core), h_core[0].shape[1]
    n = arriving.shape[0]
    per = 2
    bm = per * BLK
    steps = rows // bm
    wide = cols // parts
    widen = h_core[0].dtype != F32
    narrow = dtype != F32
    source = [(k, g) for k, x in enumerate(h_core) for g in range(x.shape[0] // bm)]

    def kernel(row_ref, col_ref, present_ref, in_ref, *rest):
        h_refs, outs, rest = rest[:nband], rest[nband : nband + parts], rest[nband + parts :]
        work_ref, in_sems, out_sems, num_ref, list_ref = rest[:5]
        rest = rest[5:]
        raw_ref = work_ref
        if widen:
            raw_ref, rest = rest[0], rest[1:]
        low_refs = rest if narrow else (work_ref,)

        def band(g):
            return pl.ds(g * bm, bm)

        def read(g):
            k, at = source[g]
            return pltpu.make_async_copy(
                h_refs[k].at[band(at)], raw_ref.at[band(g)], in_sems.at[g]
            )

        def write(g, p):
            return pltpu.make_async_copy(
                low_refs[p].at[band(g)], outs[p].at[band(g)], out_sems.at[g, p]
            )

        for g in range(min(AHEAD, steps)):
            read(g).start()
        for g in range(steps):
            num_ref[g] = 0

        def note(s, carry):
            @pl.when(present_ref[s] > 0)
            def _():
                g = row_ref[s] // per
                k = num_ref[g]
                list_ref[g * n + k] = s
                num_ref[g] = k + 1

            return carry

        lax.fori_loop(0, n, note, 0)

        for g in range(steps):
            read(g).wait()
            if g + AHEAD < steps:
                read(g + AHEAD).start()
            if widen:
                work_ref[band(g), :] = raw_ref[band(g), :].astype(F32)

            def add(k, carry, g=g):
                s = list_ref[g * n + k]
                top = pl.ds(pl.multiple_of(row_ref[s] * BLK, BLK), BLK)
                left = pl.ds(pl.multiple_of(col_ref[s] * BLK, BLK), BLK)
                work_ref[top, left] = work_ref[top, left] + in_ref[s].astype(F32)
                return carry

            lax.fori_loop(0, num_ref[g], add, 0)
            for p in range(parts):
                if narrow:
                    low_refs[p][band(g), :] = work_ref[band(g), p * wide : (p + 1) * wide].astype(
                        dtype
                    )
                write(g, p).start()
        for g in range(steps):
            for p in range(parts):
                write(g, p).wait()

    scratch = [
        pltpu.VMEM((rows, cols), F32),
        pltpu.SemaphoreType.DMA((steps,)),
        pltpu.SemaphoreType.DMA((steps, parts)),
        pltpu.SMEM((steps,), jnp.int32),
        pltpu.SMEM((steps * n,), jnp.int32),
    ]
    if widen:
        scratch.append(pltpu.VMEM((rows, cols), h_core[0].dtype))
    if narrow:
        scratch.extend([pltpu.VMEM((rows, wide), dtype)] * parts)
    return pl.pallas_call(
        kernel,
        grid_spec=pltpu.PrefetchScalarGridSpec(
            num_scalar_prefetch=3,
            grid=(1,),
            in_specs=[
                pl.BlockSpec((n, BLK, BLK), lambda i, *_: (0, 0, 0)),
            ]
            + [pl.BlockSpec(memory_space=pl.ANY)] * nband,
            out_specs=[pl.BlockSpec(memory_space=pl.ANY)] * parts,
            scratch_shapes=scratch,
        ),
        out_shape=[jax.ShapeDtypeStruct((rows, wide), dtype)] * parts,
        compiler_params=pltpu.CompilerParams(vmem_limit_bytes=56 * MIB),
        cost_estimate=pl.CostEstimate(
            flops=rows * cols, bytes_accessed=rows * cols * 6, transcendentals=0
        ),
        name="assemble",
    )(*picks, arriving, *h_core)


def product(cols, dm_panel, pieces):
    ncol, rows, width = dm_panel.shape
    depth = pieces[0][0][0][0].shape[0]
    per = depth // width
    bm = min(512, rows)
    npiece = len(pieces)
    nh = sum(len(arrays) for c, _, _ in pieces for arrays in c)
    scalars = jnp.stack(
        [jnp.asarray(s, jnp.int32) for _, _, s in pieces]
        + [jnp.asarray(w, jnp.int32) for _, w, _ in pieces]
    )

    def kernel(sc_ref, *refs):
        h_refs = refs[:nh]
        d_refs = refs[nh : nh + npiece]
        out_ref = refs[nh + npiece]
        held = refs[nh + npiece + 1 : -1]
        sems = refs[-1]

        @pl.when(pl.program_id(0) == 0)
        def _():
            at = 0
            for p, (candidates, _, _) in enumerate(pieces):
                for q, arrays in enumerate(candidates):
                    mine = h_refs[at : at + len(arrays)]
                    at += len(arrays)

                    @pl.when(sc_ref[npiece + p] == q)
                    def _(p=p, mine=mine):
                        left = 0
                        for ref in mine:
                            right = left + ref.shape[1]
                            pltpu.make_async_copy(
                                ref, held[p].at[:, left:right], sems.at[p]
                            ).start()
                            left = right

            for p in range(npiece):
                pltpu.make_async_copy(held[p], held[p], sems.at[p]).wait()

        acc = None
        for p in range(npiece):
            for q in range(per):
                term = mm(d_refs[p][q], held[p][q * width : (q + 1) * width, :])
                acc = term if acc is None else acc + term
        out_ref[...] = acc

    def d_map(p):
        return lambda i, sc: (sc[p], i, 0)

    return pl.pallas_call(
        kernel,
        grid_spec=pltpu.PrefetchScalarGridSpec(
            num_scalar_prefetch=1,
            grid=(rows // bm,),
            in_specs=[pl.BlockSpec(memory_space=pl.ANY)] * nh
            + [pl.BlockSpec((per, bm, width), d_map(p)) for p in range(npiece)],
            out_specs=pl.BlockSpec((bm, cols), lambda i, sc: (i, 0)),
            scratch_shapes=[pltpu.VMEM((depth, cols), BF16)] * npiece
            + [pltpu.SemaphoreType.DMA((npiece,))],
        ),
        out_shape=jax.ShapeDtypeStruct((rows, cols), F32),
        compiler_params=pltpu.CompilerParams(vmem_limit_bytes=56 * MIB),
        cost_estimate=pl.CostEstimate(
            flops=2 * npiece * rows * depth * cols,
            bytes_accessed=npiece * (rows + cols) * depth * 2 + rows * cols * 4,
            transcendentals=0,
        ),
        name="product",
    )(scalars, *[x for c, _, _ in pieces for arrays in c for x in arrays], *[dm_panel] * npiece)


def product_add(total, part, dm_panel, candidates, which, shard):
    ncol, rows, width = dm_panel.shape
    depth, wide = candidates[0].shape
    per = depth // width
    bm = min(512, rows)
    steps = rows // bm
    nh = len(candidates)
    scalars = jnp.stack([jnp.asarray(which, jnp.int32), jnp.asarray(shard, jnp.int32)])

    def kernel(sc_ref, *refs):
        h_refs = refs[:nh]
        dm_ref, total_ref, out_ref, held, d_ref, c_ref, h_sem, d_sems, c_sems, o_sems = refs[nh:]
        columns = pl.ds(part * wide, wide)

        def read_d(i, q):
            return pltpu.make_async_copy(
                dm_ref.at[sc_ref[1] * per + q, pl.ds(i * bm, bm)],
                d_ref.at[i, :, pl.ds(q * width, width)],
                d_sems.at[i, q],
            )

        def read_c(i):
            return pltpu.make_async_copy(
                total_ref.at[pl.ds(i * bm, bm), columns], c_ref.at[i], c_sems.at[i]
            )

        def write(i):
            return pltpu.make_async_copy(
                c_ref.at[i], out_ref.at[pl.ds(i * bm, bm), columns], o_sems.at[i]
            )

        for k in range(nh):

            @pl.when(sc_ref[0] == k)
            def _(k=k):
                pltpu.make_async_copy(h_refs[k], held, h_sem.at[0]).start()

        def start(i):
            for q in range(per):
                read_d(i, q).start()
            read_c(i).start()

        for i in range(min(2, steps)):
            start(i)
        pltpu.make_async_copy(h_refs[0], held, h_sem.at[0]).wait()
        for i in range(steps):
            for q in range(per):
                read_d(i, q).wait()
            read_c(i).wait()
            if i + 2 < steps:
                start(i + 2)
            c_ref[i] = c_ref[i] + mm(d_ref[i], held[...])
            write(i).start()
        for i in range(steps):
            write(i).wait()

    return pl.pallas_call(
        kernel,
        grid_spec=pltpu.PrefetchScalarGridSpec(
            num_scalar_prefetch=1,
            grid=(1,),
            in_specs=[pl.BlockSpec(memory_space=pl.ANY)] * (nh + 2),
            out_specs=pl.BlockSpec(memory_space=pl.ANY),
            scratch_shapes=[
                pltpu.VMEM((depth, wide), BF16),
                pltpu.VMEM((steps, bm, depth), BF16),
                pltpu.VMEM((steps, bm, wide), F32),
                pltpu.SemaphoreType.DMA((1,)),
                pltpu.SemaphoreType.DMA((steps, per)),
                pltpu.SemaphoreType.DMA((steps,)),
                pltpu.SemaphoreType.DMA((steps,)),
            ],
        ),
        out_shape=jax.ShapeDtypeStruct(total.shape, F32),
        input_output_aliases={2 + nh: 0},
        compiler_params=pltpu.CompilerParams(vmem_limit_bytes=56 * MIB),
        cost_estimate=pl.CostEstimate(
            flops=2 * rows * depth * wide,
            bytes_accessed=(rows + wide) * depth * 2 + rows * wide * 8,
            transcendentals=0,
        ),
        name="product_add",
    )(scalars, *candidates, dm_panel, total)


PARTS = 2
EARLY = (3, 2, 3)


def tie(x, y):
    return lax.optimization_barrier((x, y))


def body(density, h_core, phi, v_ext, tile_blocks, tile_count):
    nrow = lax.axis_size("row")
    ncol = lax.axis_size("col")
    ndev = nrow * ncol
    row_idx = lax.axis_index("row")
    col_idx = lax.axis_index("col")
    myself = row_idx * ncol + col_idx
    rows_loc, cols_loc = density.shape
    rowb = rows_loc // BLK
    colb = cols_loc // BLK
    tdev, npts, local = phi.shape
    maxb = tile_blocks.shape[1]
    line = nrow == 4

    inward = [(0, 1), (3, 2)]
    cross = [(1, 2), (2, 1)]
    outward = [(1, 0), (2, 3)]

    blocks = tile_blocks.reshape(ndev, tdev, maxb)
    counts = tile_count.reshape(ndev, tdev)
    live = jnp.arange(maxb, dtype=jnp.int32)[None, None, :] < counts[:, :, None]
    col_hit = live & (blocks // colb == col_idx)
    col_in = jnp.sum(jnp.where(col_hit, blocks - col_idx * colb, 0), axis=2)

    def picks_of(row):
        row_hit = live & (blocks // rowb == row)
        both = jnp.any(row_hit, axis=2) & jnp.any(col_hit, axis=2)
        row_in = jnp.sum(jnp.where(row_hit, blocks - row * rowb, 0), axis=2)
        row_pick = jnp.sum(jnp.where(both, row_in, 0), axis=1)
        col_pick = jnp.sum(jnp.where(both, col_in, 0), axis=1)
        return row_pick, col_pick, jnp.any(both, axis=1).astype(jnp.int32)

    picks = picks_of(row_idx)
    mine = lax.dynamic_index_in_dim(blocks, myself, 0, keepdims=False)
    my_counts = lax.dynamic_index_in_dim(counts, myself, 0, keepdims=False)
    hold = ((mine // rowb)[:, :, None] * ncol + (mine // colb)[:, None, :]).reshape(tdev, -1)

    if line:
        unit = rows_loc // sum(EARLY)
        sizes = [unit * k for k in EARLY]
        first = round_bands(h_core, 0, sizes[:1])
        density, first = tie(density, first)
        rest = round_bands(h_core, sizes[0], sizes[1:])
        early = [lax.ppermute(x, "row", outward) for x in first + rest]
    outgoing = (gather_blocks(density, picks[0], picks[1]) * DM_SCALE).astype(jnp.float16)
    incoming = lax.all_to_all(outgoing, ("row", "col"), split_axis=0, concat_axis=0, tiled=True)

    basis = split_basis(phi, my_counts)
    if line:
        incoming, (early[0], _) = tie(incoming, (early[0], rest))
    returning, dm_low = tile_ham(incoming.astype(F32), basis, v_ext, hold, my_counts, density)
    dm_panel = lax.all_gather(dm_low, "col", axis=0, tiled=False)
    arriving = lax.all_to_all(returning, ("row", "col"), split_axis=0, concat_axis=0, tiled=True)
    if line:
        arriving, early[1] = tie(arriving, early[1])
    low = assemble([h_core], arriving, picks, BF16, PARTS if line else 1)
    (hamiltonian,) = assemble([h_core], arriving, picks, F32, 1)

    if line:
        pair_idx = row_idx + 1 - 2 * (row_idx % 2)
        is_low = row_idx < 2
        is_end = ((row_idx == 0) | (row_idx == 3)).astype(jnp.int32)
        near_idx = jnp.where(is_low, 2, 1)
        far_idx = jnp.where(is_low, 3, 0)
        pair_blocks = lax.ppermute(arriving, "row", outward)
        near_mid = []
        for p in range(PARTS):
            ready = low[p]
            if p == 1:
                ready, (pair_blocks, early[2]) = tie(ready, (pair_blocks, early[2]))
            near_mid.append(lax.ppermute(ready, "row", cross))
        near_end = [lax.ppermute(x, "row", outward) for x in near_mid]
        pair_mid = []
        for p in range(PARTS):
            ready = low[p] if p == 0 else tie(low[p], near_mid[p - 1])[0]
            pair_mid.append(lax.ppermute(ready, "row", inward))
        far_mid = [lax.ppermute(pair_mid[0], "row", cross)]
        for p in range(1, PARTS):
            ready, near_end[p - 1] = tie(pair_mid[p], near_end[p - 1])
            far_mid.append(lax.ppermute(ready, "row", cross))
        far_end = [lax.ppermute(x, "row", outward) for x in far_mid[:-1]]
        ready, near_end[-1] = tie(far_mid[-1], near_end[-1])
        far_end.append(lax.ppermute(ready, "row", outward))
        pair_end = assemble(early, pair_blocks, picks_of(pair_idx), BF16, 1)
        total = product(
            cols_loc,
            dm_panel,
            [
                ((low,), 0, row_idx),
                ((pair_mid, pair_end), is_end, pair_idx),
                ((near_mid, near_end), is_end, near_idx),
            ],
        )
        for p in range(PARTS):
            total = product_add(
                total, p, dm_panel, (far_mid[p], far_end[p]), is_end, far_idx
            )
    else:
        ham_panel = lax.all_gather(low[0], "row", axis=0, tiled=False)
        total = product(cols_loc, dm_panel, [(((ham_panel[0],),), 0, 0)])
        for k in range(1, nrow):
            total = product_add(total, 0, dm_panel, (ham_panel[k],), 0, k)
    return hamiltonian, total


def solution(mesh):
    placed = (
        P("row", "col"),
        P("row", "col"),
        P(("row", "col"), None, None),
        P(("row", "col"), None),
        P(),
        P(),
    )
    return jax.shard_map(
        body,
        mesh=mesh,
        in_specs=placed,
        out_specs=(P("row", "col"), P("row", "col")),
        check_vma=False,
    )
```

```python
import jax
import jax.numpy as jnp
from jax import lax
from jax.experimental import pallas as pl
from jax.experimental.pallas import tpu as pltpu
from jax.sharding import PartitionSpec as P

BLK = 128

cube_coef = 0.5
cell_volume = 0.03125
DM_SCALE = float(2**20)

F32 = jnp.float32
BF16 = jnp.bfloat16
MIB = 1 << 20
AHEAD = 3


def gather_kernel(row_ref, col_ref, dens_ref, out_ref, sems):
    n = out_ref.shape[0]

    def copy(s):
        r = pl.multiple_of(row_ref[s] * BLK, BLK)
        c = pl.multiple_of(col_ref[s] * BLK, BLK)
        return pltpu.make_async_copy(
            dens_ref.at[pl.ds(r, BLK), pl.ds(c, BLK)], out_ref.at[s], sems.at[s]
        )

    def start(s, carry):
        copy(s).start()
        return carry

    def wait(s, carry):
        copy(s).wait()
        return carry

    lax.fori_loop(0, n, start, 0)
    lax.fori_loop(0, n, wait, 0)


def gather_blocks(density, row_pick, col_pick):
    n = row_pick.shape[0]
    return pl.pallas_call(
        gather_kernel,
        grid_spec=pltpu.PrefetchScalarGridSpec(
            num_scalar_prefetch=2,
            grid=(1,),
            in_specs=[pl.BlockSpec(memory_space=pl.ANY)],
            out_specs=pl.BlockSpec((n, BLK, BLK), lambda i, *_: (0, 0, 0)),
            scratch_shapes=[pltpu.SemaphoreType.DMA((n,))],
        ),
        out_shape=jax.ShapeDtypeStruct((n, BLK, BLK), F32),
        compiler_params=pltpu.CompilerParams(vmem_limit_bytes=56 * MIB),
        cost_estimate=pl.CostEstimate(
            flops=0, bytes_accessed=2 * n * BLK * BLK * 4, transcendentals=0
        ),
        name="gather_blocks",
    )(row_pick, col_pick, density)


def round_bands(x, top, sizes):
    cols = x.shape[1]
    bm = min(256, min(sizes))
    source = [(k, g) for k, size in enumerate(sizes) for g in range(size // bm)]
    steps = len(source)

    def kernel(x_ref, *rest):
        outs = rest[: len(sizes)]
        raw_ref, low_ref, in_sems, out_sems = rest[len(sizes) :]

        def read(g):
            return pltpu.make_async_copy(
                x_ref.at[pl.ds(top + g * bm, bm)], raw_ref.at[g], in_sems.at[g]
            )

        def write(g):
            k, at = source[g]
            return pltpu.make_async_copy(
                low_ref.at[g], outs[k].at[pl.ds(at * bm, bm)], out_sems.at[g]
            )

        for g in range(min(AHEAD, steps)):
            read(g).start()
        for g in range(steps):
            read(g).wait()
            if g + AHEAD < steps:
                read(g + AHEAD).start()
            low_ref[g] = raw_ref[g].astype(BF16)
            write(g).start()
        for g in range(steps):
            write(g).wait()

    return pl.pallas_call(
        kernel,
        grid=(1,),
        in_specs=[pl.BlockSpec(memory_space=pl.ANY)],
        out_specs=[pl.BlockSpec(memory_space=pl.ANY)] * len(sizes),
        scratch_shapes=[
            pltpu.VMEM((steps, bm, cols), F32),
            pltpu.VMEM((steps, bm, cols), BF16),
            pltpu.SemaphoreType.DMA((steps,)),
            pltpu.SemaphoreType.DMA((steps,)),
        ],
        out_shape=[jax.ShapeDtypeStruct((size, cols), BF16) for size in sizes],
        compiler_params=pltpu.CompilerParams(vmem_limit_bytes=56 * MIB),
        cost_estimate=pl.CostEstimate(
            flops=sum(sizes) * cols, bytes_accessed=sum(sizes) * cols * 6, transcendentals=0
        ),
        name="round_bands",
    )(x)


def split(x):
    hi = x.astype(BF16)
    return hi, (x - hi.astype(F32)).astype(BF16)


def basis_kernel(count_ref, phi_ref, hi_ref, lo_ref, hit_ref, lot_ref):
    basis = phi_ref[0]
    column = lax.broadcasted_iota(jnp.int32, basis.shape, 1)
    masked = jnp.where(column < count_ref[pl.program_id(0)] * BLK, basis, 0.0)
    hi, lo = split(masked)
    hi_ref[0] = hi
    lo_ref[0] = lo
    hit_ref[0] = hi.T
    lot_ref[0] = lo.T


def split_basis(phi, counts):
    tdev, npts, local = phi.shape
    spec = pl.BlockSpec((1, npts, local), lambda t, *_: (t, 0, 0))
    spec_t = pl.BlockSpec((1, local, npts), lambda t, *_: (t, 0, 0))
    return pl.pallas_call(
        basis_kernel,
        grid_spec=pltpu.PrefetchScalarGridSpec(
            num_scalar_prefetch=1,
            grid=(tdev,),
            in_specs=[spec],
            out_specs=[spec, spec, spec_t, spec_t],
        ),
        out_shape=[jax.ShapeDtypeStruct((tdev, npts, local), BF16)] * 2
        + [jax.ShapeDtypeStruct((tdev, local, npts), BF16)] * 2,
        compiler_params=pltpu.CompilerParams(vmem_limit_bytes=40 * MIB),
        cost_estimate=pl.CostEstimate(
            flops=4 * phi.size, bytes_accessed=12 * phi.size, transcendentals=0
        ),
        name="split_basis",
    )(counts, phi)


def mm(x, y):
    return jnp.dot(x, y, preferred_element_type=F32)


def tile_kernel(
    hold_ref,
    count_ref,
    in_ref,
    hi_ref,
    lo_ref,
    hit_ref,
    lot_ref,
    v_ref,
    out_ref,
    dh_ref,
    dl_ref,
):
    t = pl.program_id(0)
    maxb = hi_ref.shape[2] // BLK
    for i in range(maxb):
        for j in range(maxb):
            blk = in_ref[hold_ref[t, i * maxb + j]].astype(F32) * (1.0 / DM_SCALE)
            hi, lo = split(blk)
            dh_ref[i * BLK : (i + 1) * BLK, j * BLK : (j + 1) * BLK] = hi
            dl_ref[i * BLK : (i + 1) * BLK, j * BLK : (j + 1) * BLK] = lo
    count = count_ref[t]
    mh, ml = hi_ref[0], lo_ref[0]
    dh, dl = dh_ref[...], dl_ref[...]
    spread = mm(mh, dh) + (mm(ml, dh) + mm(mh, dl))
    masked = mh.astype(F32) + ml.astype(F32)
    rho = jnp.sum(spread * masked, axis=1, keepdims=True)
    potential = v_ref[0] + rho + cube_coef * rho * rho * rho
    wh, wl = split(masked * (potential * cell_volume))
    mht, mlt = hit_ref[0], lot_ref[0]
    ham = (mm(mht, wh) + (mm(mlt, wh) + mm(mht, wl))).astype(BF16)
    for i in range(maxb):
        for j in range(maxb):

            @pl.when((i < count) & (j < count))
            def _():
                out_ref[hold_ref[t, i * maxb + j]] = ham[
                    i * BLK : (i + 1) * BLK, j * BLK : (j + 1) * BLK
                ]


def tile_ham(incoming, basis, v_ext, hold, counts):
    n = incoming.shape[0]
    tdev, npts, local = basis[0].shape
    flops = tdev * 3 * 2 * 2 * npts * local * local
    spec = pl.BlockSpec((1, npts, local), lambda t, *_: (t, 0, 0))
    spec_t = pl.BlockSpec((1, local, npts), lambda t, *_: (t, 0, 0))
    return pl.pallas_call(
        tile_kernel,
        grid_spec=pltpu.PrefetchScalarGridSpec(
            num_scalar_prefetch=2,
            grid=(tdev,),
            in_specs=[
                pl.BlockSpec((n, BLK, BLK), lambda t, *_: (0, 0, 0)),
                spec,
                spec,
                spec_t,
                spec_t,
                pl.BlockSpec((1, npts, 1), lambda t, *_: (t, 0, 0)),
            ],
            out_specs=pl.BlockSpec((n, BLK, BLK), lambda t, *_: (0, 0, 0)),
            scratch_shapes=[
                pltpu.VMEM((local, local), BF16),
                pltpu.VMEM((local, local), BF16),
            ],
        ),
        out_shape=jax.ShapeDtypeStruct((n, BLK, BLK), BF16),
        compiler_params=pltpu.CompilerParams(vmem_limit_bytes=44 * MIB),
        cost_estimate=pl.CostEstimate(
            flops=flops, bytes_accessed=tdev * npts * local * 8, transcendentals=0
        ),
        name="tile_ham",
    )(hold, counts, incoming, *basis, v_ext[:, :, None])


def assemble(h_core, arriving, picks, dtype, parts):
    nband = len(h_core)
    rows, cols = sum(x.shape[0] for x in h_core), h_core[0].shape[1]
    n = arriving.shape[0]
    per = 2
    bm = per * BLK
    steps = rows // bm
    wide = cols // parts
    widen = h_core[0].dtype != F32
    narrow = dtype != F32
    source = [(k, g) for k, x in enumerate(h_core) for g in range(x.shape[0] // bm)]

    def kernel(row_ref, col_ref, present_ref, in_ref, *rest):
        h_refs, outs, rest = rest[:nband], rest[nband : nband + parts], rest[nband + parts :]
        work_ref, in_sems, out_sems, num_ref, list_ref = rest[:5]
        rest = rest[5:]
        raw_ref = work_ref
        if widen:
            raw_ref, rest = rest[0], rest[1:]
        low_refs = rest if narrow else (work_ref,)

        def band(g):
            return pl.ds(g * bm, bm)

        def read(g):
            k, at = source[g]
            return pltpu.make_async_copy(
                h_refs[k].at[band(at)], raw_ref.at[band(g)], in_sems.at[g]
            )

        def write(g, p):
            return pltpu.make_async_copy(
                low_refs[p].at[band(g)], outs[p].at[band(g)], out_sems.at[g, p]
            )

        for g in range(min(AHEAD, steps)):
            read(g).start()
        for g in range(steps):
            num_ref[g] = 0

        def note(s, carry):
            @pl.when(present_ref[s] > 0)
            def _():
                g = row_ref[s] // per
                k = num_ref[g]
                list_ref[g * n + k] = s
                num_ref[g] = k + 1

            return carry

        lax.fori_loop(0, n, note, 0)

        for g in range(steps):
            read(g).wait()
            if g + AHEAD < steps:
                read(g + AHEAD).start()
            if widen:
                work_ref[band(g), :] = raw_ref[band(g), :].astype(F32)

            def add(k, carry, g=g):
                s = list_ref[g * n + k]
                top = pl.ds(pl.multiple_of(row_ref[s] * BLK, BLK), BLK)
                left = pl.ds(pl.multiple_of(col_ref[s] * BLK, BLK), BLK)
                work_ref[top, left] = work_ref[top, left] + in_ref[s].astype(F32)
                return carry

            lax.fori_loop(0, num_ref[g], add, 0)
            for p in range(parts):
                if narrow:
                    low_refs[p][band(g), :] = work_ref[band(g), p * wide : (p + 1) * wide].astype(
                        dtype
                    )
                write(g, p).start()
        for g in range(steps):
            for p in range(parts):
                write(g, p).wait()

    scratch = [
        pltpu.VMEM((rows, cols), F32),
        pltpu.SemaphoreType.DMA((steps,)),
        pltpu.SemaphoreType.DMA((steps, parts)),
        pltpu.SMEM((steps,), jnp.int32),
        pltpu.SMEM((steps * n,), jnp.int32),
    ]
    if widen:
        scratch.append(pltpu.VMEM((rows, cols), h_core[0].dtype))
    if narrow:
        scratch.extend([pltpu.VMEM((rows, wide), dtype)] * parts)
    return pl.pallas_call(
        kernel,
        grid_spec=pltpu.PrefetchScalarGridSpec(
            num_scalar_prefetch=3,
            grid=(1,),
            in_specs=[
                pl.BlockSpec((n, BLK, BLK), lambda i, *_: (0, 0, 0)),
            ]
            + [pl.BlockSpec(memory_space=pl.ANY)] * nband,
            out_specs=[pl.BlockSpec(memory_space=pl.ANY)] * parts,
            scratch_shapes=scratch,
        ),
        out_shape=[jax.ShapeDtypeStruct((rows, wide), dtype)] * parts,
        compiler_params=pltpu.CompilerParams(vmem_limit_bytes=56 * MIB),
        cost_estimate=pl.CostEstimate(
            flops=rows * cols, bytes_accessed=rows * cols * 6, transcendentals=0
        ),
        name="assemble",
    )(*picks, arriving, *h_core)


def product(cols, dm_panel, pieces):
    ncol, rows, width = dm_panel.shape
    depth = pieces[0][0][0][0].shape[0]
    per = depth // width
    bm = min(512, rows)
    npiece = len(pieces)
    nh = sum(len(arrays) for c, _, _ in pieces for arrays in c)
    scalars = jnp.stack(
        [jnp.asarray(s, jnp.int32) for _, _, s in pieces]
        + [jnp.asarray(w, jnp.int32) for _, w, _ in pieces]
    )

    def kernel(sc_ref, *refs):
        h_refs = refs[:nh]
        d_refs = refs[nh : nh + npiece]
        out_ref = refs[nh + npiece]
        held = refs[nh + npiece + 1 : -1]
        sems = refs[-1]

        @pl.when(pl.program_id(0) == 0)
        def _():
            at = 0
            for p, (candidates, _, _) in enumerate(pieces):
                for q, arrays in enumerate(candidates):
                    mine = h_refs[at : at + len(arrays)]
                    at += len(arrays)

                    @pl.when(sc_ref[npiece + p] == q)
                    def _(p=p, mine=mine):
                        left = 0
                        for ref in mine:
                            right = left + ref.shape[1]
                            pltpu.make_async_copy(
                                ref, held[p].at[:, left:right], sems.at[p]
                            ).start()
                            left = right

            for p in range(npiece):
                pltpu.make_async_copy(held[p], held[p], sems.at[p]).wait()

        acc = None
        for p in range(npiece):
            for q in range(per):
                term = mm(d_refs[p][q], held[p][q * width : (q + 1) * width, :])
                acc = term if acc is None else acc + term
        out_ref[...] = acc

    def d_map(p):
        return lambda i, sc: (sc[p], i, 0)

    return pl.pallas_call(
        kernel,
        grid_spec=pltpu.PrefetchScalarGridSpec(
            num_scalar_prefetch=1,
            grid=(rows // bm,),
            in_specs=[pl.BlockSpec(memory_space=pl.ANY)] * nh
            + [pl.BlockSpec((per, bm, width), d_map(p)) for p in range(npiece)],
            out_specs=pl.BlockSpec((bm, cols), lambda i, sc: (i, 0)),
            scratch_shapes=[pltpu.VMEM((depth, cols), BF16)] * npiece
            + [pltpu.SemaphoreType.DMA((npiece,))],
        ),
        out_shape=jax.ShapeDtypeStruct((rows, cols), F32),
        compiler_params=pltpu.CompilerParams(vmem_limit_bytes=56 * MIB),
        cost_estimate=pl.CostEstimate(
            flops=2 * npiece * rows * depth * cols,
            bytes_accessed=npiece * (rows + cols) * depth * 2 + rows * cols * 4,
            transcendentals=0,
        ),
        name="product",
    )(scalars, *[x for c, _, _ in pieces for arrays in c for x in arrays], *[dm_panel] * npiece)


def product_add(total, part, dm_panel, candidates, which, shard):
    ncol, rows, width = dm_panel.shape
    depth, wide = candidates[0].shape
    per = depth // width
    bm = min(512, rows)
    steps = rows // bm
    nh = len(candidates)
    scalars = jnp.stack([jnp.asarray(which, jnp.int32), jnp.asarray(shard, jnp.int32)])

    def kernel(sc_ref, *refs):
        h_refs = refs[:nh]
        dm_ref, total_ref, out_ref, held, d_ref, c_ref, h_sem, d_sems, c_sems, o_sems = refs[nh:]
        columns = pl.ds(part * wide, wide)

        def read_d(i, q):
            return pltpu.make_async_copy(
                dm_ref.at[sc_ref[1] * per + q, pl.ds(i * bm, bm)],
                d_ref.at[i, :, pl.ds(q * width, width)],
                d_sems.at[i, q],
            )

        def read_c(i):
            return pltpu.make_async_copy(
                total_ref.at[pl.ds(i * bm, bm), columns], c_ref.at[i], c_sems.at[i]
            )

        def write(i):
            return pltpu.make_async_copy(
                c_ref.at[i], out_ref.at[pl.ds(i * bm, bm), columns], o_sems.at[i]
            )

        for k in range(nh):

            @pl.when(sc_ref[0] == k)
            def _(k=k):
                pltpu.make_async_copy(h_refs[k], held, h_sem.at[0]).start()

        def start(i):
            for q in range(per):
                read_d(i, q).start()
            read_c(i).start()

        for i in range(min(2, steps)):
            start(i)
        pltpu.make_async_copy(h_refs[0], held, h_sem.at[0]).wait()
        for i in range(steps):
            for q in range(per):
                read_d(i, q).wait()
            read_c(i).wait()
            if i + 2 < steps:
                start(i + 2)
            c_ref[i] = c_ref[i] + mm(d_ref[i], held[...])
            write(i).start()
        for i in range(steps):
            write(i).wait()

    return pl.pallas_call(
        kernel,
        grid_spec=pltpu.PrefetchScalarGridSpec(
            num_scalar_prefetch=1,
            grid=(1,),
            in_specs=[pl.BlockSpec(memory_space=pl.ANY)] * (nh + 2),
            out_specs=pl.BlockSpec(memory_space=pl.ANY),
            scratch_shapes=[
                pltpu.VMEM((depth, wide), BF16),
                pltpu.VMEM((steps, bm, depth), BF16),
                pltpu.VMEM((steps, bm, wide), F32),
                pltpu.SemaphoreType.DMA((1,)),
                pltpu.SemaphoreType.DMA((steps, per)),
                pltpu.SemaphoreType.DMA((steps,)),
                pltpu.SemaphoreType.DMA((steps,)),
            ],
        ),
        out_shape=jax.ShapeDtypeStruct(total.shape, F32),
        input_output_aliases={2 + nh: 0},
        compiler_params=pltpu.CompilerParams(vmem_limit_bytes=56 * MIB),
        cost_estimate=pl.CostEstimate(
            flops=2 * rows * depth * wide,
            bytes_accessed=(rows + wide) * depth * 2 + rows * wide * 8,
            transcendentals=0,
        ),
        name="product_add",
    )(scalars, *candidates, dm_panel, total)


PARTS = 2


def tie(x, y):
    return lax.optimization_barrier((x, y))


def body(density, h_core, phi, v_ext, tile_blocks, tile_count):
    nrow = lax.axis_size("row")
    ncol = lax.axis_size("col")
    ndev = nrow * ncol
    row_idx = lax.axis_index("row")
    col_idx = lax.axis_index("col")
    myself = row_idx * ncol + col_idx
    rows_loc, cols_loc = density.shape
    rowb = rows_loc // BLK
    colb = cols_loc // BLK
    tdev, npts, local = phi.shape
    maxb = tile_blocks.shape[1]
    line = nrow == 4

    swap = [(0, 1), (1, 0), (2, 3), (3, 2)]
    cross = [(1, 2), (2, 1)]
    outward = [(1, 0), (2, 3)]

    blocks = tile_blocks.reshape(ndev, tdev, maxb)
    counts = tile_count.reshape(ndev, tdev)
    live = jnp.arange(maxb, dtype=jnp.int32)[None, None, :] < counts[:, :, None]
    col_hit = live & (blocks // colb == col_idx)
    col_in = jnp.sum(jnp.where(col_hit, blocks - col_idx * colb, 0), axis=2)

    def picks_of(row):
        row_hit = live & (blocks // rowb == row)
        both = jnp.any(row_hit, axis=2) & jnp.any(col_hit, axis=2)
        row_in = jnp.sum(jnp.where(row_hit, blocks - row * rowb, 0), axis=2)
        row_pick = jnp.sum(jnp.where(both, row_in, 0), axis=1)
        col_pick = jnp.sum(jnp.where(both, col_in, 0), axis=1)
        return row_pick, col_pick, jnp.any(both, axis=1).astype(jnp.int32)

    picks = picks_of(row_idx)
    mine = lax.dynamic_index_in_dim(blocks, myself, 0, keepdims=False)
    my_counts = lax.dynamic_index_in_dim(counts, myself, 0, keepdims=False)
    hold = ((mine // rowb)[:, :, None] * ncol + (mine // colb)[:, None, :]).reshape(tdev, -1)

    outgoing = (gather_blocks(density, picks[0], picks[1]) * DM_SCALE).astype(jnp.float16)
    incoming = lax.all_to_all(outgoing, ("row", "col"), split_axis=0, concat_axis=0, tiled=True)
    basis = split_basis(phi, my_counts)
    (dm_low,) = round_bands(density, 0, [rows_loc])
    incoming, dm_low = tie(incoming, dm_low)
    dm_panel = lax.all_gather(dm_low, "col", axis=0, tiled=False)

    returning = tile_ham(incoming.astype(F32), basis, v_ext, hold, my_counts)
    arriving = lax.all_to_all(returning, ("row", "col"), split_axis=0, concat_axis=0, tiled=True)
    low = assemble([h_core], arriving, picks, BF16, PARTS if line else 1)
    (hamiltonian,) = assemble([h_core], arriving, picks, F32, 1)

    if line:
        pair_idx = row_idx + 1 - 2 * (row_idx % 2)
        is_low = row_idx < 2
        is_end = ((row_idx == 0) | (row_idx == 3)).astype(jnp.int32)
        near_idx = jnp.where(is_low, 2, 1)
        far_idx = jnp.where(is_low, 3, 0)
        pair = [lax.ppermute(x, "row", swap) for x in low]
        near_mid = [lax.ppermute(x, "row", cross) for x in low]
        near_end = [lax.ppermute(x, "row", outward) for x in near_mid]
        far_mid = [lax.ppermute(pair[0], "row", cross)]
        for p in range(1, PARTS):
            ready, near_end[p - 1] = tie(pair[p], near_end[p - 1])
            far_mid.append(lax.ppermute(ready, "row", cross))
        far_end = [lax.ppermute(x, "row", outward) for x in far_mid[:-1]]
        ready, near_end[-1] = tie(far_mid[-1], near_end[-1])
        far_end.append(lax.ppermute(ready, "row", outward))
        total = product(
            cols_loc,
            dm_panel,
            [
                ((low,), 0, row_idx),
                ((pair,), 0, pair_idx),
                ((near_mid, near_end), is_end, near_idx),
            ],
        )
        for p in range(PARTS):
            total = product_add(
                total, p, dm_panel, (far_mid[p], far_end[p]), is_end, far_idx
            )
    else:
        ham_panel = lax.all_gather(low[0], "row", axis=0, tiled=False)
        total = product(cols_loc, dm_panel, [(((ham_panel[0],),), 0, 0)])
        for k in range(1, nrow):
            total = product_add(total, 0, dm_panel, (ham_panel[k],), 0, k)
    return hamiltonian, total


def solution(mesh):
    placed = (
        P("row", "col"),
        P("row", "col"),
        P(("row", "col"), None, None),
        P(("row", "col"), None),
        P(),
        P(),
    )
    return jax.shard_map(
        body,
        mesh=mesh,
        in_specs=placed,
        out_specs=(P("row", "col"), P("row", "col")),
        check_vma=False,
    )
```

```python
import jax
import jax.numpy as jnp
from jax import lax
from jax.experimental import pallas as pl
from jax.experimental.pallas import tpu as pltpu
from jax.sharding import PartitionSpec as P

BLK = 128

cube_coef = 0.5
cell_volume = 0.03125
DM_SCALE = float(2**20)

F32 = jnp.float32
BF16 = jnp.bfloat16
MIB = 1 << 20
AHEAD = 3


def gather_kernel(row_ref, col_ref, dens_ref, out_ref, sems):
    n = out_ref.shape[0]

    def copy(s):
        r = pl.multiple_of(row_ref[s] * BLK, BLK)
        c = pl.multiple_of(col_ref[s] * BLK, BLK)
        return pltpu.make_async_copy(
            dens_ref.at[pl.ds(r, BLK), pl.ds(c, BLK)], out_ref.at[s], sems.at[s]
        )

    def start(s, carry):
        copy(s).start()
        return carry

    def wait(s, carry):
        copy(s).wait()
        return carry

    lax.fori_loop(0, n, start, 0)
    lax.fori_loop(0, n, wait, 0)


def gather_blocks(density, row_pick, col_pick):
    n = row_pick.shape[0]
    return pl.pallas_call(
        gather_kernel,
        grid_spec=pltpu.PrefetchScalarGridSpec(
            num_scalar_prefetch=2,
            grid=(1,),
            in_specs=[pl.BlockSpec(memory_space=pl.ANY)],
            out_specs=pl.BlockSpec((n, BLK, BLK), lambda i, *_: (0, 0, 0)),
            scratch_shapes=[pltpu.SemaphoreType.DMA((n,))],
        ),
        out_shape=jax.ShapeDtypeStruct((n, BLK, BLK), F32),
        compiler_params=pltpu.CompilerParams(vmem_limit_bytes=56 * MIB),
        cost_estimate=pl.CostEstimate(
            flops=0, bytes_accessed=2 * n * BLK * BLK * 4, transcendentals=0
        ),
        name="gather_blocks",
    )(row_pick, col_pick, density)


def round_bands(x, top, sizes):
    cols = x.shape[1]
    bm = min(256, min(sizes))
    source = [(k, g) for k, size in enumerate(sizes) for g in range(size // bm)]
    steps = len(source)

    def kernel(x_ref, *rest):
        outs = rest[: len(sizes)]
        raw_ref, low_ref, in_sems, out_sems = rest[len(sizes) :]

        def read(g):
            return pltpu.make_async_copy(
                x_ref.at[pl.ds(top + g * bm, bm)], raw_ref.at[g], in_sems.at[g]
            )

        def write(g):
            k, at = source[g]
            return pltpu.make_async_copy(
                low_ref.at[g], outs[k].at[pl.ds(at * bm, bm)], out_sems.at[g]
            )

        for g in range(min(AHEAD, steps)):
            read(g).start()
        for g in range(steps):
            read(g).wait()
            if g + AHEAD < steps:
                read(g + AHEAD).start()
            low_ref[g] = raw_ref[g].astype(BF16)
            write(g).start()
        for g in range(steps):
            write(g).wait()

    return pl.pallas_call(
        kernel,
        grid=(1,),
        in_specs=[pl.BlockSpec(memory_space=pl.ANY)],
        out_specs=[pl.BlockSpec(memory_space=pl.ANY)] * len(sizes),
        scratch_shapes=[
            pltpu.VMEM((steps, bm, cols), F32),
            pltpu.VMEM((steps, bm, cols), BF16),
            pltpu.SemaphoreType.DMA((steps,)),
            pltpu.SemaphoreType.DMA((steps,)),
        ],
        out_shape=[jax.ShapeDtypeStruct((size, cols), BF16) for size in sizes],
        compiler_params=pltpu.CompilerParams(vmem_limit_bytes=56 * MIB),
        cost_estimate=pl.CostEstimate(
            flops=sum(sizes) * cols, bytes_accessed=sum(sizes) * cols * 6, transcendentals=0
        ),
        name="round_bands",
    )(x)


def split(x):
    hi = x.astype(BF16)
    return hi, (x - hi.astype(F32)).astype(BF16)


def basis_kernel(count_ref, phi_ref, hi_ref, lo_ref, hit_ref, lot_ref):
    basis = phi_ref[0]
    column = lax.broadcasted_iota(jnp.int32, basis.shape, 1)
    masked = jnp.where(column < count_ref[pl.program_id(0)] * BLK, basis, 0.0)
    hi, lo = split(masked)
    hi_ref[0] = hi
    lo_ref[0] = lo
    hit_ref[0] = hi.T
    lot_ref[0] = lo.T


def split_basis(phi, counts):
    tdev, npts, local = phi.shape
    spec = pl.BlockSpec((1, npts, local), lambda t, *_: (t, 0, 0))
    spec_t = pl.BlockSpec((1, local, npts), lambda t, *_: (t, 0, 0))
    return pl.pallas_call(
        basis_kernel,
        grid_spec=pltpu.PrefetchScalarGridSpec(
            num_scalar_prefetch=1,
            grid=(tdev,),
            in_specs=[spec],
            out_specs=[spec, spec, spec_t, spec_t],
        ),
        out_shape=[jax.ShapeDtypeStruct((tdev, npts, local), BF16)] * 2
        + [jax.ShapeDtypeStruct((tdev, local, npts), BF16)] * 2,
        compiler_params=pltpu.CompilerParams(vmem_limit_bytes=40 * MIB),
        cost_estimate=pl.CostEstimate(
            flops=4 * phi.size, bytes_accessed=12 * phi.size, transcendentals=0
        ),
        name="split_basis",
    )(counts, phi)


def mm(x, y):
    return jnp.dot(x, y, preferred_element_type=F32)


def tile_kernel(
    hold_ref,
    count_ref,
    in_ref,
    hi_ref,
    lo_ref,
    hit_ref,
    lot_ref,
    v_ref,
    out_ref,
    dh_ref,
    dl_ref,
):
    t = pl.program_id(0)
    maxb = hi_ref.shape[2] // BLK
    for i in range(maxb):
        for j in range(maxb):
            blk = in_ref[hold_ref[t, i * maxb + j]].astype(F32) * (1.0 / DM_SCALE)
            hi, lo = split(blk)
            dh_ref[i * BLK : (i + 1) * BLK, j * BLK : (j + 1) * BLK] = hi
            dl_ref[i * BLK : (i + 1) * BLK, j * BLK : (j + 1) * BLK] = lo
    count = count_ref[t]
    mh, ml = hi_ref[0], lo_ref[0]
    dh, dl = dh_ref[...], dl_ref[...]
    spread = mm(mh, dh) + (mm(ml, dh) + mm(mh, dl))
    masked = mh.astype(F32) + ml.astype(F32)
    rho = jnp.sum(spread * masked, axis=1, keepdims=True)
    potential = v_ref[0] + rho + cube_coef * rho * rho * rho
    wh, wl = split(masked * (potential * cell_volume))
    mht, mlt = hit_ref[0], lot_ref[0]
    ham = (mm(mht, wh) + (mm(mlt, wh) + mm(mht, wl))).astype(BF16)
    for i in range(maxb):
        for j in range(maxb):

            @pl.when((i < count) & (j < count))
            def _():
                out_ref[hold_ref[t, i * maxb + j]] = ham[
                    i * BLK : (i + 1) * BLK, j * BLK : (j + 1) * BLK
                ]


def tile_ham(incoming, basis, v_ext, hold, counts):
    n = incoming.shape[0]
    tdev, npts, local = basis[0].shape
    flops = tdev * 3 * 2 * 2 * npts * local * local
    spec = pl.BlockSpec((1, npts, local), lambda t, *_: (t, 0, 0))
    spec_t = pl.BlockSpec((1, local, npts), lambda t, *_: (t, 0, 0))
    return pl.pallas_call(
        tile_kernel,
        grid_spec=pltpu.PrefetchScalarGridSpec(
            num_scalar_prefetch=2,
            grid=(tdev,),
            in_specs=[
                pl.BlockSpec((n, BLK, BLK), lambda t, *_: (0, 0, 0)),
                spec,
                spec,
                spec_t,
                spec_t,
                pl.BlockSpec((1, npts, 1), lambda t, *_: (t, 0, 0)),
            ],
            out_specs=pl.BlockSpec((n, BLK, BLK), lambda t, *_: (0, 0, 0)),
            scratch_shapes=[
                pltpu.VMEM((local, local), BF16),
                pltpu.VMEM((local, local), BF16),
            ],
        ),
        out_shape=jax.ShapeDtypeStruct((n, BLK, BLK), BF16),
        compiler_params=pltpu.CompilerParams(vmem_limit_bytes=44 * MIB),
        cost_estimate=pl.CostEstimate(
            flops=flops, bytes_accessed=tdev * npts * local * 8, transcendentals=0
        ),
        name="tile_ham",
    )(hold, counts, incoming, *basis, v_ext[:, :, None])


def assemble(h_core, arriving, picks, dtype, first, parts, wide):
    rows, cols = h_core.shape[0], parts * wide
    n = arriving.shape[0]
    per = 2
    bm = per * BLK
    steps = rows // bm
    narrow = dtype != F32

    def kernel(row_ref, col_ref, present_ref, in_ref, h_ref, *rest):
        outs, rest = rest[:parts], rest[parts:]
        work_ref, in_sems, out_sems, num_ref, list_ref = rest[:5]
        low_refs = rest[5:] if narrow else (work_ref,)

        def band(g):
            return pl.ds(g * bm, bm)

        def read(g):
            return pltpu.make_async_copy(
                h_ref.at[band(g), pl.ds(first, cols)], work_ref.at[band(g)], in_sems.at[g]
            )

        def write(g, p):
            return pltpu.make_async_copy(
                low_refs[p].at[band(g)], outs[p].at[band(g)], out_sems.at[g, p]
            )

        for g in range(min(AHEAD, steps)):
            read(g).start()
        for g in range(steps):
            num_ref[g] = 0

        def note(s, carry):
            c = col_ref[s] * BLK

            @pl.when((present_ref[s] > 0) & (c >= first) & (c < first + cols))
            def _():
                g = row_ref[s] // per
                k = num_ref[g]
                list_ref[g * n + k] = s
                num_ref[g] = k + 1

            return carry

        lax.fori_loop(0, n, note, 0)

        for g in range(steps):
            read(g).wait()
            if g + AHEAD < steps:
                read(g + AHEAD).start()

            def add(k, carry, g=g):
                s = list_ref[g * n + k]
                top = pl.ds(pl.multiple_of(row_ref[s] * BLK, BLK), BLK)
                left = pl.ds(pl.multiple_of(col_ref[s] * BLK - first, BLK), BLK)
                work_ref[top, left] = work_ref[top, left] + in_ref[s].astype(F32)
                return carry

            lax.fori_loop(0, num_ref[g], add, 0)
            for p in range(parts):
                if narrow:
                    low_refs[p][band(g), :] = work_ref[band(g), p * wide : (p + 1) * wide].astype(
                        dtype
                    )
                write(g, p).start()
        for g in range(steps):
            for p in range(parts):
                write(g, p).wait()

    scratch = [
        pltpu.VMEM((rows, cols), F32),
        pltpu.SemaphoreType.DMA((steps,)),
        pltpu.SemaphoreType.DMA((steps, parts)),
        pltpu.SMEM((steps,), jnp.int32),
        pltpu.SMEM((steps * n,), jnp.int32),
    ]
    if narrow:
        scratch.extend([pltpu.VMEM((rows, wide), dtype)] * parts)
    return pl.pallas_call(
        kernel,
        grid_spec=pltpu.PrefetchScalarGridSpec(
            num_scalar_prefetch=3,
            grid=(1,),
            in_specs=[
                pl.BlockSpec((n, BLK, BLK), lambda i, *_: (0, 0, 0)),
                pl.BlockSpec(memory_space=pl.ANY),
            ],
            out_specs=[pl.BlockSpec(memory_space=pl.ANY)] * parts,
            scratch_shapes=scratch,
        ),
        out_shape=[jax.ShapeDtypeStruct((rows, wide), dtype)] * parts,
        compiler_params=pltpu.CompilerParams(vmem_limit_bytes=56 * MIB),
        cost_estimate=pl.CostEstimate(
            flops=rows * cols, bytes_accessed=rows * cols * 6, transcendentals=0
        ),
        name="assemble",
    )(*picks, arriving, h_core)


def product(cols, dm_panel, pieces):
    ncol, rows, width = dm_panel.shape
    depth = pieces[0][0][0][0].shape[0]
    per = depth // width
    bm = min(512, rows)
    npiece = len(pieces)
    nh = sum(len(arrays) for c, _, _ in pieces for arrays in c)
    scalars = jnp.stack(
        [jnp.asarray(s, jnp.int32) for _, _, s in pieces]
        + [jnp.asarray(w, jnp.int32) for _, w, _ in pieces]
    )

    def kernel(sc_ref, *refs):
        h_refs = refs[:nh]
        d_refs = refs[nh : nh + npiece]
        out_ref = refs[nh + npiece]
        held = refs[nh + npiece + 1 : -1]
        sems = refs[-1]

        @pl.when(pl.program_id(0) == 0)
        def _():
            at = 0
            for p, (candidates, _, _) in enumerate(pieces):
                for q, arrays in enumerate(candidates):
                    mine = h_refs[at : at + len(arrays)]
                    at += len(arrays)

                    @pl.when(sc_ref[npiece + p] == q)
                    def _(p=p, mine=mine):
                        left = 0
                        for ref in mine:
                            right = left + ref.shape[1]
                            pltpu.make_async_copy(
                                ref, held[p].at[:, left:right], sems.at[p]
                            ).start()
                            left = right

            for p in range(npiece):
                pltpu.make_async_copy(held[p], held[p], sems.at[p]).wait()

        acc = None
        for p in range(npiece):
            for q in range(per):
                term = mm(d_refs[p][q], held[p][q * width : (q + 1) * width, :])
                acc = term if acc is None else acc + term
        out_ref[...] = acc

    def d_map(p):
        return lambda i, sc: (sc[p], i, 0)

    return pl.pallas_call(
        kernel,
        grid_spec=pltpu.PrefetchScalarGridSpec(
            num_scalar_prefetch=1,
            grid=(rows // bm,),
            in_specs=[pl.BlockSpec(memory_space=pl.ANY)] * nh
            + [pl.BlockSpec((per, bm, width), d_map(p)) for p in range(npiece)],
            out_specs=pl.BlockSpec((bm, cols), lambda i, sc: (i, 0)),
            scratch_shapes=[pltpu.VMEM((depth, cols), BF16)] * npiece
            + [pltpu.SemaphoreType.DMA((npiece,))],
        ),
        out_shape=jax.ShapeDtypeStruct((rows, cols), F32),
        compiler_params=pltpu.CompilerParams(vmem_limit_bytes=56 * MIB),
        cost_estimate=pl.CostEstimate(
            flops=2 * npiece * rows * depth * cols,
            bytes_accessed=npiece * (rows + cols) * depth * 2 + rows * cols * 4,
            transcendentals=0,
        ),
        name="product",
    )(scalars, *[x for c, _, _ in pieces for arrays in c for x in arrays], *[dm_panel] * npiece)


def product_add(total, part, dm_panel, candidates, which, shard):
    ncol, rows, width = dm_panel.shape
    depth, wide = candidates[0].shape
    per = depth // width
    bm = min(512, rows)
    steps = rows // bm
    nh = len(candidates)
    scalars = jnp.stack([jnp.asarray(which, jnp.int32), jnp.asarray(shard, jnp.int32)])

    def kernel(sc_ref, *refs):
        h_refs = refs[:nh]
        dm_ref, total_ref, out_ref, held, d_ref, c_ref, h_sem, d_sems, c_sems, o_sems = refs[nh:]
        columns = pl.ds(part * wide, wide)

        def read_d(i, q):
            return pltpu.make_async_copy(
                dm_ref.at[sc_ref[1] * per + q, pl.ds(i * bm, bm)],
                d_ref.at[i, :, pl.ds(q * width, width)],
                d_sems.at[i, q],
            )

        def read_c(i):
            return pltpu.make_async_copy(
                total_ref.at[pl.ds(i * bm, bm), columns], c_ref.at[i], c_sems.at[i]
            )

        def write(i):
            return pltpu.make_async_copy(
                c_ref.at[i], out_ref.at[pl.ds(i * bm, bm), columns], o_sems.at[i]
            )

        for k in range(nh):

            @pl.when(sc_ref[0] == k)
            def _(k=k):
                pltpu.make_async_copy(h_refs[k], held, h_sem.at[0]).start()

        def start(i):
            for q in range(per):
                read_d(i, q).start()
            read_c(i).start()

        for i in range(min(2, steps)):
            start(i)
        pltpu.make_async_copy(h_refs[0], held, h_sem.at[0]).wait()
        for i in range(steps):
            for q in range(per):
                read_d(i, q).wait()
            read_c(i).wait()
            if i + 2 < steps:
                start(i + 2)
            c_ref[i] = c_ref[i] + mm(d_ref[i], held[...])
            write(i).start()
        for i in range(steps):
            write(i).wait()

    return pl.pallas_call(
        kernel,
        grid_spec=pltpu.PrefetchScalarGridSpec(
            num_scalar_prefetch=1,
            grid=(1,),
            in_specs=[pl.BlockSpec(memory_space=pl.ANY)] * (nh + 2),
            out_specs=pl.BlockSpec(memory_space=pl.ANY),
            scratch_shapes=[
                pltpu.VMEM((depth, wide), BF16),
                pltpu.VMEM((steps, bm, depth), BF16),
                pltpu.VMEM((steps, bm, wide), F32),
                pltpu.SemaphoreType.DMA((1,)),
                pltpu.SemaphoreType.DMA((steps, per)),
                pltpu.SemaphoreType.DMA((steps,)),
                pltpu.SemaphoreType.DMA((steps,)),
            ],
        ),
        out_shape=jax.ShapeDtypeStruct(total.shape, F32),
        input_output_aliases={2 + nh: 0},
        compiler_params=pltpu.CompilerParams(vmem_limit_bytes=56 * MIB),
        cost_estimate=pl.CostEstimate(
            flops=2 * rows * depth * wide,
            bytes_accessed=(rows + wide) * depth * 2 + rows * wide * 8,
            transcendentals=0,
        ),
        name="product_add",
    )(scalars, *candidates, dm_panel, total)


PARTS = 4


def tie(x, y):
    return lax.optimization_barrier((x, y))


def body(density, h_core, phi, v_ext, tile_blocks, tile_count):
    nrow = lax.axis_size("row")
    ncol = lax.axis_size("col")
    ndev = nrow * ncol
    row_idx = lax.axis_index("row")
    col_idx = lax.axis_index("col")
    myself = row_idx * ncol + col_idx
    rows_loc, cols_loc = density.shape
    rowb = rows_loc // BLK
    colb = cols_loc // BLK
    tdev, npts, local = phi.shape
    maxb = tile_blocks.shape[1]
    line = nrow == 4

    swap = [(0, 1), (1, 0), (2, 3), (3, 2)]
    cross = [(1, 2), (2, 1)]
    outward = [(1, 0), (2, 3)]

    blocks = tile_blocks.reshape(ndev, tdev, maxb)
    counts = tile_count.reshape(ndev, tdev)
    live = jnp.arange(maxb, dtype=jnp.int32)[None, None, :] < counts[:, :, None]
    col_hit = live & (blocks // colb == col_idx)
    col_in = jnp.sum(jnp.where(col_hit, blocks - col_idx * colb, 0), axis=2)

    def picks_of(row):
        row_hit = live & (blocks // rowb == row)
        both = jnp.any(row_hit, axis=2) & jnp.any(col_hit, axis=2)
        row_in = jnp.sum(jnp.where(row_hit, blocks - row * rowb, 0), axis=2)
        row_pick = jnp.sum(jnp.where(both, row_in, 0), axis=1)
        col_pick = jnp.sum(jnp.where(both, col_in, 0), axis=1)
        return row_pick, col_pick, jnp.any(both, axis=1).astype(jnp.int32)

    picks = picks_of(row_idx)
    mine = lax.dynamic_index_in_dim(blocks, myself, 0, keepdims=False)
    my_counts = lax.dynamic_index_in_dim(counts, myself, 0, keepdims=False)
    hold = ((mine // rowb)[:, :, None] * ncol + (mine // colb)[:, None, :]).reshape(tdev, -1)

    outgoing = (gather_blocks(density, picks[0], picks[1]) * DM_SCALE).astype(jnp.float16)
    incoming = lax.all_to_all(outgoing, ("row", "col"), split_axis=0, concat_axis=0, tiled=True)
    basis = split_basis(phi, my_counts)
    (dm_low,) = round_bands(density, 0, [rows_loc])
    incoming, (dm_low, basis) = tie(incoming, (dm_low, basis))
    dm_panel = lax.all_gather(dm_low, "col", axis=0, tiled=False)

    returning = tile_ham(incoming.astype(F32), basis, v_ext, hold, my_counts)
    arriving = lax.all_to_all(returning, ("row", "col"), split_axis=0, concat_axis=0, tiled=True)
    parts = PARTS if line and cols_loc % (PARTS * BLK) == 0 else 1
    wide = cols_loc // parts
    low = assemble(h_core, arriving, picks, BF16, 0, 1, wide)
    if parts > 1:
        low = low + assemble(h_core, arriving, picks, BF16, wide, parts - 1, wide)
    (hamiltonian,) = assemble(h_core, arriving, picks, F32, 0, 1, cols_loc)

    if line:
        pair_idx = row_idx + 1 - 2 * (row_idx % 2)
        is_low = row_idx < 2
        is_end = ((row_idx == 0) | (row_idx == 3)).astype(jnp.int32)
        near_idx = jnp.where(is_low, 2, 1)
        far_idx = jnp.where(is_low, 3, 0)
        pair, near_mid = [], []
        for p in range(parts):
            ready = low[p] if p < 2 else tie(low[p], near_mid[p - 2])[0]
            pair.append(lax.ppermute(ready, "row", swap))
            near_mid.append(lax.ppermute(ready, "row", cross))
        near_end = [lax.ppermute(x, "row", outward) for x in near_mid]
        far_mid = []
        for p in range(parts):
            ready = pair[p]
            if p > 0:
                ready, near_end[p - 1] = tie(ready, near_end[p - 1])
            far_mid.append(lax.ppermute(ready, "row", cross))
        far_end = []
        for p in range(parts):
            ready = far_mid[p]
            if p == parts - 1:
                ready, near_end[p] = tie(ready, near_end[p])
            far_end.append(lax.ppermute(ready, "row", outward))
        total = product(
            cols_loc,
            dm_panel,
            [
                ((low,), 0, row_idx),
                ((pair,), 0, pair_idx),
                ((near_mid, near_end), is_end, near_idx),
            ],
        )
        for p in range(parts):
            total = product_add(
                total, p, dm_panel, (far_mid[p], far_end[p]), is_end, far_idx
            )
    else:
        ham_panel = lax.all_gather(low[0], "row", axis=0, tiled=False)
        total = product(cols_loc, dm_panel, [(((ham_panel[0],),), 0, 0)])
        for k in range(1, nrow):
            total = product_add(total, 0, dm_panel, (ham_panel[k],), 0, k)
    return hamiltonian, total


def solution(mesh):
    placed = (
        P("row", "col"),
        P("row", "col"),
        P(("row", "col"), None, None),
        P(("row", "col"), None),
        P(),
        P(),
    )
    return jax.shard_map(
        body,
        mesh=mesh,
        in_specs=placed,
        out_specs=(P("row", "col"), P("row", "col")),
        check_vma=False,
    )
```

```python
import jax
import jax.numpy as jnp
from jax import lax
from jax.experimental import pallas as pl
from jax.experimental.pallas import tpu as pltpu
from jax.sharding import PartitionSpec as P

BLK = 128

cube_coef = 0.5
cell_volume = 0.03125
DM_SCALE = float(2**20)

F32 = jnp.float32
BF16 = jnp.bfloat16
MIB = 1 << 20
AHEAD = 3


def gather_kernel(row_ref, col_ref, dens_ref, out_ref, sems):
    n = out_ref.shape[0]

    def copy(s):
        r = pl.multiple_of(row_ref[s] * BLK, BLK)
        c = pl.multiple_of(col_ref[s] * BLK, BLK)
        return pltpu.make_async_copy(
            dens_ref.at[pl.ds(r, BLK), pl.ds(c, BLK)], out_ref.at[s], sems.at[s]
        )

    def start(s, carry):
        copy(s).start()
        return carry

    def wait(s, carry):
        copy(s).wait()
        return carry

    lax.fori_loop(0, n, start, 0)
    lax.fori_loop(0, n, wait, 0)


def gather_blocks(density, row_pick, col_pick):
    n = row_pick.shape[0]
    return pl.pallas_call(
        gather_kernel,
        grid_spec=pltpu.PrefetchScalarGridSpec(
            num_scalar_prefetch=2,
            grid=(1,),
            in_specs=[pl.BlockSpec(memory_space=pl.ANY)],
            out_specs=pl.BlockSpec((n, BLK, BLK), lambda i, *_: (0, 0, 0)),
            scratch_shapes=[pltpu.SemaphoreType.DMA((n,))],
        ),
        out_shape=jax.ShapeDtypeStruct((n, BLK, BLK), F32),
        compiler_params=pltpu.CompilerParams(vmem_limit_bytes=56 * MIB),
        cost_estimate=pl.CostEstimate(
            flops=0, bytes_accessed=2 * n * BLK * BLK * 4, transcendentals=0
        ),
        name="gather_blocks",
    )(row_pick, col_pick, density)


def round_parts(x, parts):
    rows, cols = x.shape
    wide = cols // parts
    bm = min(256, rows)
    steps = rows // bm

    def kernel(x_ref, *rest):
        outs, (raw_ref, low_ref, in_sems, out_sems) = rest[:parts], rest[parts:]

        def read(g):
            return pltpu.make_async_copy(
                x_ref.at[pl.ds(g * bm, bm)], raw_ref.at[g], in_sems.at[g]
            )

        def write(g, p):
            return pltpu.make_async_copy(
                low_ref.at[g, :, pl.ds(p * wide, wide)],
                outs[p].at[pl.ds(g * bm, bm)],
                out_sems.at[g, p],
            )

        for g in range(min(AHEAD, steps)):
            read(g).start()
        for g in range(steps):
            read(g).wait()
            if g + AHEAD < steps:
                read(g + AHEAD).start()
            low_ref[g] = raw_ref[g].astype(BF16)
            for p in range(parts):
                write(g, p).start()
        for g in range(steps):
            for p in range(parts):
                write(g, p).wait()

    return pl.pallas_call(
        kernel,
        grid=(1,),
        in_specs=[pl.BlockSpec(memory_space=pl.ANY)],
        out_specs=[pl.BlockSpec(memory_space=pl.ANY)] * parts,
        scratch_shapes=[
            pltpu.VMEM((steps, bm, cols), F32),
            pltpu.VMEM((steps, bm, cols), BF16),
            pltpu.SemaphoreType.DMA((steps,)),
            pltpu.SemaphoreType.DMA((steps, parts)),
        ],
        out_shape=[jax.ShapeDtypeStruct((rows, wide), BF16)] * parts,
        compiler_params=pltpu.CompilerParams(vmem_limit_bytes=56 * MIB),
        cost_estimate=pl.CostEstimate(
            flops=rows * cols, bytes_accessed=rows * cols * 6, transcendentals=0
        ),
        name="round_parts",
    )(x)


def update_blocks(low, h_blocks, arriving, picks):
    parts, wide = len(low), low[0].shape[1]
    n = arriving.shape[0]
    row_pick, col_pick, present = picks
    order = jnp.arange(n, dtype=jnp.int32)
    same = (
        (row_pick[:, None] == row_pick[None, :])
        & (col_pick[:, None] == col_pick[None, :])
        & (present[:, None] * present[None, :] > 0)
    )
    leader = jnp.min(jnp.where(same, order[None, :], n), axis=1)

    def kernel(row_ref, col_ref, lead_ref, in_ref, h_ref, *rest):
        outs, (work_ref, low_ref, sems) = rest[parts : 2 * parts], rest[2 * parts :]

        def add(s, carry):
            first = lead_ref[s]

            @pl.when(first == s)
            def _():
                work_ref[s] = h_ref[s] + in_ref[s].astype(F32)

            @pl.when(first < s)
            def _():
                work_ref[first] = work_ref[first] + in_ref[s].astype(F32)

            return carry

        def write(s, carry):
            @pl.when(lead_ref[s] == s)
            def _():
                low_ref[s] = work_ref[s].astype(BF16)
                top = pl.ds(pl.multiple_of(row_ref[s] * BLK, BLK), BLK)
                column = col_ref[s] * BLK
                for p in range(parts):

                    @pl.when((column >= p * wide) & (column < (p + 1) * wide))
                    def _(p=p):
                        left = pl.ds(pl.multiple_of(column - p * wide, BLK), BLK)
                        pltpu.make_async_copy(
                            low_ref.at[s], outs[p].at[top, left], sems.at[s]
                        ).start()

            return carry

        def wait(s, carry):
            @pl.when(lead_ref[s] == s)
            def _():
                pltpu.make_async_copy(
                    low_ref.at[s], outs[0].at[pl.ds(0, BLK), pl.ds(0, BLK)], sems.at[s]
                ).wait()

            return carry

        lax.fori_loop(0, n, add, 0)
        lax.fori_loop(0, n, write, 0)
        lax.fori_loop(0, n, wait, 0)

    whole = pl.BlockSpec((n, BLK, BLK), lambda i, *_: (0, 0, 0))
    return pl.pallas_call(
        kernel,
        grid_spec=pltpu.PrefetchScalarGridSpec(
            num_scalar_prefetch=3,
            grid=(1,),
            in_specs=[whole, whole] + [pl.BlockSpec(memory_space=pl.ANY)] * parts,
            out_specs=[pl.BlockSpec(memory_space=pl.ANY)] * parts,
            scratch_shapes=[
                pltpu.VMEM((n, BLK, BLK), F32),
                pltpu.VMEM((n, BLK, BLK), BF16),
                pltpu.SemaphoreType.DMA((n,)),
            ],
        ),
        out_shape=[jax.ShapeDtypeStruct(x.shape, x.dtype) for x in low],
        input_output_aliases={5 + p: p for p in range(parts)},
        compiler_params=pltpu.CompilerParams(vmem_limit_bytes=40 * MIB),
        cost_estimate=pl.CostEstimate(
            flops=n * BLK * BLK, bytes_accessed=n * BLK * BLK * 8, transcendentals=0
        ),
        name="update_blocks",
    )(row_pick, col_pick, leader, arriving, h_blocks, *low)


def split(x):
    hi = x.astype(BF16)
    return hi, (x - hi.astype(F32)).astype(BF16)


def basis_kernel(count_ref, phi_ref, hi_ref, lo_ref, hit_ref, lot_ref):
    basis = phi_ref[0]
    column = lax.broadcasted_iota(jnp.int32, basis.shape, 1)
    masked = jnp.where(column < count_ref[pl.program_id(0)] * BLK, basis, 0.0)
    hi, lo = split(masked)
    hi_ref[0] = hi
    lo_ref[0] = lo
    hit_ref[0] = hi.T
    lot_ref[0] = lo.T


def split_basis(phi, counts):
    tdev, npts, local = phi.shape
    spec = pl.BlockSpec((1, npts, local), lambda t, *_: (t, 0, 0))
    spec_t = pl.BlockSpec((1, local, npts), lambda t, *_: (t, 0, 0))
    return pl.pallas_call(
        basis_kernel,
        grid_spec=pltpu.PrefetchScalarGridSpec(
            num_scalar_prefetch=1,
            grid=(tdev,),
            in_specs=[spec],
            out_specs=[spec, spec, spec_t, spec_t],
        ),
        out_shape=[jax.ShapeDtypeStruct((tdev, npts, local), BF16)] * 2
        + [jax.ShapeDtypeStruct((tdev, local, npts), BF16)] * 2,
        compiler_params=pltpu.CompilerParams(vmem_limit_bytes=40 * MIB),
        cost_estimate=pl.CostEstimate(
            flops=4 * phi.size, bytes_accessed=12 * phi.size, transcendentals=0
        ),
        name="split_basis",
    )(counts, phi)


def mm(x, y):
    return jnp.dot(x, y, preferred_element_type=F32)


def tile_kernel(
    hold_ref,
    count_ref,
    in_ref,
    hi_ref,
    lo_ref,
    hit_ref,
    lot_ref,
    v_ref,
    out_ref,
    dh_ref,
    dl_ref,
):
    t = pl.program_id(0)
    maxb = hi_ref.shape[2] // BLK
    for i in range(maxb):
        for j in range(maxb):
            blk = in_ref[hold_ref[t, i * maxb + j]].astype(F32) * (1.0 / DM_SCALE)
            hi, lo = split(blk)
            dh_ref[i * BLK : (i + 1) * BLK, j * BLK : (j + 1) * BLK] = hi
            dl_ref[i * BLK : (i + 1) * BLK, j * BLK : (j + 1) * BLK] = lo
    count = count_ref[t]
    mh, ml = hi_ref[0], lo_ref[0]
    dh, dl = dh_ref[...], dl_ref[...]
    spread = mm(mh, dh) + (mm(ml, dh) + mm(mh, dl))
    masked = mh.astype(F32) + ml.astype(F32)
    rho = jnp.sum(spread * masked, axis=1, keepdims=True)
    potential = v_ref[0] + rho + cube_coef * rho * rho * rho
    wh, wl = split(masked * (potential * cell_volume))
    mht, mlt = hit_ref[0], lot_ref[0]
    ham = (mm(mht, wh) + (mm(mlt, wh) + mm(mht, wl))).astype(BF16)
    for i in range(maxb):
        for j in range(maxb):

            @pl.when((i < count) & (j < count))
            def _():
                out_ref[hold_ref[t, i * maxb + j]] = ham[
                    i * BLK : (i + 1) * BLK, j * BLK : (j + 1) * BLK
                ]


def tile_ham(incoming, basis, v_ext, hold, counts):
    n = incoming.shape[0]
    tdev, npts, local = basis[0].shape
    flops = tdev * 3 * 2 * 2 * npts * local * local
    spec = pl.BlockSpec((1, npts, local), lambda t, *_: (t, 0, 0))
    spec_t = pl.BlockSpec((1, local, npts), lambda t, *_: (t, 0, 0))
    return pl.pallas_call(
        tile_kernel,
        grid_spec=pltpu.PrefetchScalarGridSpec(
            num_scalar_prefetch=2,
            grid=(tdev,),
            in_specs=[
                pl.BlockSpec((n, BLK, BLK), lambda t, *_: (0, 0, 0)),
                spec,
                spec,
                spec_t,
                spec_t,
                pl.BlockSpec((1, npts, 1), lambda t, *_: (t, 0, 0)),
            ],
            out_specs=pl.BlockSpec((n, BLK, BLK), lambda t, *_: (0, 0, 0)),
            scratch_shapes=[
                pltpu.VMEM((local, local), BF16),
                pltpu.VMEM((local, local), BF16),
            ],
        ),
        out_shape=jax.ShapeDtypeStruct((n, BLK, BLK), BF16),
        compiler_params=pltpu.CompilerParams(vmem_limit_bytes=44 * MIB),
        cost_estimate=pl.CostEstimate(
            flops=flops, bytes_accessed=tdev * npts * local * 8, transcendentals=0
        ),
        name="tile_ham",
    )(hold, counts, incoming, *basis, v_ext[:, :, None])


def assemble(h_core, arriving, picks, dtype, first, parts, wide):
    rows, cols = h_core.shape[0], parts * wide
    n = arriving.shape[0]
    per = 2
    bm = per * BLK
    steps = rows // bm
    narrow = dtype != F32

    def kernel(row_ref, col_ref, present_ref, in_ref, h_ref, *rest):
        outs, rest = rest[:parts], rest[parts:]
        work_ref, in_sems, out_sems, num_ref, list_ref = rest[:5]
        low_refs = rest[5:] if narrow else (work_ref,)

        def band(g):
            return pl.ds(g * bm, bm)

        def read(g):
            return pltpu.make_async_copy(
                h_ref.at[band(g), pl.ds(first, cols)], work_ref.at[band(g)], in_sems.at[g]
            )

        def write(g, p):
            return pltpu.make_async_copy(
                low_refs[p].at[band(g)], outs[p].at[band(g)], out_sems.at[g, p]
            )

        for g in range(min(AHEAD, steps)):
            read(g).start()
        for g in range(steps):
            num_ref[g] = 0

        def note(s, carry):
            c = col_ref[s] * BLK

            @pl.when((present_ref[s] > 0) & (c >= first) & (c < first + cols))
            def _():
                g = row_ref[s] // per
                k = num_ref[g]
                list_ref[g * n + k] = s
                num_ref[g] = k + 1

            return carry

        lax.fori_loop(0, n, note, 0)

        for g in range(steps):
            read(g).wait()
            if g + AHEAD < steps:
                read(g + AHEAD).start()

            def add(k, carry, g=g):
                s = list_ref[g * n + k]
                top = pl.ds(pl.multiple_of(row_ref[s] * BLK, BLK), BLK)
                left = pl.ds(pl.multiple_of(col_ref[s] * BLK - first, BLK), BLK)
                work_ref[top, left] = work_ref[top, left] + in_ref[s].astype(F32)
                return carry

            lax.fori_loop(0, num_ref[g], add, 0)
            for p in range(parts):
                if narrow:
                    low_refs[p][band(g), :] = work_ref[band(g), p * wide : (p + 1) * wide].astype(
                        dtype
                    )
                write(g, p).start()
        for g in range(steps):
            for p in range(parts):
                write(g, p).wait()

    scratch = [
        pltpu.VMEM((rows, cols), F32),
        pltpu.SemaphoreType.DMA((steps,)),
        pltpu.SemaphoreType.DMA((steps, parts)),
        pltpu.SMEM((steps,), jnp.int32),
        pltpu.SMEM((steps * n,), jnp.int32),
    ]
    if narrow:
        scratch.extend([pltpu.VMEM((rows, wide), dtype)] * parts)
    return pl.pallas_call(
        kernel,
        grid_spec=pltpu.PrefetchScalarGridSpec(
            num_scalar_prefetch=3,
            grid=(1,),
            in_specs=[
                pl.BlockSpec((n, BLK, BLK), lambda i, *_: (0, 0, 0)),
                pl.BlockSpec(memory_space=pl.ANY),
            ],
            out_specs=[pl.BlockSpec(memory_space=pl.ANY)] * parts,
            scratch_shapes=scratch,
        ),
        out_shape=[jax.ShapeDtypeStruct((rows, wide), dtype)] * parts,
        compiler_params=pltpu.CompilerParams(vmem_limit_bytes=56 * MIB),
        cost_estimate=pl.CostEstimate(
            flops=rows * cols, bytes_accessed=rows * cols * 6, transcendentals=0
        ),
        name="assemble",
    )(*picks, arriving, h_core)


def product(cols, dm_panel, pieces):
    ncol, rows, width = dm_panel.shape
    depth = pieces[0][0][0][0].shape[0]
    per = depth // width
    bm = min(512, rows)
    npiece = len(pieces)
    nh = sum(len(arrays) for c, _, _ in pieces for arrays in c)
    scalars = jnp.stack(
        [jnp.asarray(s, jnp.int32) for _, _, s in pieces]
        + [jnp.asarray(w, jnp.int32) for _, w, _ in pieces]
    )

    def kernel(sc_ref, *refs):
        h_refs = refs[:nh]
        d_refs = refs[nh : nh + npiece]
        out_ref = refs[nh + npiece]
        held = refs[nh + npiece + 1 : -1]
        sems = refs[-1]

        @pl.when(pl.program_id(0) == 0)
        def _():
            at = 0
            for p, (candidates, _, _) in enumerate(pieces):
                for q, arrays in enumerate(candidates):
                    mine = h_refs[at : at + len(arrays)]
                    at += len(arrays)

                    @pl.when(sc_ref[npiece + p] == q)
                    def _(p=p, mine=mine):
                        left = 0
                        for ref in mine:
                            right = left + ref.shape[1]
                            pltpu.make_async_copy(
                                ref, held[p].at[:, left:right], sems.at[p]
                            ).start()
                            left = right

            for p in range(npiece):
                pltpu.make_async_copy(held[p], held[p], sems.at[p]).wait()

        acc = None
        for p in range(npiece):
            for q in range(per):
                term = mm(d_refs[p][q], held[p][q * width : (q + 1) * width, :])
                acc = term if acc is None else acc + term
        out_ref[...] = acc

    def d_map(p):
        return lambda i, sc: (sc[p], i, 0)

    return pl.pallas_call(
        kernel,
        grid_spec=pltpu.PrefetchScalarGridSpec(
            num_scalar_prefetch=1,
            grid=(rows // bm,),
            in_specs=[pl.BlockSpec(memory_space=pl.ANY)] * nh
            + [pl.BlockSpec((per, bm, width), d_map(p)) for p in range(npiece)],
            out_specs=pl.BlockSpec((bm, cols), lambda i, sc: (i, 0)),
            scratch_shapes=[pltpu.VMEM((depth, cols), BF16)] * npiece
            + [pltpu.SemaphoreType.DMA((npiece,))],
        ),
        out_shape=jax.ShapeDtypeStruct((rows, cols), F32),
        compiler_params=pltpu.CompilerParams(vmem_limit_bytes=56 * MIB),
        cost_estimate=pl.CostEstimate(
            flops=2 * npiece * rows * depth * cols,
            bytes_accessed=npiece * (rows + cols) * depth * 2 + rows * cols * 4,
            transcendentals=0,
        ),
        name="product",
    )(scalars, *[x for c, _, _ in pieces for arrays in c for x in arrays], *[dm_panel] * npiece)


def product_add(total, part, dm_panel, candidates, which, shard):
    ncol, rows, width = dm_panel.shape
    depth, wide = candidates[0].shape
    per = depth // width
    bm = min(512, rows)
    steps = rows // bm
    nh = len(candidates)
    scalars = jnp.stack([jnp.asarray(which, jnp.int32), jnp.asarray(shard, jnp.int32)])

    def kernel(sc_ref, *refs):
        h_refs = refs[:nh]
        dm_ref, total_ref, out_ref, held, d_ref, c_ref, h_sem, d_sems, c_sems, o_sems = refs[nh:]
        columns = pl.ds(part * wide, wide)

        def read_d(i, q):
            return pltpu.make_async_copy(
                dm_ref.at[sc_ref[1] * per + q, pl.ds(i * bm, bm)],
                d_ref.at[i, :, pl.ds(q * width, width)],
                d_sems.at[i, q],
            )

        def read_c(i):
            return pltpu.make_async_copy(
                total_ref.at[pl.ds(i * bm, bm), columns], c_ref.at[i], c_sems.at[i]
            )

        def write(i):
            return pltpu.make_async_copy(
                c_ref.at[i], out_ref.at[pl.ds(i * bm, bm), columns], o_sems.at[i]
            )

        for k in range(nh):

            @pl.when(sc_ref[0] == k)
            def _(k=k):
                pltpu.make_async_copy(h_refs[k], held, h_sem.at[0]).start()

        def start(i):
            for q in range(per):
                read_d(i, q).start()
            read_c(i).start()

        for i in range(min(2, steps)):
            start(i)
        pltpu.make_async_copy(h_refs[0], held, h_sem.at[0]).wait()
        for i in range(steps):
            for q in range(per):
                read_d(i, q).wait()
            read_c(i).wait()
            if i + 2 < steps:
                start(i + 2)
            c_ref[i] = c_ref[i] + mm(d_ref[i], held[...])
            write(i).start()
        for i in range(steps):
            write(i).wait()

    return pl.pallas_call(
        kernel,
        grid_spec=pltpu.PrefetchScalarGridSpec(
            num_scalar_prefetch=1,
            grid=(1,),
            in_specs=[pl.BlockSpec(memory_space=pl.ANY)] * (nh + 2),
            out_specs=pl.BlockSpec(memory_space=pl.ANY),
            scratch_shapes=[
                pltpu.VMEM((depth, wide), BF16),
                pltpu.VMEM((steps, bm, depth), BF16),
                pltpu.VMEM((steps, bm, wide), F32),
                pltpu.SemaphoreType.DMA((1,)),
                pltpu.SemaphoreType.DMA((steps, per)),
                pltpu.SemaphoreType.DMA((steps,)),
                pltpu.SemaphoreType.DMA((steps,)),
            ],
        ),
        out_shape=jax.ShapeDtypeStruct(total.shape, F32),
        input_output_aliases={2 + nh: 0},
        compiler_params=pltpu.CompilerParams(vmem_limit_bytes=56 * MIB),
        cost_estimate=pl.CostEstimate(
            flops=2 * rows * depth * wide,
            bytes_accessed=(rows + wide) * depth * 2 + rows * wide * 8,
            transcendentals=0,
        ),
        name="product_add",
    )(scalars, *candidates, dm_panel, total)


PARTS = 4


def tie(x, y):
    return lax.optimization_barrier((x, y))


def body(density, h_core, phi, v_ext, tile_blocks, tile_count):
    nrow = lax.axis_size("row")
    ncol = lax.axis_size("col")
    ndev = nrow * ncol
    row_idx = lax.axis_index("row")
    col_idx = lax.axis_index("col")
    myself = row_idx * ncol + col_idx
    rows_loc, cols_loc = density.shape
    rowb = rows_loc // BLK
    colb = cols_loc // BLK
    tdev, npts, local = phi.shape
    maxb = tile_blocks.shape[1]
    line = nrow == 4

    swap = [(0, 1), (1, 0), (2, 3), (3, 2)]
    cross = [(1, 2), (2, 1)]
    outward = [(1, 0), (2, 3)]

    blocks = tile_blocks.reshape(ndev, tdev, maxb)
    counts = tile_count.reshape(ndev, tdev)
    live = jnp.arange(maxb, dtype=jnp.int32)[None, None, :] < counts[:, :, None]
    col_hit = live & (blocks // colb == col_idx)
    col_in = jnp.sum(jnp.where(col_hit, blocks - col_idx * colb, 0), axis=2)

    def picks_of(row):
        row_hit = live & (blocks // rowb == row)
        both = jnp.any(row_hit, axis=2) & jnp.any(col_hit, axis=2)
        row_in = jnp.sum(jnp.where(row_hit, blocks - row * rowb, 0), axis=2)
        row_pick = jnp.sum(jnp.where(both, row_in, 0), axis=1)
        col_pick = jnp.sum(jnp.where(both, col_in, 0), axis=1)
        return row_pick, col_pick, jnp.any(both, axis=1).astype(jnp.int32)

    picks = picks_of(row_idx)
    mine = lax.dynamic_index_in_dim(blocks, myself, 0, keepdims=False)
    my_counts = lax.dynamic_index_in_dim(counts, myself, 0, keepdims=False)
    hold = ((mine // rowb)[:, :, None] * ncol + (mine // colb)[:, None, :]).reshape(tdev, -1)

    outgoing = (gather_blocks(density, picks[0], picks[1]) * DM_SCALE).astype(jnp.float16)
    incoming = lax.all_to_all(outgoing, ("row", "col"), split_axis=0, concat_axis=0, tiled=True)
    basis = split_basis(phi, my_counts)
    (dm_low,) = round_parts(density, 1)
    incoming, (dm_low, basis) = tie(incoming, (dm_low, basis))
    dm_panel = lax.all_gather(dm_low, "col", axis=0, tiled=False)

    returning = tile_ham(incoming.astype(F32), basis, v_ext, hold, my_counts)
    arriving = lax.all_to_all(returning, ("row", "col"), split_axis=0, concat_axis=0, tiled=True)
    parts = PARTS if line and cols_loc % (PARTS * BLK) == 0 else 1
    wide = cols_loc // parts
    low = round_parts(h_core, parts)
    h_blocks = gather_blocks(h_core, picks[0], picks[1])
    arriving, (low, h_blocks) = tie(arriving, (low, h_blocks))
    low = update_blocks(low, h_blocks, arriving, picks)
    (hamiltonian,) = assemble(h_core, arriving, picks, F32, 0, 1, cols_loc)

    if line:
        pair_idx = row_idx + 1 - 2 * (row_idx % 2)
        is_low = row_idx < 2
        is_end = ((row_idx == 0) | (row_idx == 3)).astype(jnp.int32)
        near_idx = jnp.where(is_low, 2, 1)
        far_idx = jnp.where(is_low, 3, 0)
        pair, near_mid = [], []
        for p in range(parts):
            ready = low[p] if p < 2 else tie(low[p], near_mid[p - 2])[0]
            pair.append(lax.ppermute(ready, "row", swap))
            near_mid.append(lax.ppermute(ready, "row", cross))
        near_end = [lax.ppermute(x, "row", outward) for x in near_mid]
        far_mid = []
        for p in range(parts):
            ready = pair[p]
            if p > 0:
                ready, near_end[p - 1] = tie(ready, near_end[p - 1])
            far_mid.append(lax.ppermute(ready, "row", cross))
        far_end = []
        for p in range(parts):
            ready = far_mid[p]
            if p == parts - 1:
                ready, near_end[p] = tie(ready, near_end[p])
            far_end.append(lax.ppermute(ready, "row", outward))
        total = product(
            cols_loc,
            dm_panel,
            [
                ((low,), 0, row_idx),
                ((pair,), 0, pair_idx),
                ((near_mid, near_end), is_end, near_idx),
            ],
        )
        for p in range(parts):
            total = product_add(
                total, p, dm_panel, (far_mid[p], far_end[p]), is_end, far_idx
            )
    else:
        ham_panel = lax.all_gather(low[0], "row", axis=0, tiled=False)
        total = product(cols_loc, dm_panel, [(((ham_panel[0],),), 0, 0)])
        for k in range(1, nrow):
            total = product_add(total, 0, dm_panel, (ham_panel[k],), 0, k)
    return hamiltonian, total


def solution(mesh):
    placed = (
        P("row", "col"),
        P("row", "col"),
        P(("row", "col"), None, None),
        P(("row", "col"), None),
        P(),
        P(),
    )
    return jax.shard_map(
        body,
        mesh=mesh,
        in_specs=placed,
        out_specs=(P("row", "col"), P("row", "col")),
        check_vma=False,
    )
```

```python
import jax
import jax.numpy as jnp
from jax import lax
from jax.experimental import pallas as pl
from jax.experimental.pallas import tpu as pltpu
from jax.sharding import PartitionSpec as P

BLK = 128

cube_coef = 0.5
cell_volume = 0.03125
DM_SCALE = float(2**20)

F32 = jnp.float32
BF16 = jnp.bfloat16
MIB = 1 << 20
AHEAD = 3


def gather_kernel(row_ref, col_ref, dens_ref, out_ref, sems):
    n = out_ref.shape[0]

    def copy(s):
        r = pl.multiple_of(row_ref[s] * BLK, BLK)
        c = pl.multiple_of(col_ref[s] * BLK, BLK)
        return pltpu.make_async_copy(
            dens_ref.at[pl.ds(r, BLK), pl.ds(c, BLK)], out_ref.at[s], sems.at[s]
        )

    def start(s, carry):
        copy(s).start()
        return carry

    def wait(s, carry):
        copy(s).wait()
        return carry

    lax.fori_loop(0, n, start, 0)
    lax.fori_loop(0, n, wait, 0)


def gather_blocks(density, row_pick, col_pick):
    n = row_pick.shape[0]
    return pl.pallas_call(
        gather_kernel,
        grid_spec=pltpu.PrefetchScalarGridSpec(
            num_scalar_prefetch=2,
            grid=(1,),
            in_specs=[pl.BlockSpec(memory_space=pltpu.HBM)],
            out_specs=pl.BlockSpec((n, BLK, BLK), lambda i, *_: (0, 0, 0)),
            scratch_shapes=[pltpu.SemaphoreType.DMA((n,))],
        ),
        out_shape=jax.ShapeDtypeStruct((n, BLK, BLK), F32),
        compiler_params=pltpu.CompilerParams(vmem_limit_bytes=60 * MIB),
        cost_estimate=pl.CostEstimate(
            flops=0, bytes_accessed=2 * n * BLK * BLK * 4, transcendentals=0
        ),
        name="gather_blocks",
    )(row_pick, col_pick, density)


def round_parts(x, parts):
    rows, cols = x.shape
    wide = cols // parts
    bm = min(256, rows)
    steps = rows // bm

    def kernel(x_ref, *rest):
        outs, (raw_ref, low_ref, in_sems, out_sems) = rest[:parts], rest[parts:]

        def read(g):
            return pltpu.make_async_copy(
                x_ref.at[pl.ds(g * bm, bm)], raw_ref.at[g], in_sems.at[g]
            )

        def write(g, p):
            return pltpu.make_async_copy(
                low_ref.at[g, :, pl.ds(p * wide, wide)],
                outs[p].at[pl.ds(g * bm, bm)],
                out_sems.at[g, p],
            )

        for g in range(min(AHEAD, steps)):
            read(g).start()
        for g in range(steps):
            read(g).wait()
            if g + AHEAD < steps:
                read(g + AHEAD).start()
            low_ref[g] = raw_ref[g].astype(BF16)
            for p in range(parts):
                write(g, p).start()
        for g in range(steps):
            for p in range(parts):
                write(g, p).wait()

    return pl.pallas_call(
        kernel,
        grid=(1,),
        in_specs=[pl.BlockSpec(memory_space=pltpu.HBM)],
        out_specs=[pl.BlockSpec(memory_space=pltpu.HBM)] * parts,
        scratch_shapes=[
            pltpu.VMEM((steps, bm, cols), F32),
            pltpu.VMEM((steps, bm, cols), BF16),
            pltpu.SemaphoreType.DMA((steps,)),
            pltpu.SemaphoreType.DMA((steps, parts)),
        ],
        out_shape=[jax.ShapeDtypeStruct((rows, wide), BF16)] * parts,
        compiler_params=pltpu.CompilerParams(vmem_limit_bytes=60 * MIB),
        cost_estimate=pl.CostEstimate(
            flops=rows * cols, bytes_accessed=rows * cols * 6, transcendentals=0
        ),
        name="round_parts",
    )(x)


def update_blocks(low, h_blocks, arriving, picks):
    parts, wide = len(low), low[0].shape[1]
    n = arriving.shape[0]
    row_pick, col_pick, present = picks
    order = jnp.arange(n, dtype=jnp.int32)
    same = (
        (row_pick[:, None] == row_pick[None, :])
        & (col_pick[:, None] == col_pick[None, :])
        & (present[:, None] * present[None, :] > 0)
    )
    leader = jnp.min(jnp.where(same, order[None, :], n), axis=1)

    def kernel(row_ref, col_ref, lead_ref, in_ref, h_ref, *rest):
        outs, (work_ref, low_ref, sems) = rest[parts : 2 * parts], rest[2 * parts :]

        def add(s, carry):
            first = lead_ref[s]

            @pl.when(first == s)
            def _():
                work_ref[s] = h_ref[s] + in_ref[s].astype(F32)

            @pl.when(first < s)
            def _():
                work_ref[first] = work_ref[first] + in_ref[s].astype(F32)

            return carry

        def write(s, carry):
            @pl.when(lead_ref[s] == s)
            def _():
                low_ref[s] = work_ref[s].astype(BF16)
                top = pl.ds(pl.multiple_of(row_ref[s] * BLK, BLK), BLK)
                column = col_ref[s] * BLK
                for p in range(parts):

                    @pl.when((column >= p * wide) & (column < (p + 1) * wide))
                    def _(p=p):
                        left = pl.ds(pl.multiple_of(column - p * wide, BLK), BLK)
                        pltpu.make_async_copy(
                            low_ref.at[s], outs[p].at[top, left], sems.at[s]
                        ).start()

            return carry

        def wait(s, carry):
            @pl.when(lead_ref[s] == s)
            def _():
                pltpu.make_async_copy(
                    low_ref.at[s], outs[0].at[pl.ds(0, BLK), pl.ds(0, BLK)], sems.at[s]
                ).wait()

            return carry

        lax.fori_loop(0, n, add, 0)
        lax.fori_loop(0, n, write, 0)
        lax.fori_loop(0, n, wait, 0)

    whole = pl.BlockSpec((n, BLK, BLK), lambda i, *_: (0, 0, 0))
    return pl.pallas_call(
        kernel,
        grid_spec=pltpu.PrefetchScalarGridSpec(
            num_scalar_prefetch=3,
            grid=(1,),
            in_specs=[whole, whole] + [pl.BlockSpec(memory_space=pltpu.HBM)] * parts,
            out_specs=[pl.BlockSpec(memory_space=pltpu.HBM)] * parts,
            scratch_shapes=[
                pltpu.VMEM((n, BLK, BLK), F32),
                pltpu.VMEM((n, BLK, BLK), BF16),
                pltpu.SemaphoreType.DMA((n,)),
            ],
        ),
        out_shape=[jax.ShapeDtypeStruct(x.shape, x.dtype) for x in low],
        input_output_aliases={5 + p: p for p in range(parts)},
        compiler_params=pltpu.CompilerParams(vmem_limit_bytes=60 * MIB),
        cost_estimate=pl.CostEstimate(
            flops=n * BLK * BLK, bytes_accessed=n * BLK * BLK * 8, transcendentals=0
        ),
        name="update_blocks",
    )(row_pick, col_pick, leader, arriving, h_blocks, *low)


def split(x):
    hi = x.astype(BF16)
    return hi, (x - hi.astype(F32)).astype(BF16)


def basis_kernel(count_ref, phi_ref, hi_ref, lo_ref, hit_ref, lot_ref):
    basis = phi_ref[0]
    column = lax.broadcasted_iota(jnp.int32, basis.shape, 1)
    masked = jnp.where(column < count_ref[pl.program_id(0)] * BLK, basis, 0.0)
    hi, lo = split(masked)
    hi_ref[0] = hi
    lo_ref[0] = lo
    hit_ref[0] = hi.T
    lot_ref[0] = lo.T


def split_basis(phi, counts):
    tdev, npts, local = phi.shape
    spec = pl.BlockSpec((1, npts, local), lambda t, *_: (t, 0, 0))
    spec_t = pl.BlockSpec((1, local, npts), lambda t, *_: (t, 0, 0))
    return pl.pallas_call(
        basis_kernel,
        grid_spec=pltpu.PrefetchScalarGridSpec(
            num_scalar_prefetch=1,
            grid=(tdev,),
            in_specs=[spec],
            out_specs=[spec, spec, spec_t, spec_t],
        ),
        out_shape=[jax.ShapeDtypeStruct((tdev, npts, local), BF16)] * 2
        + [jax.ShapeDtypeStruct((tdev, local, npts), BF16)] * 2,
        compiler_params=pltpu.CompilerParams(vmem_limit_bytes=60 * MIB),
        cost_estimate=pl.CostEstimate(
            flops=4 * phi.size, bytes_accessed=12 * phi.size, transcendentals=0
        ),
        name="split_basis",
    )(counts, phi)


def mm(x, y):
    return jnp.dot(x, y, preferred_element_type=F32)


def tile_kernel(
    hold_ref,
    count_ref,
    in_ref,
    hi_ref,
    lo_ref,
    hit_ref,
    lot_ref,
    v_ref,
    out_ref,
    dh_ref,
    dl_ref,
):
    t = pl.program_id(0)
    maxb = hi_ref.shape[2] // BLK
    for i in range(maxb):
        for j in range(maxb):
            blk = in_ref[hold_ref[t, i * maxb + j]].astype(F32) * (1.0 / DM_SCALE)
            hi, lo = split(blk)
            dh_ref[i * BLK : (i + 1) * BLK, j * BLK : (j + 1) * BLK] = hi
            dl_ref[i * BLK : (i + 1) * BLK, j * BLK : (j + 1) * BLK] = lo
    count = count_ref[t]
    mh, ml = hi_ref[0], lo_ref[0]
    dh, dl = dh_ref[...], dl_ref[...]
    spread = mm(mh, dh) + (mm(ml, dh) + mm(mh, dl))
    masked = mh.astype(F32) + ml.astype(F32)
    rho = jnp.sum(spread * masked, axis=1, keepdims=True)
    potential = v_ref[0] + rho + cube_coef * rho * rho * rho
    wh, wl = split(masked * (potential * cell_volume))
    mht, mlt = hit_ref[0], lot_ref[0]
    ham = (mm(mht, wh) + (mm(mlt, wh) + mm(mht, wl))).astype(BF16)
    for i in range(maxb):
        for j in range(maxb):

            @pl.when((i < count) & (j < count))
            def _():
                out_ref[hold_ref[t, i * maxb + j]] = ham[
                    i * BLK : (i + 1) * BLK, j * BLK : (j + 1) * BLK
                ]


def tile_ham(incoming, basis, v_ext, hold, counts):
    n = incoming.shape[0]
    tdev, npts, local = basis[0].shape
    flops = tdev * 3 * 2 * 2 * npts * local * local
    spec = pl.BlockSpec((1, npts, local), lambda t, *_: (t, 0, 0))
    spec_t = pl.BlockSpec((1, local, npts), lambda t, *_: (t, 0, 0))
    return pl.pallas_call(
        tile_kernel,
        grid_spec=pltpu.PrefetchScalarGridSpec(
            num_scalar_prefetch=2,
            grid=(tdev,),
            in_specs=[
                pl.BlockSpec((n, BLK, BLK), lambda t, *_: (0, 0, 0)),
                spec,
                spec,
                spec_t,
                spec_t,
                pl.BlockSpec((1, npts, 1), lambda t, *_: (t, 0, 0)),
            ],
            out_specs=pl.BlockSpec((n, BLK, BLK), lambda t, *_: (0, 0, 0)),
            scratch_shapes=[
                pltpu.VMEM((local, local), BF16),
                pltpu.VMEM((local, local), BF16),
            ],
        ),
        out_shape=jax.ShapeDtypeStruct((n, BLK, BLK), BF16),
        compiler_params=pltpu.CompilerParams(vmem_limit_bytes=60 * MIB),
        cost_estimate=pl.CostEstimate(
            flops=flops, bytes_accessed=tdev * npts * local * 8, transcendentals=0
        ),
        name="tile_ham",
    )(hold, counts, incoming, *basis, v_ext[:, :, None])


def assemble(h_core, arriving, picks, dtype, first, parts, wide):
    rows, cols = h_core.shape[0], parts * wide
    n = arriving.shape[0]
    per = 2
    bm = per * BLK
    steps = rows // bm
    narrow = dtype != F32

    def kernel(row_ref, col_ref, present_ref, in_ref, h_ref, *rest):
        outs, rest = rest[:parts], rest[parts:]
        work_ref, in_sems, out_sems, num_ref, list_ref = rest[:5]
        low_refs = rest[5:] if narrow else (work_ref,)

        def band(g):
            return pl.ds(g * bm, bm)

        def read(g):
            return pltpu.make_async_copy(
                h_ref.at[band(g), pl.ds(first, cols)], work_ref.at[band(g)], in_sems.at[g]
            )

        def write(g, p):
            return pltpu.make_async_copy(
                low_refs[p].at[band(g)], outs[p].at[band(g)], out_sems.at[g, p]
            )

        for g in range(min(AHEAD, steps)):
            read(g).start()
        for g in range(steps):
            num_ref[g] = 0

        def note(s, carry):
            c = col_ref[s] * BLK

            @pl.when((present_ref[s] > 0) & (c >= first) & (c < first + cols))
            def _():
                g = row_ref[s] // per
                k = num_ref[g]
                list_ref[g * n + k] = s
                num_ref[g] = k + 1

            return carry

        lax.fori_loop(0, n, note, 0)

        for g in range(steps):
            read(g).wait()
            if g + AHEAD < steps:
                read(g + AHEAD).start()

            def add(k, carry, g=g):
                s = list_ref[g * n + k]
                top = pl.ds(pl.multiple_of(row_ref[s] * BLK, BLK), BLK)
                left = pl.ds(pl.multiple_of(col_ref[s] * BLK - first, BLK), BLK)
                work_ref[top, left] = work_ref[top, left] + in_ref[s].astype(F32)
                return carry

            lax.fori_loop(0, num_ref[g], add, 0)
            for p in range(parts):
                if narrow:
                    low_refs[p][band(g), :] = work_ref[band(g), p * wide : (p + 1) * wide].astype(
                        dtype
                    )
                write(g, p).start()
        for g in range(steps):
            for p in range(parts):
                write(g, p).wait()

    scratch = [
        pltpu.VMEM((rows, cols), F32),
        pltpu.SemaphoreType.DMA((steps,)),
        pltpu.SemaphoreType.DMA((steps, parts)),
        pltpu.SMEM((steps,), jnp.int32),
        pltpu.SMEM((steps * n,), jnp.int32),
    ]
    if narrow:
        scratch.extend([pltpu.VMEM((rows, wide), dtype)] * parts)
    return pl.pallas_call(
        kernel,
        grid_spec=pltpu.PrefetchScalarGridSpec(
            num_scalar_prefetch=3,
            grid=(1,),
            in_specs=[
                pl.BlockSpec((n, BLK, BLK), lambda i, *_: (0, 0, 0)),
                pl.BlockSpec(memory_space=pl.ANY),
            ],
            out_specs=[pl.BlockSpec(memory_space=pl.ANY)] * parts,
            scratch_shapes=scratch,
        ),
        out_shape=[jax.ShapeDtypeStruct((rows, wide), dtype)] * parts,
        compiler_params=pltpu.CompilerParams(vmem_limit_bytes=60 * MIB),
        cost_estimate=pl.CostEstimate(
            flops=rows * cols, bytes_accessed=rows * cols * 6, transcendentals=0
        ),
        name="assemble",
    )(*picks, arriving, h_core)


def product(cols, dm_panel, pieces):
    ncol, rows, width = dm_panel.shape
    depth = pieces[0][0][0][0].shape[0]
    per = depth // width
    bm = min(512, rows)
    npiece = len(pieces)
    nh = sum(len(arrays) for c, _, _ in pieces for arrays in c)
    scalars = jnp.stack(
        [jnp.asarray(s, jnp.int32) for _, _, s in pieces]
        + [jnp.asarray(w, jnp.int32) for _, w, _ in pieces]
    )

    def kernel(sc_ref, *refs):
        h_refs = refs[:nh]
        d_refs = refs[nh : nh + npiece]
        out_ref = refs[nh + npiece]
        held = refs[nh + npiece + 1 : -1]
        sems = refs[-1]

        @pl.when(pl.program_id(0) == 0)
        def _():
            at = 0
            for p, (candidates, _, _) in enumerate(pieces):
                for q, arrays in enumerate(candidates):
                    mine = h_refs[at : at + len(arrays)]
                    at += len(arrays)

                    @pl.when(sc_ref[npiece + p] == q)
                    def _(p=p, mine=mine):
                        left = 0
                        for ref in mine:
                            right = left + ref.shape[1]
                            pltpu.make_async_copy(
                                ref, held[p].at[:, left:right], sems.at[p]
                            ).start()
                            left = right

            for p in range(npiece):
                pltpu.make_async_copy(held[p], held[p], sems.at[p]).wait()

        acc = None
        for p in range(npiece):
            for q in range(per):
                term = mm(d_refs[p][q], held[p][q * width : (q + 1) * width, :])
                acc = term if acc is None else acc + term
        out_ref[...] = acc

    def d_map(p):
        return lambda i, sc: (sc[p], i, 0)

    return pl.pallas_call(
        kernel,
        grid_spec=pltpu.PrefetchScalarGridSpec(
            num_scalar_prefetch=1,
            grid=(rows // bm,),
            in_specs=[pl.BlockSpec(memory_space=pl.ANY)] * nh
            + [pl.BlockSpec((per, bm, width), d_map(p)) for p in range(npiece)],
            out_specs=pl.BlockSpec((bm, cols), lambda i, sc: (i, 0)),
            scratch_shapes=[pltpu.VMEM((depth, cols), BF16)] * npiece
            + [pltpu.SemaphoreType.DMA((npiece,))],
        ),
        out_shape=jax.ShapeDtypeStruct((rows, cols), F32),
        compiler_params=pltpu.CompilerParams(vmem_limit_bytes=60 * MIB),
        cost_estimate=pl.CostEstimate(
            flops=2 * npiece * rows * depth * cols,
            bytes_accessed=npiece * (rows + cols) * depth * 2 + rows * cols * 4,
            transcendentals=0,
        ),
        name="product",
    )(scalars, *[x for c, _, _ in pieces for arrays in c for x in arrays], *[dm_panel] * npiece)


def product_add(total, part, dm_panel, candidates, which, shard):
    ncol, rows, width = dm_panel.shape
    depth, wide = candidates[0].shape
    per = depth // width
    bm = min(512, rows)
    steps = rows // bm
    nh = len(candidates)
    scalars = jnp.stack([jnp.asarray(which, jnp.int32), jnp.asarray(shard, jnp.int32)])

    def kernel(sc_ref, *refs):
        h_refs = refs[:nh]
        dm_ref, total_ref, out_ref, held, d_ref, c_ref, h_sem, d_sems, c_sems, o_sems = refs[nh:]
        columns = pl.ds(part * wide, wide)

        def read_d(i, q):
            return pltpu.make_async_copy(
                dm_ref.at[sc_ref[1] * per + q, pl.ds(i * bm, bm)],
                d_ref.at[i, :, pl.ds(q * width, width)],
                d_sems.at[i, q],
            )

        def read_c(i):
            return pltpu.make_async_copy(
                total_ref.at[pl.ds(i * bm, bm), columns], c_ref.at[i], c_sems.at[i]
            )

        def write(i):
            return pltpu.make_async_copy(
                c_ref.at[i], out_ref.at[pl.ds(i * bm, bm), columns], o_sems.at[i]
            )

        for k in range(nh):

            @pl.when(sc_ref[0] == k)
            def _(k=k):
                pltpu.make_async_copy(h_refs[k], held, h_sem.at[0]).start()

        def start(i):
            for q in range(per):
                read_d(i, q).start()
            read_c(i).start()

        for i in range(min(2, steps)):
            start(i)
        pltpu.make_async_copy(h_refs[0], held, h_sem.at[0]).wait()
        for i in range(steps):
            for q in range(per):
                read_d(i, q).wait()
            read_c(i).wait()
            if i + 2 < steps:
                start(i + 2)
            c_ref[i] = c_ref[i] + mm(d_ref[i], held[...])
            write(i).start()
        for i in range(steps):
            write(i).wait()

    return pl.pallas_call(
        kernel,
        grid_spec=pltpu.PrefetchScalarGridSpec(
            num_scalar_prefetch=1,
            grid=(1,),
            in_specs=[pl.BlockSpec(memory_space=pl.ANY)] * (nh + 2),
            out_specs=pl.BlockSpec(memory_space=pl.ANY),
            scratch_shapes=[
                pltpu.VMEM((depth, wide), BF16),
                pltpu.VMEM((steps, bm, depth), BF16),
                pltpu.VMEM((steps, bm, wide), F32),
                pltpu.SemaphoreType.DMA((1,)),
                pltpu.SemaphoreType.DMA((steps, per)),
                pltpu.SemaphoreType.DMA((steps,)),
                pltpu.SemaphoreType.DMA((steps,)),
            ],
        ),
        out_shape=jax.ShapeDtypeStruct(total.shape, F32),
        input_output_aliases={2 + nh: 0},
        compiler_params=pltpu.CompilerParams(vmem_limit_bytes=60 * MIB),
        cost_estimate=pl.CostEstimate(
            flops=2 * rows * depth * wide,
            bytes_accessed=(rows + wide) * depth * 2 + rows * wide * 8,
            transcendentals=0,
        ),
        name="product_add",
    )(scalars, *candidates, dm_panel, total)


PARTS = 4


def tie(x, y):
    return lax.optimization_barrier((x, y))


def body(density, h_core, phi, v_ext, tile_blocks, tile_count):
    nrow = lax.axis_size("row")
    ncol = lax.axis_size("col")
    ndev = nrow * ncol
    row_idx = lax.axis_index("row")
    col_idx = lax.axis_index("col")
    myself = row_idx * ncol + col_idx
    rows_loc, cols_loc = density.shape
    rowb = rows_loc // BLK
    colb = cols_loc // BLK
    tdev, npts, local = phi.shape
    maxb = tile_blocks.shape[1]
    line = nrow == 4

    swap = [(0, 1), (1, 0), (2, 3), (3, 2)]
    cross = [(1, 2), (2, 1)]
    outward = [(1, 0), (2, 3)]

    blocks = tile_blocks.reshape(ndev, tdev, maxb)
    counts = tile_count.reshape(ndev, tdev)
    live = jnp.arange(maxb, dtype=jnp.int32)[None, None, :] < counts[:, :, None]
    col_hit = live & (blocks // colb == col_idx)
    col_in = jnp.sum(jnp.where(col_hit, blocks - col_idx * colb, 0), axis=2)

    def picks_of(row):
        row_hit = live & (blocks // rowb == row)
        both = jnp.any(row_hit, axis=2) & jnp.any(col_hit, axis=2)
        row_in = jnp.sum(jnp.where(row_hit, blocks - row * rowb, 0), axis=2)
        row_pick = jnp.sum(jnp.where(both, row_in, 0), axis=1)
        col_pick = jnp.sum(jnp.where(both, col_in, 0), axis=1)
        return row_pick, col_pick, jnp.any(both, axis=1).astype(jnp.int32)

    picks = picks_of(row_idx)
    mine = lax.dynamic_index_in_dim(blocks, myself, 0, keepdims=False)
    my_counts = lax.dynamic_index_in_dim(counts, myself, 0, keepdims=False)
    hold = ((mine // rowb)[:, :, None] * ncol + (mine // colb)[:, None, :]).reshape(tdev, -1)

    outgoing = (gather_blocks(density, picks[0], picks[1]) * DM_SCALE).astype(jnp.float16)
    incoming = lax.all_to_all(outgoing, ("row", "col"), split_axis=0, concat_axis=0, tiled=True)
    basis = split_basis(phi, my_counts)
    (dm_low,) = round_parts(density, 1)
    incoming, (dm_low, basis) = tie(incoming, (dm_low, basis))
    dm_panel = lax.all_gather(dm_low, "col", axis=0, tiled=False)

    returning = tile_ham(incoming.astype(F32), basis, v_ext, hold, my_counts)
    arriving = lax.all_to_all(returning, ("row", "col"), split_axis=0, concat_axis=0, tiled=True)
    parts = PARTS if line and cols_loc % (PARTS * BLK) == 0 else 1
    wide = cols_loc // parts
    low = round_parts(h_core, parts)
    h_blocks = gather_blocks(h_core, picks[0], picks[1])
    arriving, (low, h_blocks) = tie(arriving, (low, h_blocks))
    low = update_blocks(low, h_blocks, arriving, picks)
    (hamiltonian,) = assemble(h_core, arriving, picks, F32, 0, 1, cols_loc)

    if line:
        pair_idx = row_idx + 1 - 2 * (row_idx % 2)
        is_low = row_idx < 2
        is_end = ((row_idx == 0) | (row_idx == 3)).astype(jnp.int32)
        near_idx = jnp.where(is_low, 2, 1)
        far_idx = jnp.where(is_low, 3, 0)
        pair, near_mid = [], []
        for p in range(parts):
            ready = low[p] if p < 2 else tie(low[p], near_mid[p - 2])[0]
            pair.append(lax.ppermute(ready, "row", swap))
            near_mid.append(lax.ppermute(ready, "row", cross))
        near_end = [lax.ppermute(x, "row", outward) for x in near_mid]
        far_mid = []
        for p in range(parts):
            ready = pair[p]
            if p > 0:
                ready, near_end[p - 1] = tie(ready, near_end[p - 1])
            far_mid.append(lax.ppermute(ready, "row", cross))
        far_end = []
        for p in range(parts):
            ready = far_mid[p]
            if p == parts - 1:
                ready, near_end[p] = tie(ready, near_end[p])
            far_end.append(lax.ppermute(ready, "row", outward))
        total = product(
            cols_loc,
            dm_panel,
            [
                ((low,), 0, row_idx),
                ((pair,), 0, pair_idx),
                ((near_mid, near_end), is_end, near_idx),
            ],
        )
        for p in range(parts):
            total = product_add(
                total, p, dm_panel, (far_mid[p], far_end[p]), is_end, far_idx
            )
    else:
        ham_panel = lax.all_gather(low[0], "row", axis=0, tiled=False)
        total = product(cols_loc, dm_panel, [(((ham_panel[0],),), 0, 0)])
        for k in range(1, nrow):
            total = product_add(total, 0, dm_panel, (ham_panel[k],), 0, k)
    return hamiltonian, total


def solution(mesh):
    placed = (
        P("row", "col"),
        P("row", "col"),
        P(("row", "col"), None, None),
        P(("row", "col"), None),
        P(),
        P(),
    )
    return jax.shard_map(
        body,
        mesh=mesh,
        in_specs=placed,
        out_specs=(P("row", "col"), P("row", "col")),
        check_vma=False,
    )
```

```python
import jax
import jax.numpy as jnp
from jax import lax
from jax.experimental import pallas as pl
from jax.experimental.pallas import tpu as pltpu
from jax.sharding import PartitionSpec as P

BLK = 128

cube_coef = 0.5
cell_volume = 0.03125
DM_SCALE = float(2**20)

F32 = jnp.float32
BF16 = jnp.bfloat16
MIB = 1 << 20
AHEAD = 3


def gather_kernel(row_ref, col_ref, dens_ref, out_ref, sems):
    n = out_ref.shape[0]

    def copy(s):
        r = pl.multiple_of(row_ref[s] * BLK, BLK)
        c = pl.multiple_of(col_ref[s] * BLK, BLK)
        return pltpu.make_async_copy(
            dens_ref.at[pl.ds(r, BLK), pl.ds(c, BLK)], out_ref.at[s], sems.at[s]
        )

    def start(s, carry):
        copy(s).start()
        return carry

    def wait(s, carry):
        copy(s).wait()
        return carry

    lax.fori_loop(0, n, start, 0)
    lax.fori_loop(0, n, wait, 0)


def gather_blocks(density, row_pick, col_pick):
    n = row_pick.shape[0]
    return pl.pallas_call(
        gather_kernel,
        grid_spec=pltpu.PrefetchScalarGridSpec(
            num_scalar_prefetch=2,
            grid=(1,),
            in_specs=[pl.BlockSpec(memory_space=pltpu.HBM)],
            out_specs=pl.BlockSpec((n, BLK, BLK), lambda i, *_: (0, 0, 0)),
            scratch_shapes=[pltpu.SemaphoreType.DMA((n,))],
        ),
        out_shape=jax.ShapeDtypeStruct((n, BLK, BLK), F32),
        compiler_params=pltpu.CompilerParams(vmem_limit_bytes=57 * MIB),
        cost_estimate=pl.CostEstimate(
            flops=0, bytes_accessed=2 * n * BLK * BLK * 4, transcendentals=0
        ),
        name="gather_blocks",
    )(row_pick, col_pick, density)


def round_parts(x, parts):
    rows, cols = x.shape
    wide = cols // parts
    bm = min(256, rows)
    steps = rows // bm

    def kernel(x_ref, *rest):
        outs, (raw_ref, low_ref, in_sems, out_sems) = rest[:parts], rest[parts:]

        def read(g):
            return pltpu.make_async_copy(
                x_ref.at[pl.ds(g * bm, bm)], raw_ref.at[g], in_sems.at[g]
            )

        def write(g, p):
            return pltpu.make_async_copy(
                low_ref.at[g, :, pl.ds(p * wide, wide)],
                outs[p].at[pl.ds(g * bm, bm)],
                out_sems.at[g, p],
            )

        for g in range(min(AHEAD, steps)):
            read(g).start()
        for g in range(steps):
            read(g).wait()
            if g + AHEAD < steps:
                read(g + AHEAD).start()
            low_ref[g] = raw_ref[g].astype(BF16)
            for p in range(parts):
                write(g, p).start()
        for g in range(steps):
            for p in range(parts):
                write(g, p).wait()

    return pl.pallas_call(
        kernel,
        grid=(1,),
        in_specs=[pl.BlockSpec(memory_space=pltpu.HBM)],
        out_specs=[pl.BlockSpec(memory_space=pltpu.HBM)] * parts,
        scratch_shapes=[
            pltpu.VMEM((steps, bm, cols), F32),
            pltpu.VMEM((steps, bm, cols), BF16),
            pltpu.SemaphoreType.DMA((steps,)),
            pltpu.SemaphoreType.DMA((steps, parts)),
        ],
        out_shape=[jax.ShapeDtypeStruct((rows, wide), BF16)] * parts,
        compiler_params=pltpu.CompilerParams(vmem_limit_bytes=60 * MIB),
        cost_estimate=pl.CostEstimate(
            flops=rows * cols, bytes_accessed=rows * cols * 6, transcendentals=0
        ),
        name="round_parts",
    )(x)


def update_blocks(low, h_blocks, arriving, picks):
    parts, wide = len(low), low[0].shape[1]
    n = arriving.shape[0]
    row_pick, col_pick, present = picks
    order = jnp.arange(n, dtype=jnp.int32)
    same = (
        (row_pick[:, None] == row_pick[None, :])
        & (col_pick[:, None] == col_pick[None, :])
        & (present[:, None] * present[None, :] > 0)
    )
    leader = jnp.min(jnp.where(same, order[None, :], n), axis=1)

    def kernel(row_ref, col_ref, lead_ref, in_ref, h_ref, *rest):
        outs, (work_ref, low_ref, sems) = rest[parts : 2 * parts], rest[2 * parts :]

        def add(s, carry):
            first = lead_ref[s]

            @pl.when(first == s)
            def _():
                work_ref[s] = h_ref[s] + in_ref[s].astype(F32)

            @pl.when(first < s)
            def _():
                work_ref[first] = work_ref[first] + in_ref[s].astype(F32)

            return carry

        def write(s, carry):
            @pl.when(lead_ref[s] == s)
            def _():
                low_ref[s] = work_ref[s].astype(BF16)
                top = pl.ds(pl.multiple_of(row_ref[s] * BLK, BLK), BLK)
                column = col_ref[s] * BLK
                for p in range(parts):

                    @pl.when((column >= p * wide) & (column < (p + 1) * wide))
                    def _(p=p):
                        left = pl.ds(pl.multiple_of(column - p * wide, BLK), BLK)
                        pltpu.make_async_copy(
                            low_ref.at[s], outs[p].at[top, left], sems.at[s]
                        ).start()

            return carry

        def wait(s, carry):
            @pl.when(lead_ref[s] == s)
            def _():
                pltpu.make_async_copy(
                    low_ref.at[s], outs[0].at[pl.ds(0, BLK), pl.ds(0, BLK)], sems.at[s]
                ).wait()

            return carry

        lax.fori_loop(0, n, add, 0)
        lax.fori_loop(0, n, write, 0)
        lax.fori_loop(0, n, wait, 0)

    whole = pl.BlockSpec((n, BLK, BLK), lambda i, *_: (0, 0, 0))
    return pl.pallas_call(
        kernel,
        grid_spec=pltpu.PrefetchScalarGridSpec(
            num_scalar_prefetch=3,
            grid=(1,),
            in_specs=[whole, whole] + [pl.BlockSpec(memory_space=pltpu.HBM)] * parts,
            out_specs=[pl.BlockSpec(memory_space=pltpu.HBM)] * parts,
            scratch_shapes=[
                pltpu.VMEM((n, BLK, BLK), F32),
                pltpu.VMEM((n, BLK, BLK), BF16),
                pltpu.SemaphoreType.DMA((n,)),
            ],
        ),
        out_shape=[jax.ShapeDtypeStruct(x.shape, x.dtype) for x in low],
        input_output_aliases={5 + p: p for p in range(parts)},
        compiler_params=pltpu.CompilerParams(vmem_limit_bytes=60 * MIB),
        cost_estimate=pl.CostEstimate(
            flops=n * BLK * BLK, bytes_accessed=n * BLK * BLK * 8, transcendentals=0
        ),
        name="update_blocks",
    )(row_pick, col_pick, leader, arriving, h_blocks, *low)


def split(x):
    hi = x.astype(BF16)
    return hi, (x - hi.astype(F32)).astype(BF16)


def basis_kernel(count_ref, phi_ref, hi_ref, lo_ref, hit_ref, lot_ref):
    basis = phi_ref[0]
    column = lax.broadcasted_iota(jnp.int32, basis.shape, 1)
    masked = jnp.where(column < count_ref[pl.program_id(0)] * BLK, basis, 0.0)
    hi, lo = split(masked)
    hi_ref[0] = hi
    lo_ref[0] = lo
    hit_ref[0] = hi.T
    lot_ref[0] = lo.T


def split_basis(phi, counts):
    tdev, npts, local = phi.shape
    spec = pl.BlockSpec((1, npts, local), lambda t, *_: (t, 0, 0))
    spec_t = pl.BlockSpec((1, local, npts), lambda t, *_: (t, 0, 0))
    return pl.pallas_call(
        basis_kernel,
        grid_spec=pltpu.PrefetchScalarGridSpec(
            num_scalar_prefetch=1,
            grid=(tdev,),
            in_specs=[spec],
            out_specs=[spec, spec, spec_t, spec_t],
        ),
        out_shape=[jax.ShapeDtypeStruct((tdev, npts, local), BF16)] * 2
        + [jax.ShapeDtypeStruct((tdev, local, npts), BF16)] * 2,
        compiler_params=pltpu.CompilerParams(vmem_limit_bytes=24 * MIB),
        cost_estimate=pl.CostEstimate(
            flops=4 * phi.size, bytes_accessed=12 * phi.size, transcendentals=0
        ),
        name="split_basis",
    )(counts, phi)


def mm(x, y):
    return jnp.dot(x, y, preferred_element_type=F32)


def tile_kernel(
    hold_ref,
    count_ref,
    in_ref,
    hi_ref,
    lo_ref,
    hit_ref,
    lot_ref,
    v_ref,
    out_ref,
    dh_ref,
    dl_ref,
):
    t = pl.program_id(0)
    maxb = hi_ref.shape[2] // BLK
    for i in range(maxb):
        for j in range(maxb):
            blk = in_ref[hold_ref[t, i * maxb + j]].astype(F32) * (1.0 / DM_SCALE)
            hi, lo = split(blk)
            dh_ref[i * BLK : (i + 1) * BLK, j * BLK : (j + 1) * BLK] = hi
            dl_ref[i * BLK : (i + 1) * BLK, j * BLK : (j + 1) * BLK] = lo
    count = count_ref[t]
    mh, ml = hi_ref[0], lo_ref[0]
    dh, dl = dh_ref[...], dl_ref[...]
    spread = mm(mh, dh) + (mm(ml, dh) + mm(mh, dl))
    masked = mh.astype(F32) + ml.astype(F32)
    rho = jnp.sum(spread * masked, axis=1, keepdims=True)
    potential = v_ref[0] + rho + cube_coef * rho * rho * rho
    wh, wl = split(masked * (potential * cell_volume))
    mht, mlt = hit_ref[0], lot_ref[0]
    ham = (mm(mht, wh) + (mm(mlt, wh) + mm(mht, wl))).astype(BF16)
    for i in range(maxb):
        for j in range(maxb):

            @pl.when((i < count) & (j < count))
            def _():
                out_ref[hold_ref[t, i * maxb + j]] = ham[
                    i * BLK : (i + 1) * BLK, j * BLK : (j + 1) * BLK
                ]


def tile_ham(incoming, basis, v_column, hold, counts):
    n = incoming.shape[0]
    tdev, npts, local = basis[0].shape
    flops = tdev * 3 * 2 * 2 * npts * local * local
    spec = pl.BlockSpec((1, npts, local), lambda t, *_: (t, 0, 0))
    spec_t = pl.BlockSpec((1, local, npts), lambda t, *_: (t, 0, 0))
    return pl.pallas_call(
        tile_kernel,
        grid_spec=pltpu.PrefetchScalarGridSpec(
            num_scalar_prefetch=2,
            grid=(tdev,),
            in_specs=[
                pl.BlockSpec((n, BLK, BLK), lambda t, *_: (0, 0, 0)),
                spec,
                spec,
                spec_t,
                spec_t,
                pl.BlockSpec((1, npts, 1), lambda t, *_: (t, 0, 0)),
            ],
            out_specs=pl.BlockSpec((n, BLK, BLK), lambda t, *_: (0, 0, 0)),
            scratch_shapes=[
                pltpu.VMEM((local, local), BF16),
                pltpu.VMEM((local, local), BF16),
            ],
        ),
        out_shape=jax.ShapeDtypeStruct((n, BLK, BLK), BF16),
        compiler_params=pltpu.CompilerParams(vmem_limit_bytes=34 * MIB),
        cost_estimate=pl.CostEstimate(
            flops=flops, bytes_accessed=tdev * npts * local * 8, transcendentals=0
        ),
        name="tile_ham",
    )(hold, counts, incoming, *basis, v_column)


def assemble(h_core, arriving, picks, dtype, first, parts, wide):
    rows, cols = h_core.shape[0], parts * wide
    n = arriving.shape[0]
    per = 2
    bm = per * BLK
    steps = rows // bm
    narrow = dtype != F32

    def kernel(row_ref, col_ref, present_ref, in_ref, h_ref, *rest):
        outs, rest = rest[:parts], rest[parts:]
        work_ref, in_sems, out_sems, num_ref, list_ref = rest[:5]
        low_refs = rest[5:] if narrow else (work_ref,)

        def band(g):
            return pl.ds(g * bm, bm)

        def read(g):
            return pltpu.make_async_copy(
                h_ref.at[band(g), pl.ds(first, cols)], work_ref.at[band(g)], in_sems.at[g]
            )

        def write(g, p):
            return pltpu.make_async_copy(
                low_refs[p].at[band(g)], outs[p].at[band(g)], out_sems.at[g, p]
            )

        for g in range(min(AHEAD, steps)):
            read(g).start()
        for g in range(steps):
            num_ref[g] = 0

        def note(s, carry):
            c = col_ref[s] * BLK

            @pl.when((present_ref[s] > 0) & (c >= first) & (c < first + cols))
            def _():
                g = row_ref[s] // per
                k = num_ref[g]
                list_ref[g * n + k] = s
                num_ref[g] = k + 1

            return carry

        lax.fori_loop(0, n, note, 0)

        for g in range(steps):
            read(g).wait()
            if g + AHEAD < steps:
                read(g + AHEAD).start()

            def add(k, carry, g=g):
                s = list_ref[g * n + k]
                top = pl.ds(pl.multiple_of(row_ref[s] * BLK, BLK), BLK)
                left = pl.ds(pl.multiple_of(col_ref[s] * BLK - first, BLK), BLK)
                work_ref[top, left] = work_ref[top, left] + in_ref[s].astype(F32)
                return carry

            lax.fori_loop(0, num_ref[g], add, 0)
            for p in range(parts):
                if narrow:
                    low_refs[p][band(g), :] = work_ref[band(g), p * wide : (p + 1) * wide].astype(
                        dtype
                    )
                write(g, p).start()
        for g in range(steps):
            for p in range(parts):
                write(g, p).wait()

    scratch = [
        pltpu.VMEM((rows, cols), F32),
        pltpu.SemaphoreType.DMA((steps,)),
        pltpu.SemaphoreType.DMA((steps, parts)),
        pltpu.SMEM((steps,), jnp.int32),
        pltpu.SMEM((steps * n,), jnp.int32),
    ]
    if narrow:
        scratch.extend([pltpu.VMEM((rows, wide), dtype)] * parts)
    return pl.pallas_call(
        kernel,
        grid_spec=pltpu.PrefetchScalarGridSpec(
            num_scalar_prefetch=3,
            grid=(1,),
            in_specs=[
                pl.BlockSpec((n, BLK, BLK), lambda i, *_: (0, 0, 0)),
                pl.BlockSpec(memory_space=pl.ANY),
            ],
            out_specs=[pl.BlockSpec(memory_space=pl.ANY)] * parts,
            scratch_shapes=scratch,
        ),
        out_shape=[jax.ShapeDtypeStruct((rows, wide), dtype)] * parts,
        compiler_params=pltpu.CompilerParams(vmem_limit_bytes=60 * MIB),
        cost_estimate=pl.CostEstimate(
            flops=rows * cols, bytes_accessed=rows * cols * 6, transcendentals=0
        ),
        name="assemble",
    )(*picks, arriving, h_core)


def product(cols, dm_panel, pieces):
    ncol, rows, width = dm_panel.shape
    depth = pieces[0][0][0][0].shape[0]
    per = depth // width
    bm = min(512, rows)
    npiece = len(pieces)
    nh = sum(len(arrays) for c, _, _ in pieces for arrays in c)
    scalars = jnp.stack(
        [jnp.asarray(s, jnp.int32) for _, _, s in pieces]
        + [jnp.asarray(w, jnp.int32) for _, w, _ in pieces]
    )

    def kernel(sc_ref, *refs):
        h_refs = refs[:nh]
        d_refs = refs[nh : nh + npiece]
        out_ref = refs[nh + npiece]
        held = refs[nh + npiece + 1 : -1]
        sems = refs[-1]

        @pl.when(pl.program_id(0) == 0)
        def _():
            at = 0
            for p, (candidates, _, _) in enumerate(pieces):
                for q, arrays in enumerate(candidates):
                    mine = h_refs[at : at + len(arrays)]
                    at += len(arrays)

                    @pl.when(sc_ref[npiece + p] == q)
                    def _(p=p, mine=mine):
                        left = 0
                        for ref in mine:
                            right = left + ref.shape[1]
                            pltpu.make_async_copy(
                                ref, held[p].at[:, left:right], sems.at[p]
                            ).start()
                            left = right

            for p in range(npiece):
                pltpu.make_async_copy(held[p], held[p], sems.at[p]).wait()

        acc = None
        for p in range(npiece):
            for q in range(per):
                term = mm(d_refs[p][q], held[p][q * width : (q + 1) * width, :])
                acc = term if acc is None else acc + term
        out_ref[...] = acc

    def d_map(p):
        return lambda i, sc: (sc[p], i, 0)

    return pl.pallas_call(
        kernel,
        grid_spec=pltpu.PrefetchScalarGridSpec(
            num_scalar_prefetch=1,
            grid=(rows // bm,),
            in_specs=[pl.BlockSpec(memory_space=pl.ANY)] * nh
            + [pl.BlockSpec((per, bm, width), d_map(p)) for p in range(npiece)],
            out_specs=pl.BlockSpec((bm, cols), lambda i, sc: (i, 0)),
            scratch_shapes=[pltpu.VMEM((depth, cols), BF16)] * npiece
            + [pltpu.SemaphoreType.DMA((npiece,))],
        ),
        out_shape=jax.ShapeDtypeStruct((rows, cols), F32),
        compiler_params=pltpu.CompilerParams(vmem_limit_bytes=60 * MIB),
        cost_estimate=pl.CostEstimate(
            flops=2 * npiece * rows * depth * cols,
            bytes_accessed=npiece * (rows + cols) * depth * 2 + rows * cols * 4,
            transcendentals=0,
        ),
        name="product",
    )(scalars, *[x for c, _, _ in pieces for arrays in c for x in arrays], *[dm_panel] * npiece)


def product_add(total, part, dm_panel, candidates, which, shard):
    ncol, rows, width = dm_panel.shape
    depth, wide = candidates[0].shape
    per = depth // width
    bm = min(512, rows)
    steps = rows // bm
    nh = len(candidates)
    scalars = jnp.stack([jnp.asarray(which, jnp.int32), jnp.asarray(shard, jnp.int32)])

    def kernel(sc_ref, *refs):
        h_refs = refs[:nh]
        dm_ref, total_ref, out_ref, held, d_ref, c_ref, h_sem, d_sems, c_sems, o_sems = refs[nh:]
        columns = pl.ds(part * wide, wide)

        def read_d(i, q):
            return pltpu.make_async_copy(
                dm_ref.at[sc_ref[1] * per + q, pl.ds(i * bm, bm)],
                d_ref.at[i, :, pl.ds(q * width, width)],
                d_sems.at[i, q],
            )

        def read_c(i):
            return pltpu.make_async_copy(
                total_ref.at[pl.ds(i * bm, bm), columns], c_ref.at[i], c_sems.at[i]
            )

        def write(i):
            return pltpu.make_async_copy(
                c_ref.at[i], out_ref.at[pl.ds(i * bm, bm), columns], o_sems.at[i]
            )

        for k in range(nh):

            @pl.when(sc_ref[0] == k)
            def _(k=k):
                pltpu.make_async_copy(h_refs[k], held, h_sem.at[0]).start()

        def start(i):
            for q in range(per):
                read_d(i, q).start()
            read_c(i).start()

        for i in range(min(2, steps)):
            start(i)
        pltpu.make_async_copy(h_refs[0], held, h_sem.at[0]).wait()
        for i in range(steps):
            for q in range(per):
                read_d(i, q).wait()
            read_c(i).wait()
            if i + 2 < steps:
                start(i + 2)
            c_ref[i] = c_ref[i] + mm(d_ref[i], held[...])
            write(i).start()
        for i in range(steps):
            write(i).wait()

    return pl.pallas_call(
        kernel,
        grid_spec=pltpu.PrefetchScalarGridSpec(
            num_scalar_prefetch=1,
            grid=(1,),
            in_specs=[pl.BlockSpec(memory_space=pl.ANY)] * (nh + 2),
            out_specs=pl.BlockSpec(memory_space=pl.ANY),
            scratch_shapes=[
                pltpu.VMEM((depth, wide), BF16),
                pltpu.VMEM((steps, bm, depth), BF16),
                pltpu.VMEM((steps, bm, wide), F32),
                pltpu.SemaphoreType.DMA((1,)),
                pltpu.SemaphoreType.DMA((steps, per)),
                pltpu.SemaphoreType.DMA((steps,)),
                pltpu.SemaphoreType.DMA((steps,)),
            ],
        ),
        out_shape=jax.ShapeDtypeStruct(total.shape, F32),
        input_output_aliases={2 + nh: 0},
        compiler_params=pltpu.CompilerParams(vmem_limit_bytes=60 * MIB),
        cost_estimate=pl.CostEstimate(
            flops=2 * rows * depth * wide,
            bytes_accessed=(rows + wide) * depth * 2 + rows * wide * 8,
            transcendentals=0,
        ),
        name="product_add",
    )(scalars, *candidates, dm_panel, total)


PARTS = 4


def tie(x, y):
    return lax.optimization_barrier((x, y))


def body(density, h_core, phi, v_ext, tile_blocks, tile_count):
    nrow = lax.axis_size("row")
    ncol = lax.axis_size("col")
    ndev = nrow * ncol
    row_idx = lax.axis_index("row")
    col_idx = lax.axis_index("col")
    myself = row_idx * ncol + col_idx
    rows_loc, cols_loc = density.shape
    rowb = rows_loc // BLK
    colb = cols_loc // BLK
    tdev, npts, local = phi.shape
    maxb = tile_blocks.shape[1]
    line = nrow == 4

    swap = [(0, 1), (1, 0), (2, 3), (3, 2)]
    cross = [(1, 2), (2, 1)]
    outward = [(1, 0), (2, 3)]

    blocks = tile_blocks.reshape(ndev, tdev, maxb)
    counts = tile_count.reshape(ndev, tdev)
    live = jnp.arange(maxb, dtype=jnp.int32)[None, None, :] < counts[:, :, None]
    col_hit = live & (blocks // colb == col_idx)
    col_in = jnp.sum(jnp.where(col_hit, blocks - col_idx * colb, 0), axis=2)

    def picks_of(row):
        row_hit = live & (blocks // rowb == row)
        both = jnp.any(row_hit, axis=2) & jnp.any(col_hit, axis=2)
        row_in = jnp.sum(jnp.where(row_hit, blocks - row * rowb, 0), axis=2)
        row_pick = jnp.sum(jnp.where(both, row_in, 0), axis=1)
        col_pick = jnp.sum(jnp.where(both, col_in, 0), axis=1)
        return row_pick, col_pick, jnp.any(both, axis=1).astype(jnp.int32)

    picks = picks_of(row_idx)
    mine = lax.dynamic_index_in_dim(blocks, myself, 0, keepdims=False)
    my_counts = lax.dynamic_index_in_dim(counts, myself, 0, keepdims=False)
    hold = ((mine // rowb)[:, :, None] * ncol + (mine // colb)[:, None, :]).reshape(tdev, -1)

    outgoing = (gather_blocks(density, picks[0], picks[1]) * DM_SCALE).astype(jnp.float16)
    incoming = lax.all_to_all(outgoing, ("row", "col"), split_axis=0, concat_axis=0, tiled=True)
    basis = split_basis(phi, my_counts)
    (dm_low,) = round_parts(density, 1)
    v_column = v_ext[:, :, None]
    incoming, (dm_low, basis, v_column) = tie(incoming, (dm_low, basis, v_column))
    dm_panel = lax.all_gather(dm_low, "col", axis=0, tiled=False)

    returning = tile_ham(incoming.astype(F32), basis, v_column, hold, my_counts)
    arriving = lax.all_to_all(returning, ("row", "col"), split_axis=0, concat_axis=0, tiled=True)
    parts = PARTS if line and cols_loc % (PARTS * BLK) == 0 else 1
    wide = cols_loc // parts
    low = round_parts(h_core, parts)
    h_blocks = gather_blocks(h_core, picks[0], picks[1])
    arriving, (low, h_blocks) = tie(arriving, (low, h_blocks))
    low = update_blocks(low, h_blocks, arriving, picks)
    (hamiltonian,) = assemble(h_core, arriving, picks, F32, 0, 1, cols_loc)

    if line:
        pair_idx = row_idx + 1 - 2 * (row_idx % 2)
        is_low = row_idx < 2
        is_end = ((row_idx == 0) | (row_idx == 3)).astype(jnp.int32)
        near_idx = jnp.where(is_low, 2, 1)
        far_idx = jnp.where(is_low, 3, 0)
        pair, near_mid = [], []
        for p in range(parts):
            ready = low[p] if p < 2 else tie(low[p], near_mid[p - 2])[0]
            pair.append(lax.ppermute(ready, "row", swap))
            near_mid.append(lax.ppermute(ready, "row", cross))
        near_end = [lax.ppermute(x, "row", outward) for x in near_mid]
        far_mid = []
        for p in range(parts):
            ready = pair[p]
            if p > 0:
                ready, near_end[p - 1] = tie(ready, near_end[p - 1])
            far_mid.append(lax.ppermute(ready, "row", cross))
        far_end = []
        for p in range(parts):
            ready = far_mid[p]
            if p == parts - 1:
                ready, near_end[p] = tie(ready, near_end[p])
            far_end.append(lax.ppermute(ready, "row", outward))
        total = product(
            cols_loc,
            dm_panel,
            [
                ((low,), 0, row_idx),
                ((pair,), 0, pair_idx),
                ((near_mid, near_end), is_end, near_idx),
            ],
        )
        for p in range(parts):
            total = product_add(
                total, p, dm_panel, (far_mid[p], far_end[p]), is_end, far_idx
            )
    else:
        ham_panel = lax.all_gather(low[0], "row", axis=0, tiled=False)
        total = product(cols_loc, dm_panel, [(((ham_panel[0],),), 0, 0)])
        for k in range(1, nrow):
            total = product_add(total, 0, dm_panel, (ham_panel[k],), 0, k)
    return hamiltonian, total


def solution(mesh):
    placed = (
        P("row", "col"),
        P("row", "col"),
        P(("row", "col"), None, None),
        P(("row", "col"), None),
        P(),
        P(),
    )
    return jax.shard_map(
        body,
        mesh=mesh,
        in_specs=placed,
        out_specs=(P("row", "col"), P("row", "col")),
        check_vma=False,
    )
```

```python
import jax
import jax.numpy as jnp
from jax import lax
from jax.experimental import pallas as pl
from jax.experimental.pallas import tpu as pltpu
from jax.sharding import PartitionSpec as P

BLK = 128

cube_coef = 0.5
cell_volume = 0.03125
DM_SCALE = float(2**20)

F32 = jnp.float32
BF16 = jnp.bfloat16
MIB = 1 << 20
AHEAD = 3


def gather_kernel(row_ref, col_ref, dens_ref, out_ref, sems):
    n = out_ref.shape[0]

    def copy(s):
        r = pl.multiple_of(row_ref[s] * BLK, BLK)
        c = pl.multiple_of(col_ref[s] * BLK, BLK)
        return pltpu.make_async_copy(
            dens_ref.at[pl.ds(r, BLK), pl.ds(c, BLK)], out_ref.at[s], sems.at[s]
        )

    def start(s, carry):
        copy(s).start()
        return carry

    def wait(s, carry):
        copy(s).wait()
        return carry

    lax.fori_loop(0, n, start, 0)
    lax.fori_loop(0, n, wait, 0)


def gather_blocks(density, row_pick, col_pick):
    n = row_pick.shape[0]
    return pl.pallas_call(
        gather_kernel,
        grid_spec=pltpu.PrefetchScalarGridSpec(
            num_scalar_prefetch=2,
            grid=(1,),
            in_specs=[pl.BlockSpec(memory_space=pltpu.HBM)],
            out_specs=pl.BlockSpec((n, BLK, BLK), lambda i, *_: (0, 0, 0)),
            scratch_shapes=[pltpu.SemaphoreType.DMA((n,))],
        ),
        out_shape=jax.ShapeDtypeStruct((n, BLK, BLK), F32),
        compiler_params=pltpu.CompilerParams(vmem_limit_bytes=57 * MIB),
        cost_estimate=pl.CostEstimate(
            flops=0, bytes_accessed=2 * n * BLK * BLK * 4, transcendentals=0
        ),
        name="gather_blocks",
    )(row_pick, col_pick, density)


def round_parts(x, parts):
    rows, cols = x.shape
    wide = cols // parts
    bm = min(256, rows)
    steps = rows // bm

    def kernel(x_ref, *rest):
        outs, (raw_ref, low_ref, in_sems, out_sems) = rest[:parts], rest[parts:]

        def read(g):
            return pltpu.make_async_copy(
                x_ref.at[pl.ds(g * bm, bm)], raw_ref.at[g], in_sems.at[g]
            )

        def write(g, p):
            return pltpu.make_async_copy(
                low_ref.at[g, :, pl.ds(p * wide, wide)],
                outs[p].at[pl.ds(g * bm, bm)],
                out_sems.at[g, p],
            )

        for g in range(min(AHEAD, steps)):
            read(g).start()
        for g in range(steps):
            read(g).wait()
            if g + AHEAD < steps:
                read(g + AHEAD).start()
            low_ref[g] = raw_ref[g].astype(BF16)
            for p in range(parts):
                write(g, p).start()
        for g in range(steps):
            for p in range(parts):
                write(g, p).wait()

    return pl.pallas_call(
        kernel,
        grid=(1,),
        in_specs=[pl.BlockSpec(memory_space=pltpu.HBM)],
        out_specs=[pl.BlockSpec(memory_space=pltpu.HBM)] * parts,
        scratch_shapes=[
            pltpu.VMEM((steps, bm, cols), F32),
            pltpu.VMEM((steps, bm, cols), BF16),
            pltpu.SemaphoreType.DMA((steps,)),
            pltpu.SemaphoreType.DMA((steps, parts)),
        ],
        out_shape=[jax.ShapeDtypeStruct((rows, wide), BF16)] * parts,
        compiler_params=pltpu.CompilerParams(vmem_limit_bytes=60 * MIB),
        cost_estimate=pl.CostEstimate(
            flops=rows * cols, bytes_accessed=rows * cols * 6, transcendentals=0
        ),
        name="round_parts",
    )(x)


def update_blocks(low, h_blocks, arriving, picks):
    parts, wide = len(low), low[0].shape[1]
    n = arriving.shape[0]
    row_pick, col_pick, present = picks
    order = jnp.arange(n, dtype=jnp.int32)
    same = (
        (row_pick[:, None] == row_pick[None, :])
        & (col_pick[:, None] == col_pick[None, :])
        & (present[:, None] * present[None, :] > 0)
    )
    leader = jnp.min(jnp.where(same, order[None, :], n), axis=1)

    def kernel(row_ref, col_ref, lead_ref, in_ref, h_ref, *rest):
        outs, (work_ref, low_ref, sems) = rest[parts : 2 * parts], rest[2 * parts :]

        def add(s, carry):
            first = lead_ref[s]

            @pl.when(first == s)
            def _():
                work_ref[s] = h_ref[s] + in_ref[s].astype(F32)

            @pl.when(first < s)
            def _():
                work_ref[first] = work_ref[first] + in_ref[s].astype(F32)

            return carry

        def write(s, carry):
            @pl.when(lead_ref[s] == s)
            def _():
                low_ref[s] = work_ref[s].astype(BF16)
                top = pl.ds(pl.multiple_of(row_ref[s] * BLK, BLK), BLK)
                column = col_ref[s] * BLK
                for p in range(parts):

                    @pl.when((column >= p * wide) & (column < (p + 1) * wide))
                    def _(p=p):
                        left = pl.ds(pl.multiple_of(column - p * wide, BLK), BLK)
                        pltpu.make_async_copy(
                            low_ref.at[s], outs[p].at[top, left], sems.at[s]
                        ).start()

            return carry

        def wait(s, carry):
            @pl.when(lead_ref[s] == s)
            def _():
                pltpu.make_async_copy(
                    low_ref.at[s], outs[0].at[pl.ds(0, BLK), pl.ds(0, BLK)], sems.at[s]
                ).wait()

            return carry

        lax.fori_loop(0, n, add, 0)
        lax.fori_loop(0, n, write, 0)
        lax.fori_loop(0, n, wait, 0)

    whole = pl.BlockSpec((n, BLK, BLK), lambda i, *_: (0, 0, 0))
    return pl.pallas_call(
        kernel,
        grid_spec=pltpu.PrefetchScalarGridSpec(
            num_scalar_prefetch=3,
            grid=(1,),
            in_specs=[whole, whole] + [pl.BlockSpec(memory_space=pltpu.HBM)] * parts,
            out_specs=[pl.BlockSpec(memory_space=pltpu.HBM)] * parts,
            scratch_shapes=[
                pltpu.VMEM((n, BLK, BLK), F32),
                pltpu.VMEM((n, BLK, BLK), BF16),
                pltpu.SemaphoreType.DMA((n,)),
            ],
        ),
        out_shape=[jax.ShapeDtypeStruct(x.shape, x.dtype) for x in low],
        input_output_aliases={5 + p: p for p in range(parts)},
        compiler_params=pltpu.CompilerParams(vmem_limit_bytes=60 * MIB),
        cost_estimate=pl.CostEstimate(
            flops=n * BLK * BLK, bytes_accessed=n * BLK * BLK * 8, transcendentals=0
        ),
        name="update_blocks",
    )(row_pick, col_pick, leader, arriving, h_blocks, *low)


def split(x):
    hi = x.astype(BF16)
    return hi, (x - hi.astype(F32)).astype(BF16)


def basis_kernel(count_ref, phi_ref, hi_ref, lo_ref, hit_ref, lot_ref):
    basis = phi_ref[0]
    column = lax.broadcasted_iota(jnp.int32, basis.shape, 1)
    masked = jnp.where(column < count_ref[pl.program_id(0)] * BLK, basis, 0.0)
    hi, lo = split(masked)
    hi_ref[0] = hi
    lo_ref[0] = lo
    hit_ref[0] = hi.T
    lot_ref[0] = lo.T


def split_basis(phi, counts):
    tdev, npts, local = phi.shape
    spec = pl.BlockSpec((1, npts, local), lambda t, *_: (t, 0, 0))
    spec_t = pl.BlockSpec((1, local, npts), lambda t, *_: (t, 0, 0))
    return pl.pallas_call(
        basis_kernel,
        grid_spec=pltpu.PrefetchScalarGridSpec(
            num_scalar_prefetch=1,
            grid=(tdev,),
            in_specs=[spec],
            out_specs=[spec, spec, spec_t, spec_t],
        ),
        out_shape=[jax.ShapeDtypeStruct((tdev, npts, local), BF16)] * 2
        + [jax.ShapeDtypeStruct((tdev, local, npts), BF16)] * 2,
        compiler_params=pltpu.CompilerParams(vmem_limit_bytes=60 * MIB),
        cost_estimate=pl.CostEstimate(
            flops=4 * phi.size, bytes_accessed=12 * phi.size, transcendentals=0
        ),
        name="split_basis",
    )(counts, phi)


def mm(x, y):
    return jnp.dot(x, y, preferred_element_type=F32)


def tile_kernel(
    hold_ref,
    count_ref,
    in_ref,
    hi_ref,
    lo_ref,
    v_ref,
    hit_ref,
    lot_ref,
    out_ref,
    dh_ref,
    dl_ref,
    mht_ref,
    mlt_ref,
    sems,
):
    t = pl.program_id(0)

    def fetch(k):
        return (
            pltpu.make_async_copy(hit_ref.at[k], mht_ref.at[k], sems.at[0, k]),
            pltpu.make_async_copy(lot_ref.at[k], mlt_ref.at[k], sems.at[1, k]),
        )

    @pl.when(t == 0)
    def _():
        for k in range(mht_ref.shape[0]):
            for copy in fetch(k):
                copy.start()

    maxb = hi_ref.shape[2] // BLK
    for i in range(maxb):
        for j in range(maxb):
            blk = in_ref[hold_ref[t, i * maxb + j]].astype(F32) * (1.0 / DM_SCALE)
            hi, lo = split(blk)
            dh_ref[i * BLK : (i + 1) * BLK, j * BLK : (j + 1) * BLK] = hi
            dl_ref[i * BLK : (i + 1) * BLK, j * BLK : (j + 1) * BLK] = lo
    count = count_ref[t]
    mh, ml = hi_ref[0], lo_ref[0]
    dh, dl = dh_ref[...], dl_ref[...]
    spread = mm(mh, dh) + (mm(ml, dh) + mm(mh, dl))
    masked = mh.astype(F32) + ml.astype(F32)
    rho = jnp.sum(spread * masked, axis=1, keepdims=True)
    potential = v_ref[0] + rho + cube_coef * rho * rho * rho
    wh, wl = split(masked * (potential * cell_volume))
    for copy in fetch(t):
        copy.wait()
    mht, mlt = mht_ref[t], mlt_ref[t]
    ham = (mm(mht, wh) + (mm(mlt, wh) + mm(mht, wl))).astype(BF16)
    for i in range(maxb):
        for j in range(maxb):

            @pl.when((i < count) & (j < count))
            def _():
                out_ref[hold_ref[t, i * maxb + j]] = ham[
                    i * BLK : (i + 1) * BLK, j * BLK : (j + 1) * BLK
                ]


def tile_ham(incoming, basis, v_column, hold, counts):
    n = incoming.shape[0]
    tdev, npts, local = basis[0].shape
    flops = tdev * 3 * 2 * 2 * npts * local * local
    spec = pl.BlockSpec((1, npts, local), lambda t, *_: (t, 0, 0))
    return pl.pallas_call(
        tile_kernel,
        grid_spec=pltpu.PrefetchScalarGridSpec(
            num_scalar_prefetch=2,
            grid=(tdev,),
            in_specs=[
                pl.BlockSpec((n, BLK, BLK), lambda t, *_: (0, 0, 0)),
                spec,
                spec,
                pl.BlockSpec((1, npts, 1), lambda t, *_: (t, 0, 0)),
                pl.BlockSpec(memory_space=pltpu.HBM),
                pl.BlockSpec(memory_space=pltpu.HBM),
            ],
            out_specs=pl.BlockSpec((n, BLK, BLK), lambda t, *_: (0, 0, 0)),
            scratch_shapes=[
                pltpu.VMEM((local, local), BF16),
                pltpu.VMEM((local, local), BF16),
                pltpu.VMEM((tdev, local, npts), BF16),
                pltpu.VMEM((tdev, local, npts), BF16),
                pltpu.SemaphoreType.DMA((2, tdev)),
            ],
        ),
        out_shape=jax.ShapeDtypeStruct((n, BLK, BLK), BF16),
        compiler_params=pltpu.CompilerParams(vmem_limit_bytes=60 * MIB),
        cost_estimate=pl.CostEstimate(
            flops=flops, bytes_accessed=tdev * npts * local * 8, transcendentals=0
        ),
        name="tile_ham",
    )(hold, counts, incoming, *basis[:2], v_column, *basis[2:])


def assemble(h_core, arriving, picks, dtype, first, parts, wide):
    rows, cols = h_core.shape[0], parts * wide
    n = arriving.shape[0]
    per = 2
    bm = per * BLK
    steps = rows // bm
    narrow = dtype != F32

    def kernel(row_ref, col_ref, present_ref, in_ref, h_ref, *rest):
        outs, rest = rest[:parts], rest[parts:]
        work_ref, in_sems, out_sems, num_ref, list_ref = rest[:5]
        low_refs = rest[5:] if narrow else (work_ref,)

        def band(g):
            return pl.ds(g * bm, bm)

        def read(g):
            return pltpu.make_async_copy(
                h_ref.at[band(g), pl.ds(first, cols)], work_ref.at[band(g)], in_sems.at[g]
            )

        def write(g, p):
            return pltpu.make_async_copy(
                low_refs[p].at[band(g)], outs[p].at[band(g)], out_sems.at[g, p]
            )

        for g in range(min(AHEAD, steps)):
            read(g).start()
        for g in range(steps):
            num_ref[g] = 0

        def note(s, carry):
            c = col_ref[s] * BLK

            @pl.when((present_ref[s] > 0) & (c >= first) & (c < first + cols))
            def _():
                g = row_ref[s] // per
                k = num_ref[g]
                list_ref[g * n + k] = s
                num_ref[g] = k + 1

            return carry

        lax.fori_loop(0, n, note, 0)

        for g in range(steps):
            read(g).wait()
            if g + AHEAD < steps:
                read(g + AHEAD).start()

            def add(k, carry, g=g):
                s = list_ref[g * n + k]
                top = pl.ds(pl.multiple_of(row_ref[s] * BLK, BLK), BLK)
                left = pl.ds(pl.multiple_of(col_ref[s] * BLK - first, BLK), BLK)
                work_ref[top, left] = work_ref[top, left] + in_ref[s].astype(F32)
                return carry

            lax.fori_loop(0, num_ref[g], add, 0)
            for p in range(parts):
                if narrow:
                    low_refs[p][band(g), :] = work_ref[band(g), p * wide : (p + 1) * wide].astype(
                        dtype
                    )
                write(g, p).start()
        for g in range(steps):
            for p in range(parts):
                write(g, p).wait()

    scratch = [
        pltpu.VMEM((rows, cols), F32),
        pltpu.SemaphoreType.DMA((steps,)),
        pltpu.SemaphoreType.DMA((steps, parts)),
        pltpu.SMEM((steps,), jnp.int32),
        pltpu.SMEM((steps * n,), jnp.int32),
    ]
    if narrow:
        scratch.extend([pltpu.VMEM((rows, wide), dtype)] * parts)
    return pl.pallas_call(
        kernel,
        grid_spec=pltpu.PrefetchScalarGridSpec(
            num_scalar_prefetch=3,
            grid=(1,),
            in_specs=[
                pl.BlockSpec((n, BLK, BLK), lambda i, *_: (0, 0, 0)),
                pl.BlockSpec(memory_space=pl.ANY),
            ],
            out_specs=[pl.BlockSpec(memory_space=pl.ANY)] * parts,
            scratch_shapes=scratch,
        ),
        out_shape=[jax.ShapeDtypeStruct((rows, wide), dtype)] * parts,
        compiler_params=pltpu.CompilerParams(vmem_limit_bytes=60 * MIB),
        cost_estimate=pl.CostEstimate(
            flops=rows * cols, bytes_accessed=rows * cols * 6, transcendentals=0
        ),
        name="assemble",
    )(*picks, arriving, h_core)


def product(cols, dm_panel, pieces):
    ncol, rows, width = dm_panel.shape
    depth = pieces[0][0][0][0].shape[0]
    per = depth // width
    bm = min(512, rows)
    npiece = len(pieces)
    nh = sum(len(arrays) for c, _, _ in pieces for arrays in c)
    scalars = jnp.stack(
        [jnp.asarray(s, jnp.int32) for _, _, s in pieces]
        + [jnp.asarray(w, jnp.int32) for _, w, _ in pieces]
    )

    def kernel(sc_ref, *refs):
        h_refs = refs[:nh]
        d_refs = refs[nh : nh + npiece]
        out_ref = refs[nh + npiece]
        held = refs[nh + npiece + 1 : -1]
        sems = refs[-1]

        @pl.when(pl.program_id(0) == 0)
        def _():
            at = 0
            for p, (candidates, _, _) in enumerate(pieces):
                for q, arrays in enumerate(candidates):
                    mine = h_refs[at : at + len(arrays)]
                    at += len(arrays)

                    @pl.when(sc_ref[npiece + p] == q)
                    def _(p=p, mine=mine):
                        left = 0
                        for ref in mine:
                            right = left + ref.shape[1]
                            pltpu.make_async_copy(
                                ref, held[p].at[:, left:right], sems.at[p]
                            ).start()
                            left = right

            for p in range(npiece):
                pltpu.make_async_copy(held[p], held[p], sems.at[p]).wait()

        acc = None
        for p in range(npiece):
            for q in range(per):
                term = mm(d_refs[p][q], held[p][q * width : (q + 1) * width, :])
                acc = term if acc is None else acc + term
        out_ref[...] = acc

    def d_map(p):
        return lambda i, sc: (sc[p], i, 0)

    return pl.pallas_call(
        kernel,
        grid_spec=pltpu.PrefetchScalarGridSpec(
            num_scalar_prefetch=1,
            grid=(rows // bm,),
            in_specs=[pl.BlockSpec(memory_space=pl.ANY)] * nh
            + [pl.BlockSpec((per, bm, width), d_map(p)) for p in range(npiece)],
            out_specs=pl.BlockSpec((bm, cols), lambda i, sc: (i, 0)),
            scratch_shapes=[pltpu.VMEM((depth, cols), BF16)] * npiece
            + [pltpu.SemaphoreType.DMA((npiece,))],
        ),
        out_shape=jax.ShapeDtypeStruct((rows, cols), F32),
        compiler_params=pltpu.CompilerParams(vmem_limit_bytes=60 * MIB),
        cost_estimate=pl.CostEstimate(
            flops=2 * npiece * rows * depth * cols,
            bytes_accessed=npiece * (rows + cols) * depth * 2 + rows * cols * 4,
            transcendentals=0,
        ),
        name="product",
    )(scalars, *[x for c, _, _ in pieces for arrays in c for x in arrays], *[dm_panel] * npiece)


def product_add(total, part, dm_panel, candidates, which, shard):
    ncol, rows, width = dm_panel.shape
    depth, wide = candidates[0].shape
    per = depth // width
    bm = min(512, rows)
    steps = rows // bm
    nh = len(candidates)
    scalars = jnp.stack([jnp.asarray(which, jnp.int32), jnp.asarray(shard, jnp.int32)])

    def kernel(sc_ref, *refs):
        h_refs = refs[:nh]
        dm_ref, total_ref, out_ref, held, d_ref, c_ref, h_sem, d_sems, c_sems, o_sems = refs[nh:]
        columns = pl.ds(part * wide, wide)

        def read_d(i, q):
            return pltpu.make_async_copy(
                dm_ref.at[sc_ref[1] * per + q, pl.ds(i * bm, bm)],
                d_ref.at[i, :, pl.ds(q * width, width)],
                d_sems.at[i, q],
            )

        def read_c(i):
            return pltpu.make_async_copy(
                total_ref.at[pl.ds(i * bm, bm), columns], c_ref.at[i], c_sems.at[i]
            )

        def write(i):
            return pltpu.make_async_copy(
                c_ref.at[i], out_ref.at[pl.ds(i * bm, bm), columns], o_sems.at[i]
            )

        for k in range(nh):

            @pl.when(sc_ref[0] == k)
            def _(k=k):
                pltpu.make_async_copy(h_refs[k], held, h_sem.at[0]).start()

        def start(i):
            for q in range(per):
                read_d(i, q).start()
            read_c(i).start()

        for i in range(min(2, steps)):
            start(i)
        pltpu.make_async_copy(h_refs[0], held, h_sem.at[0]).wait()
        for i in range(steps):
            for q in range(per):
                read_d(i, q).wait()
            read_c(i).wait()
            if i + 2 < steps:
                start(i + 2)
            c_ref[i] = c_ref[i] + mm(d_ref[i], held[...])
            write(i).start()
        for i in range(steps):
            write(i).wait()

    return pl.pallas_call(
        kernel,
        grid_spec=pltpu.PrefetchScalarGridSpec(
            num_scalar_prefetch=1,
            grid=(1,),
            in_specs=[pl.BlockSpec(memory_space=pl.ANY)] * (nh + 2),
            out_specs=pl.BlockSpec(memory_space=pl.ANY),
            scratch_shapes=[
                pltpu.VMEM((depth, wide), BF16),
                pltpu.VMEM((steps, bm, depth), BF16),
                pltpu.VMEM((steps, bm, wide), F32),
                pltpu.SemaphoreType.DMA((1,)),
                pltpu.SemaphoreType.DMA((steps, per)),
                pltpu.SemaphoreType.DMA((steps,)),
                pltpu.SemaphoreType.DMA((steps,)),
            ],
        ),
        out_shape=jax.ShapeDtypeStruct(total.shape, F32),
        input_output_aliases={2 + nh: 0},
        compiler_params=pltpu.CompilerParams(vmem_limit_bytes=60 * MIB),
        cost_estimate=pl.CostEstimate(
            flops=2 * rows * depth * wide,
            bytes_accessed=(rows + wide) * depth * 2 + rows * wide * 8,
            transcendentals=0,
        ),
        name="product_add",
    )(scalars, *candidates, dm_panel, total)


PARTS = 4


def tie(x, y):
    return lax.optimization_barrier((x, y))


def body(density, h_core, phi, v_ext, tile_blocks, tile_count):
    nrow = lax.axis_size("row")
    ncol = lax.axis_size("col")
    ndev = nrow * ncol
    row_idx = lax.axis_index("row")
    col_idx = lax.axis_index("col")
    myself = row_idx * ncol + col_idx
    rows_loc, cols_loc = density.shape
    rowb = rows_loc // BLK
    colb = cols_loc // BLK
    tdev, npts, local = phi.shape
    maxb = tile_blocks.shape[1]
    line = nrow == 4

    swap = [(0, 1), (1, 0), (2, 3), (3, 2)]
    cross = [(1, 2), (2, 1)]
    outward = [(1, 0), (2, 3)]

    blocks = tile_blocks.reshape(ndev, tdev, maxb)
    counts = tile_count.reshape(ndev, tdev)
    live = jnp.arange(maxb, dtype=jnp.int32)[None, None, :] < counts[:, :, None]
    col_hit = live & (blocks // colb == col_idx)
    col_in = jnp.sum(jnp.where(col_hit, blocks - col_idx * colb, 0), axis=2)

    def picks_of(row):
        row_hit = live & (blocks // rowb == row)
        both = jnp.any(row_hit, axis=2) & jnp.any(col_hit, axis=2)
        row_in = jnp.sum(jnp.where(row_hit, blocks - row * rowb, 0), axis=2)
        row_pick = jnp.sum(jnp.where(both, row_in, 0), axis=1)
        col_pick = jnp.sum(jnp.where(both, col_in, 0), axis=1)
        return row_pick, col_pick, jnp.any(both, axis=1).astype(jnp.int32)

    picks = picks_of(row_idx)
    mine = lax.dynamic_index_in_dim(blocks, myself, 0, keepdims=False)
    my_counts = lax.dynamic_index_in_dim(counts, myself, 0, keepdims=False)
    hold = ((mine // rowb)[:, :, None] * ncol + (mine // colb)[:, None, :]).reshape(tdev, -1)

    outgoing = (gather_blocks(density, picks[0], picks[1]) * DM_SCALE).astype(jnp.float16)
    incoming = lax.all_to_all(outgoing, ("row", "col"), split_axis=0, concat_axis=0, tiled=True)
    basis = split_basis(phi, my_counts)
    (dm_low,) = round_parts(density, 1)
    v_column = v_ext[:, :, None]
    incoming, (dm_low, basis, v_column) = tie(incoming, (dm_low, basis, v_column))
    dm_panel = lax.all_gather(dm_low, "col", axis=0, tiled=False)

    returning = tile_ham(incoming.astype(F32), basis, v_column, hold, my_counts)
    arriving = lax.all_to_all(returning, ("row", "col"), split_axis=0, concat_axis=0, tiled=True)
    parts = PARTS if line and cols_loc % (PARTS * BLK) == 0 else 1
    wide = cols_loc // parts
    low = round_parts(h_core, parts)
    h_blocks = gather_blocks(h_core, picks[0], picks[1])
    arriving, (low, h_blocks) = tie(arriving, (low, h_blocks))
    low = update_blocks(low, h_blocks, arriving, picks)
    (hamiltonian,) = assemble(h_core, arriving, picks, F32, 0, 1, cols_loc)

    if line:
        pair_idx = row_idx + 1 - 2 * (row_idx % 2)
        is_low = row_idx < 2
        is_end = ((row_idx == 0) | (row_idx == 3)).astype(jnp.int32)
        near_idx = jnp.where(is_low, 2, 1)
        far_idx = jnp.where(is_low, 3, 0)
        pair, near_mid = [], []
        for p in range(parts):
            ready = low[p] if p < 2 else tie(low[p], near_mid[p - 2])[0]
            pair.append(lax.ppermute(ready, "row", swap))
            near_mid.append(lax.ppermute(ready, "row", cross))
        near_end = [lax.ppermute(x, "row", outward) for x in near_mid]
        far_mid = []
        for p in range(parts):
            ready = pair[p]
            if p > 0:
                ready, near_end[p - 1] = tie(ready, near_end[p - 1])
            far_mid.append(lax.ppermute(ready, "row", cross))
        far_end = []
        for p in range(parts):
            ready = far_mid[p]
            if p == parts - 1:
                ready, near_end[p] = tie(ready, near_end[p])
            far_end.append(lax.ppermute(ready, "row", outward))
        total = product(
            cols_loc,
            dm_panel,
            [
                ((low,), 0, row_idx),
                ((pair,), 0, pair_idx),
                ((near_mid, near_end), is_end, near_idx),
            ],
        )
        for p in range(parts):
            total = product_add(
                total, p, dm_panel, (far_mid[p], far_end[p]), is_end, far_idx
            )
    else:
        ham_panel = lax.all_gather(low[0], "row", axis=0, tiled=False)
        total = product(cols_loc, dm_panel, [(((ham_panel[0],),), 0, 0)])
        for k in range(1, nrow):
            total = product_add(total, 0, dm_panel, (ham_panel[k],), 0, k)
    return hamiltonian, total


def solution(mesh):
    placed = (
        P("row", "col"),
        P("row", "col"),
        P(("row", "col"), None, None),
        P(("row", "col"), None),
        P(),
        P(),
    )
    return jax.shard_map(
        body,
        mesh=mesh,
        in_specs=placed,
        out_specs=(P("row", "col"), P("row", "col")),
        check_vma=False,
    )
```

```python
import jax
import jax.numpy as jnp
from jax import lax
from jax.experimental import pallas as pl
from jax.experimental.pallas import tpu as pltpu
from jax.sharding import PartitionSpec as P

BLK = 128

cube_coef = 0.5
cell_volume = 0.03125
DM_SCALE = float(2**20)

F32 = jnp.float32
BF16 = jnp.bfloat16
MIB = 1 << 20
AHEAD = 3


def gather_kernel(row_ref, col_ref, dens_ref, out_ref, sems):
    n = out_ref.shape[0]

    def copy(s):
        r = pl.multiple_of(row_ref[s] * BLK, BLK)
        c = pl.multiple_of(col_ref[s] * BLK, BLK)
        return pltpu.make_async_copy(
            dens_ref.at[pl.ds(r, BLK), pl.ds(c, BLK)], out_ref.at[s], sems.at[s]
        )

    def start(s, carry):
        copy(s).start()
        return carry

    def wait(s, carry):
        copy(s).wait()
        return carry

    lax.fori_loop(0, n, start, 0)
    lax.fori_loop(0, n, wait, 0)


def gather_blocks(density, row_pick, col_pick):
    n = row_pick.shape[0]
    return pl.pallas_call(
        gather_kernel,
        grid_spec=pltpu.PrefetchScalarGridSpec(
            num_scalar_prefetch=2,
            grid=(1,),
            in_specs=[pl.BlockSpec(memory_space=pltpu.HBM)],
            out_specs=pl.BlockSpec((n, BLK, BLK), lambda i, *_: (0, 0, 0)),
            scratch_shapes=[pltpu.SemaphoreType.DMA((n,))],
        ),
        out_shape=jax.ShapeDtypeStruct((n, BLK, BLK), F32),
        compiler_params=pltpu.CompilerParams(vmem_limit_bytes=57 * MIB),
        cost_estimate=pl.CostEstimate(
            flops=0, bytes_accessed=2 * n * BLK * BLK * 4, transcendentals=0
        ),
        name="gather_blocks",
    )(row_pick, col_pick, density)


def round_parts(x, parts):
    rows, cols = x.shape
    wide = cols // parts
    bm = min(256, rows)
    steps = rows // bm

    def kernel(x_ref, *rest):
        outs, (raw_ref, low_ref, in_sems, out_sems) = rest[:parts], rest[parts:]

        def read(g):
            return pltpu.make_async_copy(
                x_ref.at[pl.ds(g * bm, bm)], raw_ref.at[g], in_sems.at[g]
            )

        def write(g, p):
            return pltpu.make_async_copy(
                low_ref.at[g, :, pl.ds(p * wide, wide)],
                outs[p].at[pl.ds(g * bm, bm)],
                out_sems.at[g, p],
            )

        for g in range(min(AHEAD, steps)):
            read(g).start()
        for g in range(steps):
            read(g).wait()
            if g + AHEAD < steps:
                read(g + AHEAD).start()
            low_ref[g] = raw_ref[g].astype(BF16)
            for p in range(parts):
                write(g, p).start()
        for g in range(steps):
            for p in range(parts):
                write(g, p).wait()

    return pl.pallas_call(
        kernel,
        grid=(1,),
        in_specs=[pl.BlockSpec(memory_space=pltpu.HBM)],
        out_specs=[pl.BlockSpec(memory_space=pltpu.HBM)] * parts,
        scratch_shapes=[
            pltpu.VMEM((steps, bm, cols), F32),
            pltpu.VMEM((steps, bm, cols), BF16),
            pltpu.SemaphoreType.DMA((steps,)),
            pltpu.SemaphoreType.DMA((steps, parts)),
        ],
        out_shape=[jax.ShapeDtypeStruct((rows, wide), BF16)] * parts,
        compiler_params=pltpu.CompilerParams(vmem_limit_bytes=60 * MIB),
        cost_estimate=pl.CostEstimate(
            flops=rows * cols, bytes_accessed=rows * cols * 6, transcendentals=0
        ),
        name="round_parts",
    )(x)


def update_blocks(low, h_blocks, arriving, picks):
    parts, wide = len(low), low[0].shape[1]
    n = arriving.shape[0]
    row_pick, col_pick, present = picks
    order = jnp.arange(n, dtype=jnp.int32)
    same = (
        (row_pick[:, None] == row_pick[None, :])
        & (col_pick[:, None] == col_pick[None, :])
        & (present[:, None] * present[None, :] > 0)
    )
    leader = jnp.min(jnp.where(same, order[None, :], n), axis=1)

    def kernel(row_ref, col_ref, lead_ref, in_ref, h_ref, *rest):
        outs, (work_ref, low_ref, sems) = rest[parts : 2 * parts], rest[2 * parts :]

        def add(s, carry):
            first = lead_ref[s]

            @pl.when(first == s)
            def _():
                work_ref[s] = h_ref[s] + in_ref[s].astype(F32)

            @pl.when(first < s)
            def _():
                work_ref[first] = work_ref[first] + in_ref[s].astype(F32)

            return carry

        def write(s, carry):
            @pl.when(lead_ref[s] == s)
            def _():
                low_ref[s] = work_ref[s].astype(BF16)
                top = pl.ds(pl.multiple_of(row_ref[s] * BLK, BLK), BLK)
                column = col_ref[s] * BLK
                for p in range(parts):

                    @pl.when((column >= p * wide) & (column < (p + 1) * wide))
                    def _(p=p):
                        left = pl.ds(pl.multiple_of(column - p * wide, BLK), BLK)
                        pltpu.make_async_copy(
                            low_ref.at[s], outs[p].at[top, left], sems.at[s]
                        ).start()

            return carry

        def wait(s, carry):
            @pl.when(lead_ref[s] == s)
            def _():
                pltpu.make_async_copy(
                    low_ref.at[s], outs[0].at[pl.ds(0, BLK), pl.ds(0, BLK)], sems.at[s]
                ).wait()

            return carry

        lax.fori_loop(0, n, add, 0)
        lax.fori_loop(0, n, write, 0)
        lax.fori_loop(0, n, wait, 0)

    whole = pl.BlockSpec((n, BLK, BLK), lambda i, *_: (0, 0, 0))
    return pl.pallas_call(
        kernel,
        grid_spec=pltpu.PrefetchScalarGridSpec(
            num_scalar_prefetch=3,
            grid=(1,),
            in_specs=[whole, whole] + [pl.BlockSpec(memory_space=pltpu.HBM)] * parts,
            out_specs=[pl.BlockSpec(memory_space=pltpu.HBM)] * parts,
            scratch_shapes=[
                pltpu.VMEM((n, BLK, BLK), F32),
                pltpu.VMEM((n, BLK, BLK), BF16),
                pltpu.SemaphoreType.DMA((n,)),
            ],
        ),
        out_shape=[jax.ShapeDtypeStruct(x.shape, x.dtype) for x in low],
        input_output_aliases={5 + p: p for p in range(parts)},
        compiler_params=pltpu.CompilerParams(vmem_limit_bytes=60 * MIB),
        cost_estimate=pl.CostEstimate(
            flops=n * BLK * BLK, bytes_accessed=n * BLK * BLK * 8, transcendentals=0
        ),
        name="update_blocks",
    )(row_pick, col_pick, leader, arriving, h_blocks, *low)


def split(x):
    hi = x.astype(BF16)
    return hi, (x - hi.astype(F32)).astype(BF16)


def basis_kernel(count_ref, phi_ref, hi_ref, lo_ref, hit_ref, lot_ref):
    basis = phi_ref[0]
    column = lax.broadcasted_iota(jnp.int32, basis.shape, 1)
    masked = jnp.where(column < count_ref[pl.program_id(0)] * BLK, basis, 0.0)
    hi, lo = split(masked)
    hi_ref[0] = hi
    lo_ref[0] = lo
    hit_ref[0] = hi.T
    lot_ref[0] = lo.T


def split_basis(phi, counts):
    tdev, npts, local = phi.shape
    spec = pl.BlockSpec((1, npts, local), lambda t, *_: (t, 0, 0))
    spec_t = pl.BlockSpec((1, local, npts), lambda t, *_: (t, 0, 0))
    return pl.pallas_call(
        basis_kernel,
        grid_spec=pltpu.PrefetchScalarGridSpec(
            num_scalar_prefetch=1,
            grid=(tdev,),
            in_specs=[spec],
            out_specs=[spec, spec, spec_t, spec_t],
        ),
        out_shape=[jax.ShapeDtypeStruct((tdev, npts, local), BF16)] * 2
        + [jax.ShapeDtypeStruct((tdev, local, npts), BF16)] * 2,
        compiler_params=pltpu.CompilerParams(vmem_limit_bytes=40 * MIB),
        cost_estimate=pl.CostEstimate(
            flops=4 * phi.size, bytes_accessed=12 * phi.size, transcendentals=0
        ),
        name="split_basis",
    )(counts, phi)


def mm(x, y):
    return jnp.dot(x, y, preferred_element_type=F32)


def tile_kernel(
    hold_ref,
    count_ref,
    in_ref,
    hi_ref,
    lo_ref,
    hit_ref,
    lot_ref,
    v_ref,
    out_ref,
    dh_ref,
    dl_ref,
):
    t = pl.program_id(0)
    maxb = hi_ref.shape[2] // BLK
    for i in range(maxb):
        for j in range(maxb):
            blk = in_ref[hold_ref[t, i * maxb + j]].astype(F32) * (1.0 / DM_SCALE)
            hi, lo = split(blk)
            dh_ref[i * BLK : (i + 1) * BLK, j * BLK : (j + 1) * BLK] = hi
            dl_ref[i * BLK : (i + 1) * BLK, j * BLK : (j + 1) * BLK] = lo
    count = count_ref[t]
    mh, ml = hi_ref[0], lo_ref[0]
    dh, dl = dh_ref[...], dl_ref[...]
    spread = mm(mh, dh) + (mm(ml, dh) + mm(mh, dl))
    masked = mh.astype(F32) + ml.astype(F32)
    rho = jnp.sum(spread * masked, axis=1, keepdims=True)
    potential = v_ref[0] + rho + cube_coef * rho * rho * rho
    wh, wl = split(masked * (potential * cell_volume))
    mht, mlt = hit_ref[0], lot_ref[0]
    ham = (mm(mht, wh) + (mm(mlt, wh) + mm(mht, wl))).astype(BF16)
    for i in range(maxb):
        for j in range(maxb):

            @pl.when((i < count) & (j < count))
            def _():
                out_ref[hold_ref[t, i * maxb + j]] = ham[
                    i * BLK : (i + 1) * BLK, j * BLK : (j + 1) * BLK
                ]


def tile_ham(incoming, basis, v_column, hold, counts):
    n = incoming.shape[0]
    tdev, npts, local = basis[0].shape
    flops = tdev * 3 * 2 * 2 * npts * local * local
    spec = pl.BlockSpec((1, npts, local), lambda t, *_: (t, 0, 0))
    spec_t = pl.BlockSpec((1, local, npts), lambda t, *_: (t, 0, 0))
    return pl.pallas_call(
        tile_kernel,
        grid_spec=pltpu.PrefetchScalarGridSpec(
            num_scalar_prefetch=2,
            grid=(tdev,),
            in_specs=[
                pl.BlockSpec((n, BLK, BLK), lambda t, *_: (0, 0, 0)),
                spec,
                spec,
                spec_t,
                spec_t,
                pl.BlockSpec((1, npts, 1), lambda t, *_: (t, 0, 0)),
            ],
            out_specs=pl.BlockSpec((n, BLK, BLK), lambda t, *_: (0, 0, 0)),
            scratch_shapes=[
                pltpu.VMEM((local, local), BF16),
                pltpu.VMEM((local, local), BF16),
            ],
        ),
        out_shape=jax.ShapeDtypeStruct((n, BLK, BLK), BF16),
        compiler_params=pltpu.CompilerParams(vmem_limit_bytes=44 * MIB),
        cost_estimate=pl.CostEstimate(
            flops=flops, bytes_accessed=tdev * npts * local * 8, transcendentals=0
        ),
        name="tile_ham",
    )(hold, counts, incoming, *basis, v_column)


def assemble(h_core, arriving, picks, dtype, first, parts, wide):
    rows, cols = h_core.shape[0], parts * wide
    n = arriving.shape[0]
    per = 2
    bm = per * BLK
    steps = rows // bm
    narrow = dtype != F32

    def kernel(row_ref, col_ref, present_ref, in_ref, h_ref, *rest):
        outs, rest = rest[:parts], rest[parts:]
        work_ref, in_sems, out_sems, num_ref, list_ref = rest[:5]
        low_refs = rest[5:] if narrow else (work_ref,)

        def band(g):
            return pl.ds(g * bm, bm)

        def read(g):
            return pltpu.make_async_copy(
                h_ref.at[band(g), pl.ds(first, cols)], work_ref.at[band(g)], in_sems.at[g]
            )

        def write(g, p):
            return pltpu.make_async_copy(
                low_refs[p].at[band(g)], outs[p].at[band(g)], out_sems.at[g, p]
            )

        for g in range(min(AHEAD, steps)):
            read(g).start()
        for g in range(steps):
            num_ref[g] = 0

        def note(s, carry):
            c = col_ref[s] * BLK

            @pl.when((present_ref[s] > 0) & (c >= first) & (c < first + cols))
            def _():
                g = row_ref[s] // per
                k = num_ref[g]
                list_ref[g * n + k] = s
                num_ref[g] = k + 1

            return carry

        lax.fori_loop(0, n, note, 0)

        for g in range(steps):
            read(g).wait()
            if g + AHEAD < steps:
                read(g + AHEAD).start()

            def add(k, carry, g=g):
                s = list_ref[g * n + k]
                top = pl.ds(pl.multiple_of(row_ref[s] * BLK, BLK), BLK)
                left = pl.ds(pl.multiple_of(col_ref[s] * BLK - first, BLK), BLK)
                work_ref[top, left] = work_ref[top, left] + in_ref[s].astype(F32)
                return carry

            lax.fori_loop(0, num_ref[g], add, 0)
            for p in range(parts):
                if narrow:
                    low_refs[p][band(g), :] = work_ref[band(g), p * wide : (p + 1) * wide].astype(
                        dtype
                    )
                write(g, p).start()
        for g in range(steps):
            for p in range(parts):
                write(g, p).wait()

    scratch = [
        pltpu.VMEM((rows, cols), F32),
        pltpu.SemaphoreType.DMA((steps,)),
        pltpu.SemaphoreType.DMA((steps, parts)),
        pltpu.SMEM((steps,), jnp.int32),
        pltpu.SMEM((steps * n,), jnp.int32),
    ]
    if narrow:
        scratch.extend([pltpu.VMEM((rows, wide), dtype)] * parts)
    return pl.pallas_call(
        kernel,
        grid_spec=pltpu.PrefetchScalarGridSpec(
            num_scalar_prefetch=3,
            grid=(1,),
            in_specs=[
                pl.BlockSpec((n, BLK, BLK), lambda i, *_: (0, 0, 0)),
                pl.BlockSpec(memory_space=pl.ANY),
            ],
            out_specs=[pl.BlockSpec(memory_space=pl.ANY)] * parts,
            scratch_shapes=scratch,
        ),
        out_shape=[jax.ShapeDtypeStruct((rows, wide), dtype)] * parts,
        compiler_params=pltpu.CompilerParams(vmem_limit_bytes=60 * MIB),
        cost_estimate=pl.CostEstimate(
            flops=rows * cols, bytes_accessed=rows * cols * 6, transcendentals=0
        ),
        name="assemble",
    )(*picks, arriving, h_core)


def product(cols, dm_panel, pieces):
    ncol, rows, width = dm_panel.shape
    depth = pieces[0][0][0][0].shape[0]
    per = depth // width
    bm = min(512, rows)
    npiece = len(pieces)
    nh = sum(len(arrays) for c, _, _ in pieces for arrays in c)
    scalars = jnp.stack(
        [jnp.asarray(s, jnp.int32) for _, _, s in pieces]
        + [jnp.asarray(w, jnp.int32) for _, w, _ in pieces]
    )

    def kernel(sc_ref, *refs):
        h_refs = refs[:nh]
        d_refs = refs[nh : nh + npiece]
        out_ref = refs[nh + npiece]
        held = refs[nh + npiece + 1 : -1]
        sems = refs[-1]

        @pl.when(pl.program_id(0) == 0)
        def _():
            at = 0
            for p, (candidates, _, _) in enumerate(pieces):
                for q, arrays in enumerate(candidates):
                    mine = h_refs[at : at + len(arrays)]
                    at += len(arrays)

                    @pl.when(sc_ref[npiece + p] == q)
                    def _(p=p, mine=mine):
                        left = 0
                        for ref in mine:
                            right = left + ref.shape[1]
                            pltpu.make_async_copy(
                                ref, held[p].at[:, left:right], sems.at[p]
                            ).start()
                            left = right

            for p in range(npiece):
                pltpu.make_async_copy(held[p], held[p], sems.at[p]).wait()

        acc = None
        for p in range(npiece):
            for q in range(per):
                term = mm(d_refs[p][q], held[p][q * width : (q + 1) * width, :])
                acc = term if acc is None else acc + term
        out_ref[...] = acc

    def d_map(p):
        return lambda i, sc: (sc[p], i, 0)

    return pl.pallas_call(
        kernel,
        grid_spec=pltpu.PrefetchScalarGridSpec(
            num_scalar_prefetch=1,
            grid=(rows // bm,),
            in_specs=[pl.BlockSpec(memory_space=pl.ANY)] * nh
            + [pl.BlockSpec((per, bm, width), d_map(p)) for p in range(npiece)],
            out_specs=pl.BlockSpec((bm, cols), lambda i, sc: (i, 0)),
            scratch_shapes=[pltpu.VMEM((depth, cols), BF16)] * npiece
            + [pltpu.SemaphoreType.DMA((npiece,))],
        ),
        out_shape=jax.ShapeDtypeStruct((rows, cols), F32),
        compiler_params=pltpu.CompilerParams(vmem_limit_bytes=60 * MIB),
        cost_estimate=pl.CostEstimate(
            flops=2 * npiece * rows * depth * cols,
            bytes_accessed=npiece * (rows + cols) * depth * 2 + rows * cols * 4,
            transcendentals=0,
        ),
        name="product",
    )(scalars, *[x for c, _, _ in pieces for arrays in c for x in arrays], *[dm_panel] * npiece)


def product_add(total, part, dm_panel, candidates, which, shard):
    ncol, rows, width = dm_panel.shape
    depth, wide = candidates[0].shape
    per = depth // width
    bm = min(512, rows)
    steps = rows // bm
    nh = len(candidates)
    scalars = jnp.stack([jnp.asarray(which, jnp.int32), jnp.asarray(shard, jnp.int32)])

    def kernel(sc_ref, *refs):
        h_refs = refs[:nh]
        dm_ref, total_ref, out_ref, held, d_ref, c_ref, h_sem, d_sems, c_sems, o_sems = refs[nh:]
        columns = pl.ds(part * wide, wide)

        def read_d(i, q):
            return pltpu.make_async_copy(
                dm_ref.at[sc_ref[1] * per + q, pl.ds(i * bm, bm)],
                d_ref.at[i, :, pl.ds(q * width, width)],
                d_sems.at[i, q],
            )

        def read_c(i):
            return pltpu.make_async_copy(
                total_ref.at[pl.ds(i * bm, bm), columns], c_ref.at[i], c_sems.at[i]
            )

        def write(i):
            return pltpu.make_async_copy(
                c_ref.at[i], out_ref.at[pl.ds(i * bm, bm), columns], o_sems.at[i]
            )

        for k in range(nh):

            @pl.when(sc_ref[0] == k)
            def _(k=k):
                pltpu.make_async_copy(h_refs[k], held, h_sem.at[0]).start()

        def start(i):
            for q in range(per):
                read_d(i, q).start()
            read_c(i).start()

        for i in range(min(2, steps)):
            start(i)
        pltpu.make_async_copy(h_refs[0], held, h_sem.at[0]).wait()
        for i in range(steps):
            for q in range(per):
                read_d(i, q).wait()
            read_c(i).wait()
            if i + 2 < steps:
                start(i + 2)
            c_ref[i] = c_ref[i] + mm(d_ref[i], held[...])
            write(i).start()
        for i in range(steps):
            write(i).wait()

    return pl.pallas_call(
        kernel,
        grid_spec=pltpu.PrefetchScalarGridSpec(
            num_scalar_prefetch=1,
            grid=(1,),
            in_specs=[pl.BlockSpec(memory_space=pl.ANY)] * (nh + 2),
            out_specs=pl.BlockSpec(memory_space=pl.ANY),
            scratch_shapes=[
                pltpu.VMEM((depth, wide), BF16),
                pltpu.VMEM((steps, bm, depth), BF16),
                pltpu.VMEM((steps, bm, wide), F32),
                pltpu.SemaphoreType.DMA((1,)),
                pltpu.SemaphoreType.DMA((steps, per)),
                pltpu.SemaphoreType.DMA((steps,)),
                pltpu.SemaphoreType.DMA((steps,)),
            ],
        ),
        out_shape=jax.ShapeDtypeStruct(total.shape, F32),
        input_output_aliases={2 + nh: 0},
        compiler_params=pltpu.CompilerParams(vmem_limit_bytes=60 * MIB),
        cost_estimate=pl.CostEstimate(
            flops=2 * rows * depth * wide,
            bytes_accessed=(rows + wide) * depth * 2 + rows * wide * 8,
            transcendentals=0,
        ),
        name="product_add",
    )(scalars, *candidates, dm_panel, total)


PARTS = 4


def tie(x, y):
    return lax.optimization_barrier((x, y))


def body(density, h_core, phi, v_ext, tile_blocks, tile_count):
    nrow = lax.axis_size("row")
    ncol = lax.axis_size("col")
    ndev = nrow * ncol
    row_idx = lax.axis_index("row")
    col_idx = lax.axis_index("col")
    myself = row_idx * ncol + col_idx
    rows_loc, cols_loc = density.shape
    rowb = rows_loc // BLK
    colb = cols_loc // BLK
    tdev, npts, local = phi.shape
    maxb = tile_blocks.shape[1]
    line = nrow == 4

    swap = [(0, 1), (1, 0), (2, 3), (3, 2)]
    cross = [(1, 2), (2, 1)]
    outward = [(1, 0), (2, 3)]

    blocks = tile_blocks.reshape(ndev, tdev, maxb)
    counts = tile_count.reshape(ndev, tdev)
    live = jnp.arange(maxb, dtype=jnp.int32)[None, None, :] < counts[:, :, None]
    col_hit = live & (blocks // colb == col_idx)
    col_in = jnp.sum(jnp.where(col_hit, blocks - col_idx * colb, 0), axis=2)

    def picks_of(row):
        row_hit = live & (blocks // rowb == row)
        both = jnp.any(row_hit, axis=2) & jnp.any(col_hit, axis=2)
        row_in = jnp.sum(jnp.where(row_hit, blocks - row * rowb, 0), axis=2)
        row_pick = jnp.sum(jnp.where(both, row_in, 0), axis=1)
        col_pick = jnp.sum(jnp.where(both, col_in, 0), axis=1)
        return row_pick, col_pick, jnp.any(both, axis=1).astype(jnp.int32)

    picks = picks_of(row_idx)
    mine = lax.dynamic_index_in_dim(blocks, myself, 0, keepdims=False)
    my_counts = lax.dynamic_index_in_dim(counts, myself, 0, keepdims=False)
    hold = ((mine // rowb)[:, :, None] * ncol + (mine // colb)[:, None, :]).reshape(tdev, -1)

    outgoing = (gather_blocks(density, picks[0], picks[1]) * DM_SCALE).astype(jnp.float16)
    incoming = lax.all_to_all(outgoing, ("row", "col"), split_axis=0, concat_axis=0, tiled=True)
    basis = split_basis(phi, my_counts)
    (dm_low,) = round_parts(density, 1)
    v_column = v_ext[:, :, None]
    incoming, (dm_low, basis, v_column) = tie(incoming, (dm_low, basis, v_column))
    dm_panel = lax.all_gather(dm_low, "col", axis=0, tiled=False)

    returning = tile_ham(incoming.astype(F32), basis, v_column, hold, my_counts)
    arriving = lax.all_to_all(returning, ("row", "col"), split_axis=0, concat_axis=0, tiled=True)
    parts = PARTS if line and cols_loc % (PARTS * BLK) == 0 else 1
    wide = cols_loc // parts
    low = round_parts(h_core, parts)
    h_blocks = gather_blocks(h_core, picks[0], picks[1])
    arriving, (low, h_blocks) = tie(arriving, (low, h_blocks))
    low = update_blocks(low, h_blocks, arriving, picks)
    (hamiltonian,) = assemble(h_core, arriving, picks, F32, 0, 1, cols_loc)

    if line:
        pair_idx = row_idx + 1 - 2 * (row_idx % 2)
        is_low = row_idx < 2
        is_end = ((row_idx == 0) | (row_idx == 3)).astype(jnp.int32)
        near_idx = jnp.where(is_low, 2, 1)
        far_idx = jnp.where(is_low, 3, 0)
        pair, near_mid = [], []
        for p in range(parts):
            ready = low[p] if p < 2 else tie(low[p], near_mid[p - 2])[0]
            pair.append(lax.ppermute(ready, "row", swap))
            near_mid.append(lax.ppermute(ready, "row", cross))
        near_end = [lax.ppermute(x, "row", outward) for x in near_mid]
        far_mid = []
        for p in range(parts):
            ready = pair[p]
            if p > 0:
                ready, near_end[p - 1] = tie(ready, near_end[p - 1])
            far_mid.append(lax.ppermute(ready, "row", cross))
        far_end = []
        for p in range(parts):
            ready = far_mid[p]
            if p == parts - 1:
                ready, near_end[p] = tie(ready, near_end[p])
            far_end.append(lax.ppermute(ready, "row", outward))
        total = product(
            cols_loc,
            dm_panel,
            [
                ((low,), 0, row_idx),
                ((pair,), 0, pair_idx),
                ((near_mid, near_end), is_end, near_idx),
            ],
        )
        for p in range(parts):
            total = product_add(
                total, p, dm_panel, (far_mid[p], far_end[p]), is_end, far_idx
            )
    else:
        ham_panel = lax.all_gather(low[0], "row", axis=0, tiled=False)
        total = product(cols_loc, dm_panel, [(((ham_panel[0],),), 0, 0)])
        for k in range(1, nrow):
            total = product_add(total, 0, dm_panel, (ham_panel[k],), 0, k)
    return hamiltonian, total


def solution(mesh):
    placed = (
        P("row", "col"),
        P("row", "col"),
        P(("row", "col"), None, None),
        P(("row", "col"), None),
        P(),
        P(),
    )
    return jax.shard_map(
        body,
        mesh=mesh,
        in_specs=placed,
        out_specs=(P("row", "col"), P("row", "col")),
        check_vma=False,
    )
```
